128 devices in a mesh: row: 32 (over z, y_hi, x), col: 4 (over y_lo, core).
Axes of the slice: x: 4, y: 4 (y_hi: 2, y_lo: 2; y = y_hi * 2 + y_lo), z: 4, core: 2. Of those that a mesh axis runs over, the one named last changes fastest.
Arguments:
- pair_map: bfloat16 [704, 704, 128], P('row', 'col'), may hold values from -40 to 40, as said below
- in_gain: float32 [128], replicated, may hold values from 0.1 to 1.9
- project_weight: bfloat16 [128, 512], replicated, may hold values from -0.5 to 0.5
- gate_weight: bfloat16 [128, 128], replicated, may hold values from -0.5 to 0.5
- out_gain: float32 [128], replicated, may hold values from 0.1 to 1.9
- out_weight: bfloat16 [128, 128], replicated, may hold values from -0.5 to 0.5
Outputs:
- update_t: bfloat16 [704, 704, 128], P('row', 'col')
The draws below stay inside these ranges and needn't reach their ends.
Inputs may be any that keep to these rules, and one draw needn't show every extreme that they name: `pair_map`: pair features.
All inputs are finite; a program needn't handle non-finite values.
Results may differ from the reference program's by a relative error of at most 0.019.
Values may be sent and summed in bfloat16 or wider, within the bound.
A program may use at most 192 MiB of HBM per device.

```python
import jax
import jax.numpy as jnp
from jax import lax

PAIR_WIDTH = 128
CHANNELS = 128
ROWS_DEV = 22
RESIDUES = 704
N_ROW = 32


def draw_pair_map(key, part):
    key = jax.random.fold_in(key, 11)
    first, second, third = jax.random.split(key, 3)
    shape = (RESIDUES, RESIDUES, PAIR_WIDTH)
    pair_scale = jnp.exp(jax.random.uniform(second, (RESIDUES, RESIDUES, 1), minval=-1.15, maxval=1.15))
    channel_scale = jnp.exp(jax.random.uniform(third, (1, 1, PAIR_WIDTH), minval=-1.15, maxval=1.15))
    base = jnp.clip(jax.random.normal(first, shape), -4.0, 4.0)
    return (base * pair_scale * channel_scale).astype(jnp.bfloat16)


def bell_draw(stream_key, extent, scale, limit, dtype=jnp.bfloat16):
    values = scale * jax.random.normal(stream_key, extent, jnp.float32)
    return jnp.clip(values, min=-limit, max=limit).astype(dtype)


def setup_inputs(seed: int = 0) -> dict:
    key_of = jax.random.split(jax.random.key(seed), 7)
    return {
        "pair_map": draw_pair_map(jax.random.fold_in(key_of[6], 71), 0),
        "in_gain": jnp.clip(1.0 + 0.18 * jax.random.normal(key_of[1], (PAIR_WIDTH,), jnp.float32), 0.1, 1.9),
        "project_weight": bell_draw(key_of[2], (PAIR_WIDTH, 4 * CHANNELS), PAIR_WIDTH ** -0.5, 0.5),
        "gate_weight": bell_draw(key_of[3], (PAIR_WIDTH, PAIR_WIDTH), PAIR_WIDTH ** -0.5, 0.5),
        "out_gain": jnp.clip(1.0 + 0.18 * jax.random.normal(key_of[4], (CHANNELS,), jnp.float32), 0.1, 1.9),
        "out_weight": bell_draw(key_of[5], (CHANNELS, PAIR_WIDTH), CHANNELS ** -0.5, 0.5),
    }


def layer_norm(values, gain):
    values = values.astype(jnp.float32)
    center = values - lax.optimization_barrier(jnp.mean(values, axis=-1, keepdims=True))
    spread = lax.optimization_barrier(jnp.mean(center * center, axis=-1, keepdims=True))
    return center * lax.rsqrt(spread + 1e-05) * gain.astype(jnp.float32)

def reference(pair_map, in_gain, project_weight, gate_weight, out_gain, out_weight):
    width = pair_map.shape[2]
    channels = out_weight.shape[0]
    blocks = pair_map.reshape(N_ROW, ROWS_DEV, RESIDUES, width)

    def factors(block):
        normed = layer_norm(block.reshape(ROWS_DEV * RESIDUES, width), in_gain).astype(jnp.bfloat16)
        projected = jnp.dot(normed, project_weight, preferred_element_type=jnp.float32)
        left_factor = (jax.nn.sigmoid(projected[:, :channels]) * projected[:, channels:2 * channels]).astype(jnp.bfloat16)
        right_factor = (jax.nn.sigmoid(projected[:, 2 * channels:3 * channels]) * projected[:, 3 * channels:]).astype(jnp.bfloat16)
        return (left_factor.reshape(ROWS_DEV, RESIDUES, channels), right_factor.reshape(ROWS_DEV, RESIDUES, channels))
    left_blocks, right_blocks = lax.map(factors, blocks)
    left_factor = left_blocks.reshape(RESIDUES, RESIDUES, channels).astype(jnp.float32)
    right_factor = right_blocks.reshape(RESIDUES, RESIDUES, channels).astype(jnp.float32)
    products = jnp.einsum('ikc,jkc->ijc', left_factor, right_factor, precision=lax.Precision.HIGHEST)
    product_blocks = products.reshape(N_ROW, ROWS_DEV, RESIDUES, channels)

    def finish(inputs):
        block, product_block = inputs
        normed = layer_norm(block.reshape(ROWS_DEV * RESIDUES, width), in_gain).astype(jnp.bfloat16)
        hidden = layer_norm(product_block.reshape(ROWS_DEV * RESIDUES, channels), out_gain).astype(jnp.bfloat16)
        gate = jax.nn.sigmoid(jnp.dot(normed, gate_weight, preferred_element_type=jnp.float32))
        mixed = gate * jnp.dot(hidden, out_weight, preferred_element_type=jnp.float32)
        return mixed.astype(jnp.bfloat16).reshape(ROWS_DEV, RESIDUES, width)
    update = lax.map(finish, (blocks, product_blocks)).reshape(RESIDUES, RESIDUES, width)
    return jnp.transpose(update, (1, 0, 2))
```

```python
import functools

import jax
import jax.numpy as jnp
from jax import lax
from jax.experimental import pallas as pl
from jax.experimental.pallas import tpu as pltpu
from jax.sharding import PartitionSpec as P

MESH = pl.DeviceIdType.MESH
F32 = jnp.float32
BF16 = jnp.bfloat16
VMEM_LIMIT = 56 * 2**20

ROWS = 22
ROWS_PAD = 24
COLS = 176
CHANNELS = 128
HALF = 64
LANES = 384
BLOCKS = 32
NT = (((1,), (1,)), ((), ()))
TN = (((0,), (0,)), ((), ()))


def sigmoid(x):
    return 0.5 * jnp.tanh(0.5 * x) + 0.5


def place():
    row = lax.axis_index("row")
    col = lax.axis_index("col")
    return row, col


def chip_at(row, col, step):
    z, y, x = row // 8, ((row // 4) % 2) * 2 + col // 2, row % 4
    walk = (step * 37) % 64
    z, y, x = (z + walk // 16) % 4, (y + (walk // 4) % 4) % 4, (x + walk % 4) % 4
    row2 = z * 8 + (y // 2) * 4 + x
    low = y % 2
    return {"row": row2, "col": low * 2 + col % 2}, row2 * 2 + low


def project_kernel(own_ref, sib_ref, gain_ref, weight_ref, lr_ref, g_ref, wt, normed, lr32, g32):
    half = lax.axis_index("col") % 2
    wt[...] = weight_ref[...].astype(F32).T
    parts = [wt[pl.ds(pl.multiple_of(128 * n + HALF * half, HALF), HALF), :] for n in range(4)]
    weight = jnp.concatenate(parts, axis=0).astype(BF16)
    ones = jnp.full((128, 128), 1.0 / 128, BF16)
    normed[2 * COLS :, :] = jnp.zeros((LANES - 2 * COLS, 128), BF16)
    for pad in (22, 23, 46, 47):
        for t in range(3):
            lr32[t, pl.ds(pad, HALF, stride=48), :] = jnp.zeros((HALF, 128), F32)
    for pad in (22, 23):
        g32[pl.ds(pad, COLS, stride=ROWS_PAD), :] = jnp.zeros((COLS, 128), F32)

    @pl.loop(0, ROWS)
    def _(i):
        for n, ref in enumerate((own_ref, sib_ref)):
            x = ref[i]
            center = x.astype(F32) - jnp.dot(x, ones, preferred_element_type=F32)
            spread = jnp.dot((center * center).astype(BF16), ones, preferred_element_type=F32)
            y = (center * lax.rsqrt(spread + 1e-05) * gain_ref[...]).astype(BF16)
            normed[n * COLS : (n + 1) * COLS, :] = y
            if n == 0:
                g32[pl.ds(i, COLS, stride=ROWS_PAD), :] = y.astype(F32)
        projected = lax.dot_general(weight, normed[...], NT, preferred_element_type=F32)
        left = sigmoid(projected[0:64]) * projected[64:128]
        right = sigmoid(projected[128:192]) * projected[192:256]
        for t in range(3):
            tile = slice(128 * t, 128 * (t + 1))
            lr32[t, pl.ds(i, HALF, stride=48), :] = left[:, tile]
            lr32[t, pl.ds(24 + i, HALF, stride=48), :] = right[:, tile]

    @pl.loop(0, HALF)
    def _(c):
        rows = pl.ds(pl.multiple_of(c * 48, 48), 48)
        for t in range(3):
            lr_ref[c, :, 128 * t : 128 * (t + 1)] = lr32[t, rows, :].astype(BF16)

    @pl.loop(0, COLS)
    def _(j):
        g_ref[j] = g32[pl.ds(pl.multiple_of(j * ROWS_PAD, ROWS_PAD), ROWS_PAD), :].astype(BF16)


def project(own, sib, gain, weight):
    return pl.pallas_call(
        project_kernel,
        out_shape=(
            jax.ShapeDtypeStruct((HALF, 48, LANES), BF16),
            jax.ShapeDtypeStruct((COLS, ROWS_PAD, 128), BF16),
        ),
        in_specs=[pl.BlockSpec(memory_space=pltpu.VMEM)] * 4,
        out_specs=[pl.BlockSpec(memory_space=pltpu.VMEM)] * 2,
        scratch_shapes=[
            pltpu.VMEM((512, 128), F32),
            pltpu.VMEM((LANES, 128), BF16),
            pltpu.VMEM((3, HALF * 48, 128), F32),
            pltpu.VMEM((COLS * ROWS_PAD, 128), F32),
        ],
        compiler_params=pltpu.CompilerParams(vmem_limit_bytes=VMEM_LIMIT),
        name="project",
    )(own, sib, gain, weight)


def exchange_kernel(src_ref, dst_ref, send, recv, local):
    row, col = place()
    me = row * 2 + col // 2
    barrier = pltpu.get_barrier_semaphore()

    @pl.loop(1, 64)
    def _(s):
        device, _ = chip_at(row, col, s)
        pl.semaphore_signal(barrier, inc=1, device_id=device, device_id_type=MESH)

    own = pltpu.make_async_copy(src_ref.at[me], dst_ref.at[me], local)
    own.start()
    pl.semaphore_wait(barrier, 63)

    def copy(s):
        device, chip = chip_at(row, col, s)
        return pltpu.make_async_remote_copy(
            src_ref=src_ref.at[chip],
            dst_ref=dst_ref.at[me],
            send_sem=send.at[s],
            recv_sem=recv.at[s],
            device_id=device,
            device_id_type=MESH,
        )

    @pl.loop(1, 64)
    def _(s):
        copy(s).start()

    own.wait()

    @pl.loop(1, 64)
    def _(s):
        copy(s).wait()


def exchange(x, collective_id, name):
    return pl.pallas_call(
        exchange_kernel,
        out_shape=jax.ShapeDtypeStruct(x.shape, x.dtype),
        in_specs=[pl.BlockSpec(memory_space=pltpu.VMEM)],
        out_specs=pl.BlockSpec(memory_space=pltpu.VMEM),
        scratch_shapes=[
            pltpu.SemaphoreType.DMA((64,)),
            pltpu.SemaphoreType.DMA((64,)),
            pltpu.SemaphoreType.DMA,
        ],
        compiler_params=pltpu.CompilerParams(
            collective_id=collective_id, has_side_effects=True, vmem_limit_bytes=VMEM_LIMIT
        ),
        name=name,
    )(x)


def triangle_kernel(x_ref, out_ref, left, right):
    @pl.loop(0, BLOCKS // 2)
    def _(b):
        for low in range(2):
            one = x_ref[4 * b + low].astype(F32)
            two = x_ref[4 * b + 2 + low].astype(F32)
            rows = pl.ds(pl.multiple_of(48 * b, 48), 48)
            lanes = slice(LANES * low, LANES * (low + 1))
            left[rows, lanes] = jnp.concatenate([one[:24], two[:24]], axis=0).astype(BF16)
            right[rows, lanes] = jnp.concatenate([one[24:], two[24:]], axis=0).astype(BF16)

    @pl.loop(0, 4)
    def _(n):
        rows = pl.ds(pl.multiple_of(192 * n, 192), 192)
        acc = lax.dot_general(right[rows, :], left[...], NT, preferred_element_type=F32)
        for b in range(8):
            for low in range(2):
                out_ref[16 * n + 2 * b + low] = acc[
                    24 * b : 24 * b + 24, LANES * low : LANES * (low + 1)
                ].astype(BF16)


def triangle(x):
    return pl.pallas_call(
        triangle_kernel,
        out_shape=jax.ShapeDtypeStruct((64, ROWS_PAD, LANES), BF16),
        in_specs=[pl.BlockSpec(memory_space=pltpu.VMEM)],
        out_specs=pl.BlockSpec(memory_space=pltpu.VMEM),
        scratch_shapes=[pltpu.VMEM((768, 768), BF16), pltpu.VMEM((768, 768), BF16)],
        compiler_params=pltpu.CompilerParams(vmem_limit_bytes=VMEM_LIMIT),
        name="triangle",
    )(x)


def finish_kernel(own_ref, sib_ref, g_ref, gate_weight_ref, gain_ref, weight_ref, out_ref, p32, gains, ws, mixed, packed):
    half = lax.axis_index("col") % 2

    @pl.loop(0, HALF)
    def _(c):
        for t in range(2):
            lanes = pl.ds(pl.multiple_of(128 * half + 128 * t, 128), 128)
            p32[t, pl.ds(pl.multiple_of(c * 24, 24), 24), :] = own_ref[c, :, lanes].astype(F32)
            p32[t, pl.ds(pl.multiple_of((HALF + c) * 24, 24), 24), :] = sib_ref[
                c, :, 128 * t : 128 * (t + 1)
            ].astype(F32)

    gains[...] = jnp.broadcast_to(gain_ref[...], (128, 128)).T
    ws[...] = weight_ref[...].astype(F32)
    first = pl.ds(pl.multiple_of(HALF * half, HALF), HALF)
    second = pl.ds(pl.multiple_of(HALF - HALF * half, HALF), HALF)
    gain = jnp.concatenate([gains[first, :], gains[second, :]], axis=0)
    gain = jnp.concatenate([gain, gain], axis=1)
    weight = jnp.concatenate([ws[first, :], ws[second, :]], axis=0).astype(BF16)

    @pl.loop(0, ROWS)
    def _(j):
        p = jnp.concatenate([p32[t, pl.ds(j, CHANNELS, stride=24), :] for t in range(2)], axis=1)
        center = p - jnp.mean(p, axis=0, keepdims=True)
        spread = jnp.mean(center * center, axis=0, keepdims=True)
        hidden = (center * lax.rsqrt(spread + 1e-05) * gain).astype(BF16)
        mixed[...] = lax.dot_general(hidden, weight, TN, preferred_element_type=F32)
        pairs = jnp.concatenate([g_ref[s, j].astype(F32) for s in range(8)], axis=0).astype(BF16)
        gate = sigmoid(jnp.dot(pairs, gate_weight_ref[...], preferred_element_type=F32))
        update = gate * mixed[pl.ds(pl.multiple_of(64 * half, 64), 192), :]
        for s in range(8):
            packed[22 * s : 22 * s + 24, :] = update[24 * s : 24 * s + 24]
        out_ref[j] = packed[0:COLS, :].astype(BF16)


def finish(own, sib, g, gate_weight, gain, weight):
    return pl.pallas_call(
        finish_kernel,
        out_shape=jax.ShapeDtypeStruct((ROWS, COLS, 128), BF16),
        in_specs=[pl.BlockSpec(memory_space=pltpu.VMEM)] * 6,
        out_specs=pl.BlockSpec(memory_space=pltpu.VMEM),
        scratch_shapes=[
            pltpu.VMEM((2, CHANNELS * 24, 128), F32),
            pltpu.VMEM((128, 128), F32),
            pltpu.VMEM((128, 128), F32),
            pltpu.VMEM((256, 128), F32),
            pltpu.VMEM((184, 128), F32),
        ],
        compiler_params=pltpu.CompilerParams(vmem_limit_bytes=VMEM_LIMIT),
        name="finish",
    )(own, sib, g, gate_weight, gain, weight)


def swap_kernel(src_ref, dst_ref, send, recv):
    row, col = place()
    barrier = pltpu.get_barrier_semaphore()

    def target(v):
        return 8 * col + v, row // 8

    def source(s):
        return 8 * col + s, row // 8

    for n in range(8):
        row2, col2 = target(n)

        @pl.when(jnp.logical_or(row2 != row, col2 != col))
        def _():
            pl.semaphore_signal(barrier, inc=1, device_id={"row": row2, "col": col2}, device_id_type=MESH)

    same = (row // 8 == col).astype(jnp.int32)
    pl.semaphore_wait(barrier, 8 - same)

    def copy(v):
        row2, col2 = target(v)
        return pltpu.make_async_remote_copy(
            src_ref=src_ref.at[v],
            dst_ref=dst_ref.at[row % 8],
            send_sem=send.at[v],
            recv_sem=recv.at[row % 8],
            device_id={"row": row2, "col": col2},
            device_id_type=MESH,
        )

    for v in range(8):
        row2, col2 = target(v)
        mine = jnp.logical_and(row2 == row, col2 == col)

        @pl.when(mine)
        def _():
            pltpu.make_async_copy(src_ref.at[v], dst_ref.at[v], recv.at[v]).start()

        @pl.when(jnp.logical_not(mine))
        def _():
            copy(v).start()

    for v in range(8):
        row2, col2 = target(v)
        mine = jnp.logical_and(row2 == row, col2 == col)

        @pl.when(jnp.logical_not(mine))
        def _():
            copy(v).wait_send()

        pltpu.make_async_copy(src_ref.at[v], dst_ref.at[v], recv.at[v]).wait()


def swap(x, collective_id):
    return pl.pallas_call(
        swap_kernel,
        out_shape=jax.ShapeDtypeStruct(x.shape, x.dtype),
        in_specs=[pl.BlockSpec(memory_space=pltpu.VMEM)],
        out_specs=pl.BlockSpec(memory_space=pltpu.VMEM),
        scratch_shapes=[pltpu.SemaphoreType.DMA((8,)), pltpu.SemaphoreType.DMA((8,))],
        compiler_params=pltpu.CompilerParams(
            collective_id=collective_id, has_side_effects=True, vmem_limit_bytes=VMEM_LIMIT
        ),
        name="swap",
    )(x)


def body(pair_map, in_gain, project_weight, gate_weight, out_gain, out_weight):
    half = lax.axis_index("col") % 2
    pairs = [(0, 1), (1, 0), (2, 3), (3, 2)]
    sibling = lax.ppermute(pair_map, "col", pairs)
    factors, normed = project(pair_map, sibling, in_gain.reshape(1, 128), project_weight)
    factors = exchange(factors, 0, "exchange_factors")
    normed = swap(normed.reshape(8, ROWS, ROWS_PAD, 128), 2)
    products = exchange(triangle(factors), 1, "exchange_products")
    theirs = lax.dynamic_slice_in_dim(products, 128 * (1 - half), 256, axis=2)
    theirs = lax.ppermute(theirs, "col", pairs)
    return finish(products, theirs, normed, gate_weight, out_gain.reshape(1, 128), out_weight)


def solution(mesh):
    return jax.shard_map(
        body,
        mesh=mesh,
        in_specs=(P("row", "col", None), P(), P(), P(), P(), P()),
        out_specs=P("row", "col", None),
        check_vma=False,
    )
```

```python
import functools

import jax
import jax.numpy as jnp
from jax import lax
from jax.experimental import pallas as pl
from jax.experimental.pallas import tpu as pltpu
from jax.sharding import PartitionSpec as P

MESH = pl.DeviceIdType.MESH
F32 = jnp.float32
BF16 = jnp.bfloat16
VMEM_LIMIT = 56 * 2**20

ROWS = 22
ROWS_PAD = 24
COLS = 176
CHANNELS = 128
HALF = 64
LANES = 384
BLOCKS = 32
NT = (((1,), (1,)), ((), ()))
TN = (((0,), (0,)), ((), ()))


def sigmoid(x):
    return 0.5 * jnp.tanh(0.5 * x) + 0.5


def place():
    row = lax.axis_index("row")
    col = lax.axis_index("col")
    return row, col


def chip_at(row, col, hop):
    z, y, x = row // 8, ((row // 4) % 2) * 2 + col // 2, row % 4
    z, y, x = (z + hop[0]) % 4, (y + hop[1]) % 4, (x + hop[2]) % 4
    row2 = z * 8 + (y // 2) * 4 + x
    low = y % 2
    return {"row": row2, "col": low * 2 + col % 2}, row2 * 2 + low


def hop_order():
    left = [(a, b, c) for a in range(4) for b in range(4) for c in range(4)][1:]
    use = [0] * 6
    order = []

    def after(hop):
        then = list(use)
        for axis, step in enumerate(hop):
            then[2 * axis] += (0, 2, 2, 0)[step]
            then[2 * axis + 1] += (0, 0, 2, 2)[step]
        return then

    def score(hop):
        then = after(hop)
        return max(then) - min(then), sum(v * v for v in then), (hop[0] * 37 + hop[1] * 11 + hop[2] * 5) % 17

    while left:
        best = min(left, key=score)
        use = after(best)
        left.remove(best)
        order.append(best)
    return order


HOPS = hop_order()
GROUPS = ((0, 8), (8, 16), (16, 22))


def wait_bytes(ref, sem):
    pltpu.make_async_copy(ref, ref, sem).wait()


def kernel(
    own_ref, sib_ref, gain_ref, weight_ref, gate_weight_ref, out_gain_ref, out_weight_ref, out_ref,
    wt, normed, lr32, g32, lr, g, lr_in, g_in, left, right, p, p_in, p_sib, p32, gates, gains, ws, mixed, packed,
    lr_send, lr_recv, g_send, g_recv, p_send, p_recv, sib_send, sib_recv,
):
    row, col = place()
    half = col % 2
    me = row * 2 + col // 2
    sibling = {"row": row, "col": col + 1 - 2 * half}
    barrier = pltpu.get_barrier_semaphore()

    def signal(device):
        pl.semaphore_signal(barrier, inc=1, device_id=device, device_id_type=MESH)

    signal(sibling)
    for hop in HOPS:
        signal(chip_at(row, col, hop)[0])
    partners = []
    for v in range(8):
        row2, col2 = 8 * col + v, row // 8
        mine = jnp.logical_and(row2 == row, col2 == col)
        partners.append(({"row": row2, "col": col2}, mine))

        @pl.when(jnp.logical_not(mine))
        def _():
            signal(partners[v][0])

    wt[...] = weight_ref[...].astype(F32).T
    parts = [wt[pl.ds(pl.multiple_of(128 * n + HALF * half, HALF), HALF), :] for n in range(4)]
    weight = jnp.concatenate(parts, axis=0).astype(BF16)
    ones = jnp.full((128, 128), 1.0 / 128, BF16)
    for u in range(11):
        normed[u, 2 * COLS :, :] = jnp.zeros((LANES - 2 * COLS, 128), BF16)
    for pad in (22, 23, 46, 47):
        for t in range(3):
            lr32[t, pl.ds(pad, HALF, stride=48), :] = jnp.zeros((HALF, 128), F32)
    for pad in (22, 23):
        g32[pl.ds(pad, COLS, stride=ROWS_PAD), :] = jnp.zeros((COLS, 128), F32)

    @pl.loop(0, 2)
    def _(n):
        for u in range(11):
            i = 11 * n + u
            x = jnp.concatenate([own_ref[i], sib_ref[i]], axis=0)
            center = x.astype(F32) - jnp.dot(x, ones, preferred_element_type=F32)
            spread = jnp.dot((center * center).astype(BF16), ones, preferred_element_type=F32)
            y = center * lax.rsqrt(spread + 1e-05) * gain_ref[...]
            normed[u, 0 : 2 * COLS, :] = y.astype(BF16)
            g32[pl.ds(i, COLS, stride=ROWS_PAD), :] = y[0:COLS]
        for u in range(11):
            i = 11 * n + u
            projected = lax.dot_general(weight, normed[u], NT, preferred_element_type=F32)
            one = sigmoid(projected[0:64]) * projected[64:128]
            two = sigmoid(projected[128:192]) * projected[192:256]
            for t in range(3):
                tile = slice(128 * t, 128 * (t + 1))
                lr32[t, pl.ds(i, HALF, stride=48), :] = one[:, tile]
                lr32[t, pl.ds(24 + i, HALF, stride=48), :] = two[:, tile]

    pl.semaphore_wait(barrier, 72 - (row // 8 == col).astype(jnp.int32))

    def pack_factors(chip):
        rows = pl.ds(pl.multiple_of(chip * 48, 48), 48)
        for t in range(3):
            lr[chip, :, 128 * t : 128 * (t + 1)] = lr32[t, rows, :].astype(BF16)

    for hop in HOPS:
        device, chip = chip_at(row, col, hop)
        pack_factors(chip)
        pltpu.make_async_remote_copy(
            src_ref=lr.at[chip],
            dst_ref=lr_in.at[me],
            send_sem=lr_send,
            recv_sem=lr_recv.at[row // 2],
            device_id=device,
            device_id_type=MESH,
        ).start()
    pack_factors(me)
    pltpu.make_async_copy(lr.at[me], lr_in.at[me], lr_recv.at[row // 2]).start()

    for v in range(8):
        device, mine = partners[v]

        @pl.loop(0, 2)
        def _(n):
            first = 22 * v + 11 * n
            rows = pl.ds(pl.multiple_of(first * ROWS_PAD, 8), 11 * ROWS_PAD)
            g[v, pl.ds(11 * n, 11)] = g32[rows, :].reshape(11, ROWS_PAD, 128).astype(BF16)

        @pl.when(mine)
        def _():
            pltpu.make_async_copy(g.at[v], g_in.at[v], g_recv.at[v]).start()

        @pl.when(jnp.logical_not(mine))
        def _():
            pltpu.make_async_remote_copy(
                src_ref=g.at[v],
                dst_ref=g_in.at[row % 8],
                send_sem=g_send.at[v],
                recv_sem=g_recv.at[row % 8],
                device_id=device,
                device_id_type=MESH,
            ).start()

    @pl.loop(0, BLOCKS // 2)
    def _(n):
        b = (row // 2 + n) % 16
        wait_bytes(lr_in.at[pl.ds(pl.multiple_of(4 * b, 4), 4)], lr_recv.at[b])
        for low in range(2):
            one = lr_in[4 * b + low].astype(F32)
            two = lr_in[4 * b + 2 + low].astype(F32)
            rows = pl.ds(pl.multiple_of(48 * b, 48), 48)
            lanes = slice(LANES * low, LANES * (low + 1))
            left[rows, lanes] = jnp.concatenate([one[:24], two[:24]], axis=0).astype(BF16)
            right[rows, lanes] = jnp.concatenate([one[24:], two[24:]], axis=0).astype(BF16)

    for n in range(2):
        acc = lax.dot_general(right[384 * n : 384 * (n + 1), :], left[...], NT, preferred_element_type=F32)
        for b in range(16):
            for low in range(2):
                for k in range(3):
                    p[k, 32 * n + 2 * b + low] = acc[
                        24 * b + 8 * k : 24 * b + 8 * k + 8, LANES * low : LANES * (low + 1)
                    ].astype(BF16)

    for k in range(3):
        pltpu.make_async_copy(p.at[k, me], p_in.at[k, me], p_recv.at[k]).start()
        for hop in HOPS:
            device, chip = chip_at(row, col, hop)
            pltpu.make_async_remote_copy(
                src_ref=p.at[k, chip],
                dst_ref=p_in.at[k, me],
                send_sem=p_send.at[k],
                recv_sem=p_recv.at[k],
                device_id=device,
                device_id_type=MESH,
            ).start()

    for s in range(8):
        wait_bytes(g_in.at[s], g_recv.at[s])

    @pl.loop(0, 2)
    def _(n):
        for u in range(11):
            j = 11 * n + u
            pairs = jnp.concatenate([g_in[s, j].astype(F32) for s in range(8)], axis=0).astype(BF16)
            gates[j] = sigmoid(jnp.dot(pairs, gate_weight_ref[...], preferred_element_type=F32))

    gains[...] = jnp.broadcast_to(out_gain_ref[...], (128, 128)).T
    ws[...] = out_weight_ref[...].astype(F32)
    first = pl.ds(pl.multiple_of(HALF * half, HALF), HALF)
    second = pl.ds(pl.multiple_of(HALF - HALF * half, HALF), HALF)
    gain = jnp.concatenate([gains[first, :], gains[second, :]], axis=0)
    gain = jnp.concatenate([gain, gain], axis=1)
    out_weight = jnp.concatenate([ws[first, :], ws[second, :]], axis=0).astype(BF16)

    for k, (start, stop) in enumerate(GROUPS):
        wait_bytes(p_in.at[k], p_recv.at[k])
        swap = pltpu.make_async_remote_copy(
            src_ref=p_in.at[k, :, :, pl.ds(pl.multiple_of(128 - 128 * half, 128), 256)],
            dst_ref=p_sib.at[k],
            send_sem=sib_send.at[k],
            recv_sem=sib_recv.at[k],
            device_id=sibling,
            device_id_type=MESH,
        )
        swap.start()
        for t in range(2):
            lanes = pl.ds(pl.multiple_of(128 * half + 128 * t, 128), 128)
            p32[t, 0:512, :] = p_in[k, :, :, lanes].astype(F32).reshape(512, 128)
        swap.wait()
        for t in range(2):
            p32[t, 512:1024, :] = p_sib[k, :, :, 128 * t : 128 * (t + 1)].astype(F32).reshape(512, 128)
        for j in range(start, stop):
            u = j - start
            q = jnp.concatenate([p32[t, pl.ds(u, CHANNELS, stride=8), :] for t in range(2)], axis=1)
            center = q - jnp.mean(q, axis=0, keepdims=True)
            spread = jnp.mean(center * center, axis=0, keepdims=True)
            hidden = (center * lax.rsqrt(spread + 1e-05) * gain).astype(BF16)
            mixed[u] = lax.dot_general(hidden, out_weight, TN, preferred_element_type=F32)
            update = gates[j] * mixed[u, pl.ds(pl.multiple_of(64 * half, 64), 192), :]
            for s in range(8):
                packed[u, 22 * s : 22 * s + 24, :] = update[24 * s : 24 * s + 24]
            out_ref[j] = packed[u, 0:COLS, :].astype(BF16)

    wait_bytes(lr.at[pl.ds(0, 63)], lr_send)
    for k in range(3):
        wait_bytes(p.at[k, pl.ds(0, 63)], p_send.at[k])
    for v in range(8):
        @pl.when(jnp.logical_not(partners[v][1]))
        def _():
            wait_bytes(g.at[v], g_send.at[v])


def fused(*args):
    vmem = pl.BlockSpec(memory_space=pltpu.VMEM)
    return pl.pallas_call(
        kernel,
        out_shape=jax.ShapeDtypeStruct((ROWS, COLS, 128), BF16),
        in_specs=[vmem] * 7,
        out_specs=vmem,
        scratch_shapes=[
            pltpu.VMEM((512, 128), F32),
            pltpu.VMEM((11, LANES, 128), BF16),
            pltpu.VMEM((3, HALF * 48, 128), F32),
            pltpu.VMEM((COLS * ROWS_PAD, 128), F32),
            pltpu.VMEM((64, 48, LANES), BF16),
            pltpu.VMEM((8, ROWS, ROWS_PAD, 128), BF16),
            pltpu.VMEM((64, 48, LANES), BF16),
            pltpu.VMEM((8, ROWS, ROWS_PAD, 128), BF16),
            pltpu.VMEM((768, 768), BF16),
            pltpu.VMEM((768, 768), BF16),
            pltpu.VMEM((3, 64, 8, LANES), BF16),
            pltpu.VMEM((3, 64, 8, LANES), BF16),
            pltpu.VMEM((3, 64, 8, 256), BF16),
            pltpu.VMEM((2, CHANNELS * 8, 128), F32),
            pltpu.VMEM((ROWS, 192, 128), F32),
            pltpu.VMEM((128, 128), F32),
            pltpu.VMEM((128, 128), F32),
            pltpu.VMEM((8, 256, 128), F32),
            pltpu.VMEM((8, 184, 128), F32),
            pltpu.SemaphoreType.DMA,
            pltpu.SemaphoreType.DMA((16,)),
            pltpu.SemaphoreType.DMA((8,)),
            pltpu.SemaphoreType.DMA((8,)),
            pltpu.SemaphoreType.DMA((3,)),
            pltpu.SemaphoreType.DMA((3,)),
            pltpu.SemaphoreType.DMA((3,)),
            pltpu.SemaphoreType.DMA((3,)),
        ],
        compiler_params=pltpu.CompilerParams(
            collective_id=0, has_side_effects=True, vmem_limit_bytes=VMEM_LIMIT
        ),
        name="triangle_update",
    )(*args)


def body(pair_map, in_gain, project_weight, gate_weight, out_gain, out_weight):
    sibling = lax.ppermute(pair_map, "col", [(0, 1), (1, 0), (2, 3), (3, 2)])
    return fused(
        pair_map, sibling, in_gain.reshape(1, 128), project_weight, gate_weight, out_gain.reshape(1, 128), out_weight
    )


def solution(mesh):
    return jax.shard_map(
        body,
        mesh=mesh,
        in_specs=(P("row", "col", None), P(), P(), P(), P(), P()),
        out_specs=P("row", "col", None),
        check_vma=False,
    )
```

```python
import functools

import jax
import jax.numpy as jnp
from jax import lax
from jax.experimental import pallas as pl
from jax.experimental.pallas import tpu as pltpu
from jax.sharding import PartitionSpec as P

MESH = pl.DeviceIdType.MESH
F32 = jnp.float32
BF16 = jnp.bfloat16
VMEM_LIMIT = 56 * 2**20

ROWS = 22
ROWS_PAD = 24
COLS = 176
CHANNELS = 128
HALF = 64
LANES = 384
BLOCKS = 32
NT = (((1,), (1,)), ((), ()))
TN = (((0,), (0,)), ((), ()))


def sigmoid(x):
    return 0.5 * jnp.tanh(0.5 * x) + 0.5


def place():
    row = lax.axis_index("row")
    col = lax.axis_index("col")
    return row, col


def chip_at(row, col, hop):
    z, y, x = row // 8, ((row // 4) % 2) * 2 + col // 2, row % 4
    z, y, x = (z + hop[0]) % 4, (y + hop[1]) % 4, (x + hop[2]) % 4
    row2 = z * 8 + (y // 2) * 4 + x
    low = y % 2
    return {"row": row2, "col": low * 2 + col % 2}, row2 * 2 + low


def hop_order():
    left = [(a, b, c) for a in range(4) for b in range(4) for c in range(4)][1:]
    use = [0] * 6
    order = []

    def after(hop):
        then = list(use)
        for axis, step in enumerate(hop):
            then[2 * axis] += (0, 2, 2, 0)[step]
            then[2 * axis + 1] += (0, 0, 2, 2)[step]
        return then

    def score(hop):
        then = after(hop)
        return max(then) - min(then), sum(v * v for v in then), (hop[0] * 37 + hop[1] * 11 + hop[2] * 5) % 17

    while left:
        best = min(left, key=score)
        use = after(best)
        left.remove(best)
        order.append(best)
    return order


HOPS = hop_order()
GROUPS = ((0, 8), (8, 16), (16, 22))


def wait_bytes(ref, sem):
    pltpu.make_async_copy(ref, ref, sem).wait()


def kernel(
    own_ref, sib_ref, gain_ref, weight_ref, gate_weight_ref, out_gain_ref, out_weight_ref, out_ref,
    own, wt, normed, lr32, g32, lr, g, g_relay, lr_in, g_in, left, right, p, p_in, p_sib, p32, gates, gains, ws, mixed, packed,
    own_sem, lr_send, lr_recv, g_send, g_recv, relay_send, relay_recv, p_send, p_recv, sib_send, sib_recv,
):
    row, col = place()
    half = col % 2
    me = row * 2 + col // 2
    sibling = {"row": row, "col": col + 1 - 2 * half}
    barrier = pltpu.get_barrier_semaphore()

    def signal(device):
        pl.semaphore_signal(barrier, inc=1, device_id=device, device_id_type=MESH)

    z, y_hi, x = row // 8, (row // 4) % 2, row % 4
    base = 8 * col + 4 * y_hi
    other = (z + 2) % 4
    owners, relays = [], []
    for n in range(4):
        x2 = (x + n) % 4
        owners.append((4 * y_hi + x2, {"row": base + x2, "col": z}))
        relays.append((4 - 4 * y_hi + x2, {"row": base + x2, "col": other}))
    forward = {"row": row + 4 - 8 * y_hi, "col": (col + 2) % 4}
    is_own = z == col

    signal(sibling)
    for hop in HOPS:
        signal(chip_at(row, col, hop)[0])
    for n in range(4):
        signal({"row": 8 * ((col + 2) % 4) + 4 * y_hi + n, "col": z})

        @pl.when(jnp.logical_or(jnp.logical_not(is_own), n != x))
        def _():
            signal({"row": base + n, "col": z})

    own_copy = pltpu.make_async_copy(own_ref, own, own_sem)
    own_copy.start()

    wt[...] = weight_ref[...].astype(F32).T
    parts = [wt[pl.ds(pl.multiple_of(128 * n + HALF * half, HALF), HALF), :] for n in range(4)]
    weight = jnp.concatenate(parts, axis=0).astype(BF16)
    ones = jnp.full((128, 128), 1.0 / 128, BF16)
    for i in range(ROWS):
        normed[i, 2 * COLS :, :] = jnp.zeros((LANES - 2 * COLS, 128), BF16)
    for pad in (22, 23, 46, 47):
        for t in range(3):
            lr32[t, pl.ds(pad, HALF, stride=48), :] = jnp.zeros((HALF, 128), F32)
    for pad in (22, 23):
        g32[pl.ds(pad, COLS, stride=ROWS_PAD), :] = jnp.zeros((COLS, 128), F32)
    own_copy.wait()

    @pl.loop(0, 2)
    def _(n):
        for u in range(11):
            i = 11 * n + u
            v = jnp.concatenate([own[i], sib_ref[i]], axis=0)
            center = v.astype(F32) - jnp.dot(v, ones, preferred_element_type=F32)
            spread = jnp.dot((center * center).astype(BF16), ones, preferred_element_type=F32)
            y = center * lax.rsqrt(spread + 1e-05) * gain_ref[...]
            normed[i, 0 : 2 * COLS, :] = y.astype(BF16)
            g32[pl.ds(i, COLS, stride=ROWS_PAD), :] = y[0:COLS]

    def pack_pairs(v):
        for n in range(2):
            rows = pl.ds(pl.multiple_of((22 * v + 11 * n) * ROWS_PAD, 8), 11 * ROWS_PAD)
            g[v, pl.ds(11 * n, 11)] = g32[rows, :].reshape(11, ROWS_PAD, 128).astype(BF16)

    for v, _ in relays:
        pack_pairs(v)

    pl.semaphore_wait(barrier, 72 - is_own.astype(jnp.int32))

    for v, device in relays:
        pltpu.make_async_remote_copy(
            src_ref=g.at[v],
            dst_ref=g_relay.at[x],
            send_sem=g_send.at[v],
            recv_sem=relay_recv.at[x],
            device_id=device,
            device_id_type=MESH,
        ).start()

    @pl.loop(0, 2)
    def _(n):
        for u in range(11):
            i = 11 * n + u
            projected = lax.dot_general(weight, normed[i], NT, preferred_element_type=F32)
            one = sigmoid(projected[0:64]) * projected[64:128]
            two = sigmoid(projected[128:192]) * projected[192:256]
            for t in range(3):
                tile = slice(128 * t, 128 * (t + 1))
                lr32[t, pl.ds(i, HALF, stride=48), :] = one[:, tile]
                lr32[t, pl.ds(24 + i, HALF, stride=48), :] = two[:, tile]

    def pack_factors(chip):
        rows = pl.ds(pl.multiple_of(chip * 48, 48), 48)
        for t in range(3):
            lr[chip, :, 128 * t : 128 * (t + 1)] = lr32[t, rows, :].astype(BF16)

    for hop in HOPS:
        device, chip = chip_at(row, col, hop)
        pack_factors(chip)
        pltpu.make_async_remote_copy(
            src_ref=lr.at[chip],
            dst_ref=lr_in.at[me],
            send_sem=lr_send,
            recv_sem=lr_recv.at[row // 2],
            device_id=device,
            device_id_type=MESH,
        ).start()
    pack_factors(me)
    pltpu.make_async_copy(lr.at[me], lr_in.at[me], lr_recv.at[row // 2]).start()

    for n, (v, device) in enumerate(owners):
        pack_pairs(v)

        def send_pairs():
            pltpu.make_async_remote_copy(
                src_ref=g.at[v],
                dst_ref=g_in.at[row % 8],
                send_sem=g_send.at[v],
                recv_sem=g_recv.at[row % 8],
                device_id=device,
                device_id_type=MESH,
            ).start()

        if n == 0:

            @pl.when(is_own)
            def _():
                pltpu.make_async_copy(g.at[v], g_in.at[v], g_recv.at[v]).start()

            pl.when(jnp.logical_not(is_own))(send_pairs)
        else:
            send_pairs()

    for n in range(4):
        s = (x + 4 - n) % 4
        wait_bytes(g_relay.at[s], relay_recv.at[s])
        pltpu.make_async_remote_copy(
            src_ref=g_relay.at[s],
            dst_ref=g_in.at[4 * y_hi + s],
            send_sem=relay_send.at[s],
            recv_sem=g_recv.at[4 * y_hi + s],
            device_id=forward,
            device_id_type=MESH,
        ).start()

    @pl.loop(0, BLOCKS // 2)
    def _(n):
        b = (row // 2 + n) % 16
        wait_bytes(lr_in.at[pl.ds(pl.multiple_of(4 * b, 4), 4)], lr_recv.at[b])
        for low in range(2):
            one = lr_in[4 * b + low].astype(F32)
            two = lr_in[4 * b + 2 + low].astype(F32)
            rows = pl.ds(pl.multiple_of(48 * b, 48), 48)
            lanes = slice(LANES * low, LANES * (low + 1))
            left[rows, lanes] = jnp.concatenate([one[:24], two[:24]], axis=0).astype(BF16)
            right[rows, lanes] = jnp.concatenate([one[24:], two[24:]], axis=0).astype(BF16)

    for n in range(2):
        acc = lax.dot_general(right[384 * n : 384 * (n + 1), :], left[...], NT, preferred_element_type=F32)
        for b in range(16):
            for low in range(2):
                for k in range(3):
                    p[k, 32 * n + 2 * b + low] = acc[
                        24 * b + 8 * k : 24 * b + 8 * k + 8, LANES * low : LANES * (low + 1)
                    ].astype(BF16)

    for k in range(3):
        pltpu.make_async_copy(p.at[k, me], p_in.at[k, me], p_recv.at[k]).start()
        for hop in HOPS:
            device, chip = chip_at(row, col, hop)
            pltpu.make_async_remote_copy(
                src_ref=p.at[k, chip],
                dst_ref=p_in.at[k, me],
                send_sem=p_send.at[k],
                recv_sem=p_recv.at[k],
                device_id=device,
                device_id_type=MESH,
            ).start()

    for s in range(8):
        wait_bytes(g_in.at[s], g_recv.at[s])

    @pl.loop(0, 2)
    def _(n):
        for u in range(11):
            j = 11 * n + u
            pairs = jnp.concatenate([g_in[s, j].astype(F32) for s in range(8)], axis=0).astype(BF16)
            gates[j] = sigmoid(jnp.dot(pairs, gate_weight_ref[...], preferred_element_type=F32))

    gains[...] = jnp.broadcast_to(out_gain_ref[...], (128, 128)).T
    ws[...] = out_weight_ref[...].astype(F32)
    first = pl.ds(pl.multiple_of(HALF * half, HALF), HALF)
    second = pl.ds(pl.multiple_of(HALF - HALF * half, HALF), HALF)
    gain = jnp.concatenate([gains[first, :], gains[second, :]], axis=0)
    gain = jnp.concatenate([gain, gain], axis=1)
    out_weight = jnp.concatenate([ws[first, :], ws[second, :]], axis=0).astype(BF16)

    for k, (start, stop) in enumerate(GROUPS):
        wait_bytes(p_in.at[k], p_recv.at[k])
        swap = pltpu.make_async_remote_copy(
            src_ref=p_in.at[k, :, :, pl.ds(pl.multiple_of(128 - 128 * half, 128), 256)],
            dst_ref=p_sib.at[k],
            send_sem=sib_send.at[k],
            recv_sem=sib_recv.at[k],
            device_id=sibling,
            device_id_type=MESH,
        )
        swap.start()
        for t in range(2):
            lanes = pl.ds(pl.multiple_of(128 * half + 128 * t, 128), 128)
            p32[t, 0:512, :] = p_in[k, :, :, lanes].astype(F32).reshape(512, 128)
        swap.wait()
        for t in range(2):
            p32[t, 512:1024, :] = p_sib[k, :, :, 128 * t : 128 * (t + 1)].astype(F32).reshape(512, 128)
        for j in range(start, stop):
            u = j - start
            q = jnp.concatenate([p32[t, pl.ds(u, CHANNELS, stride=8), :] for t in range(2)], axis=1)
            center = q - jnp.mean(q, axis=0, keepdims=True)
            spread = jnp.mean(center * center, axis=0, keepdims=True)
            hidden = (center * lax.rsqrt(spread + 1e-05) * gain).astype(BF16)
            mixed[u] = lax.dot_general(hidden, out_weight, TN, preferred_element_type=F32)
            update = gates[j] * mixed[u, pl.ds(pl.multiple_of(64 * half, 64), 192), :]
            for s in range(8):
                packed[u, 22 * s : 22 * s + 24, :] = update[24 * s : 24 * s + 24]
            out_ref[j] = packed[u, 0:COLS, :].astype(BF16)

    wait_bytes(lr.at[pl.ds(0, 63)], lr_send)
    for k in range(3):
        wait_bytes(p.at[k, pl.ds(0, 63)], p_send.at[k])
    for v, _ in relays + owners[1:]:
        wait_bytes(g.at[v], g_send.at[v])
    for s in range(4):
        wait_bytes(g_relay.at[s], relay_send.at[s])

    @pl.when(jnp.logical_not(is_own))
    def _():
        wait_bytes(g.at[owners[0][0]], g_send.at[owners[0][0]])


def fused(*args):
    vmem = pl.BlockSpec(memory_space=pltpu.VMEM)
    return pl.pallas_call(
        kernel,
        out_shape=jax.ShapeDtypeStruct((ROWS, COLS, 128), BF16),
        in_specs=[pl.BlockSpec(memory_space=pl.ANY)] + [vmem] * 6,
        out_specs=vmem,
        scratch_shapes=[
            pltpu.VMEM((ROWS, COLS, 128), BF16),
            pltpu.VMEM((512, 128), F32),
            pltpu.VMEM((ROWS, LANES, 128), BF16),
            pltpu.VMEM((3, HALF * 48, 128), F32),
            pltpu.VMEM((COLS * ROWS_PAD, 128), F32),
            pltpu.VMEM((64, 48, LANES), BF16),
            pltpu.VMEM((8, ROWS, ROWS_PAD, 128), BF16),
            pltpu.VMEM((4, ROWS, ROWS_PAD, 128), BF16),
            pltpu.VMEM((64, 48, LANES), BF16),
            pltpu.VMEM((8, ROWS, ROWS_PAD, 128), BF16),
            pltpu.VMEM((768, 768), BF16),
            pltpu.VMEM((768, 768), BF16),
            pltpu.VMEM((3, 64, 8, LANES), BF16),
            pltpu.VMEM((3, 64, 8, LANES), BF16),
            pltpu.VMEM((3, 64, 8, 256), BF16),
            pltpu.VMEM((2, CHANNELS * 8, 128), F32),
            pltpu.VMEM((ROWS, 192, 128), F32),
            pltpu.VMEM((128, 128), F32),
            pltpu.VMEM((128, 128), F32),
            pltpu.VMEM((8, 256, 128), F32),
            pltpu.VMEM((8, 184, 128), F32),
            pltpu.SemaphoreType.DMA,
            pltpu.SemaphoreType.DMA,
            pltpu.SemaphoreType.DMA((16,)),
            pltpu.SemaphoreType.DMA((8,)),
            pltpu.SemaphoreType.DMA((8,)),
            pltpu.SemaphoreType.DMA((4,)),
            pltpu.SemaphoreType.DMA((4,)),
            pltpu.SemaphoreType.DMA((3,)),
            pltpu.SemaphoreType.DMA((3,)),
            pltpu.SemaphoreType.DMA((3,)),
            pltpu.SemaphoreType.DMA((3,)),
        ],
        compiler_params=pltpu.CompilerParams(
            collective_id=0, has_side_effects=True, vmem_limit_bytes=VMEM_LIMIT
        ),
        name="triangle_update",
    )(*args)


def body(pair_map, in_gain, project_weight, gate_weight, out_gain, out_weight):
    sibling = lax.ppermute(pair_map, "col", [(0, 1), (1, 0), (2, 3), (3, 2)])
    return fused(
        pair_map, sibling, in_gain.reshape(1, 128), project_weight, gate_weight, out_gain.reshape(1, 128), out_weight
    )


def solution(mesh):
    return jax.shard_map(
        body,
        mesh=mesh,
        in_specs=(P("row", "col", None), P(), P(), P(), P(), P()),
        out_specs=P("row", "col", None),
        check_vma=False,
    )
```

```python
import functools

import jax
import jax.numpy as jnp
from jax import lax
from jax.experimental import pallas as pl
from jax.experimental.pallas import tpu as pltpu
from jax.sharding import PartitionSpec as P

MESH = pl.DeviceIdType.MESH
F32 = jnp.float32
BF16 = jnp.bfloat16
VMEM_LIMIT = 56 * 2**20

ROWS = 22
ROWS_PAD = 24
COLS = 176
CHANNELS = 128
HALF = 64
LANES = 384
BLOCKS = 32
NT = (((1,), (1,)), ((), ()))
TN = (((0,), (0,)), ((), ()))


def sigmoid(x):
    return 0.5 * jnp.tanh(0.5 * x) + 0.5


def place():
    row = lax.axis_index("row")
    col = lax.axis_index("col")
    return row, col


def chip_at(row, col, hop):
    z, y, x = row // 8, ((row // 4) % 2) * 2 + col // 2, row % 4
    z, y, x = (z + hop[0]) % 4, (y + hop[1]) % 4, (x + hop[2]) % 4
    row2 = z * 8 + (y // 2) * 4 + x
    low = y % 2
    return {"row": row2, "col": low * 2 + col % 2}, row2 * 2 + low


def hop_order():
    left = [(a, b, c) for a in range(4) for b in range(4) for c in range(4)][1:]
    use = [0] * 6
    order = []

    def after(hop):
        then = list(use)
        for axis, step in enumerate(hop):
            then[2 * axis] += (0, 2, 2, 0)[step]
            then[2 * axis + 1] += (0, 0, 2, 2)[step]
        return then

    def score(hop):
        then = after(hop)
        return max(then) - min(then), sum(v * v for v in then), (hop[0] * 37 + hop[1] * 11 + hop[2] * 5) % 17

    while left:
        best = min(left, key=score)
        use = after(best)
        left.remove(best)
        order.append(best)
    return order


HOPS = hop_order()
GROUPS = ((0, 8), (8, 16), (16, 22))


def wait_bytes(ref, sem):
    pltpu.make_async_copy(ref, ref, sem).wait()


def kernel(
    own_ref, gain_ref, weight_ref, gate_weight_ref, out_gain_ref, out_weight_ref, out_ref,
    own, sib, wt, first, rest, lr32, g32, lr, g, g_relay, lr_in, g_in, left, right, p, p_in, p_sib, p32, gates, gains, ws, mixed, packed, out,
    own_sem, map_send, map_recv, lr_send, lr_recv, g_send, g_recv, relay_send, relay_recv, p_send, p_recv, sib_send, sib_recv, out_sem,
):
    row, col = place()
    half = col % 2
    me = row * 2 + col // 2
    sibling = {"row": row, "col": col + 1 - 2 * half}
    barrier = pltpu.get_barrier_semaphore()

    def signal(device):
        pl.semaphore_signal(barrier, inc=1, device_id=device, device_id_type=MESH)

    z, y_hi, x = row // 8, (row // 4) % 2, row % 4
    base = 8 * col + 4 * y_hi
    other = (z + 2) % 4
    owners, relays = [], []
    for n in range(4):
        x2 = (x + n) % 4
        owners.append((4 * y_hi + x2, {"row": base + x2, "col": z}))
        relays.append((4 - 4 * y_hi + x2, {"row": base + x2, "col": other}))
    forward = {"row": row + 4 - 8 * y_hi, "col": (col + 2) % 4}
    is_own = z == col

    signal(sibling)
    for hop in HOPS:
        signal(chip_at(row, col, hop)[0])
    for n in range(4):
        signal({"row": 8 * ((col + 2) % 4) + 4 * y_hi + n, "col": z})

        @pl.when(jnp.logical_or(jnp.logical_not(is_own), n != x))
        def _():
            signal({"row": base + n, "col": z})

    own_copy = pltpu.make_async_copy(own_ref, own, own_sem)
    own_copy.start()

    wt[...] = weight_ref[...].astype(F32).T
    parts = [wt[pl.ds(pl.multiple_of(128 * n + HALF * half, HALF), HALF), :] for n in range(4)]
    weight = jnp.concatenate(parts, axis=0).astype(BF16)
    ones = jnp.full((128, 128), 1.0 / 128, BF16)
    for i in range(ROWS):
        rest[i, 224:256, :] = jnp.zeros((32, 128), BF16)
    for pad in (22, 23, 46, 47):
        for t in range(3):
            lr32[t, pl.ds(pad, HALF, stride=48), :] = jnp.zeros((HALF, 128), F32)
    for pad in (22, 23):
        g32[pl.ds(pad, COLS, stride=ROWS_PAD), :] = jnp.zeros((COLS, 128), F32)

    def layer_norm(v):
        center = v.astype(F32) - jnp.dot(v, ones, preferred_element_type=F32)
        spread = jnp.dot((center * center).astype(BF16), ones, preferred_element_type=F32)
        return center * lax.rsqrt(spread + 1e-05) * gain_ref[...]

    def factors(i, t, projected):
        one = sigmoid(projected[0:64]) * projected[64:128]
        two = sigmoid(projected[128:192]) * projected[192:256]
        lr32[t, pl.ds(i, HALF, stride=48), :] = one
        lr32[t, pl.ds(24 + i, HALF, stride=48), :] = two

    def pack_pairs(v):
        for n in range(2):
            rows = pl.ds(pl.multiple_of((22 * v + 11 * n) * ROWS_PAD, 8), 11 * ROWS_PAD)
            g[v, pl.ds(11 * n, 11)] = g32[rows, :].reshape(11, ROWS_PAD, 128).astype(BF16)

    own_copy.wait()

    @pl.loop(0, 2)
    def _(n):
        for u in range(11):
            i = 11 * n + u
            y = layer_norm(own[i])
            first[i] = y[0:128].astype(BF16)
            rest[i, 128:176, :] = y[128:176].astype(BF16)
            g32[pl.ds(i, COLS, stride=ROWS_PAD), :] = y

    for n in (0, 2):
        pack_pairs(relays[n][0])
        pack_pairs(owners[n + 1][0])

    for n in range(11):
        pair = first[2 * n : 2 * n + 2].reshape(256, 128)
        projected = lax.dot_general(weight, pair, NT, preferred_element_type=F32)
        factors(2 * n, 0, projected[:, 0:128])
        factors(2 * n + 1, 0, projected[:, 128:256])

    pl.semaphore_wait(barrier, 72 - is_own.astype(jnp.int32))

    def swap_maps(n):
        rows = pl.ds(11 * n, 11)
        return pltpu.make_async_remote_copy(
            src_ref=own.at[rows],
            dst_ref=sib.at[rows],
            send_sem=map_send.at[n],
            recv_sem=map_recv.at[n],
            device_id=sibling,
            device_id_type=MESH,
        )

    def send_relayed(n):
        v, device = relays[n]
        pltpu.make_async_remote_copy(
            src_ref=g.at[v],
            dst_ref=g_relay.at[x],
            send_sem=g_send.at[v],
            recv_sem=relay_recv.at[x],
            device_id=device,
            device_id_type=MESH,
        ).start()

    def send_direct(n):
        v, device = owners[n]

        def send_pairs():
            pltpu.make_async_remote_copy(
                src_ref=g.at[v],
                dst_ref=g_in.at[row % 8],
                send_sem=g_send.at[v],
                recv_sem=g_recv.at[row % 8],
                device_id=device,
                device_id_type=MESH,
            ).start()

        if n == 0:

            @pl.when(is_own)
            def _():
                pltpu.make_async_copy(g.at[v], g_in.at[v], g_recv.at[v]).start()

            pl.when(jnp.logical_not(is_own))(send_pairs)
        else:
            send_pairs()

    def send_on(n):
        s = (x + 4 - n) % 4
        wait_bytes(g_relay.at[s], relay_recv.at[s])
        pltpu.make_async_remote_copy(
            src_ref=g_relay.at[s],
            dst_ref=g_in.at[4 * y_hi + s],
            send_sem=relay_send.at[s],
            recv_sem=g_recv.at[4 * y_hi + s],
            device_id=forward,
            device_id_type=MESH,
        ).start()

    for n in range(2):
        swap_maps(n).start()
    for n in (0, 2):
        send_relayed(n)
        send_direct(n + 1)
    for n in (0, 2):
        pack_pairs(relays[n + 1][0])
        pack_pairs(owners[n][0])

    for n in range(2):
        swap_maps(n).wait()
        for i in range(11 * n, 11 * n + 11):
            y = layer_norm(sib[i]).astype(BF16)
            rest[i, 0:128, :] = y[0:128]
            rest[i, 176:224, :] = y[128:176]
        for i in range(11 * n, 11 * n + 11):
            projected = lax.dot_general(weight, rest[i], NT, preferred_element_type=F32)
            factors(i, 1, projected[:, 0:128])
            factors(i, 2, projected[:, 128:256])

    def pack_factors(chip):
        rows = pl.ds(pl.multiple_of(chip * 48, 48), 48)
        for t in range(3):
            lr[chip, :, 128 * t : 128 * (t + 1)] = lr32[t, rows, :].astype(BF16)

    for hop in HOPS:
        device, chip = chip_at(row, col, hop)
        pack_factors(chip)
        pltpu.make_async_remote_copy(
            src_ref=lr.at[chip],
            dst_ref=lr_in.at[me],
            send_sem=lr_send,
            recv_sem=lr_recv.at[row // 2],
            device_id=device,
            device_id_type=MESH,
        ).start()
    pack_factors(me)
    pltpu.make_async_copy(lr.at[me], lr_in.at[me], lr_recv.at[row // 2]).start()

    for n in (0, 2):
        send_relayed(n + 1)
        send_direct(n)
    for n in (0, 2):
        send_on(n)

    @pl.loop(0, BLOCKS // 2)
    def _(n):
        b = (row // 2 + n) % 16
        wait_bytes(lr_in.at[pl.ds(pl.multiple_of(4 * b, 4), 4)], lr_recv.at[b])
        for low in range(2):
            one = lr_in[4 * b + low].astype(F32)
            two = lr_in[4 * b + 2 + low].astype(F32)
            rows = pl.ds(pl.multiple_of(48 * b, 48), 48)
            lanes = slice(LANES * low, LANES * (low + 1))
            left[rows, lanes] = jnp.concatenate([one[:24], two[:24]], axis=0).astype(BF16)
            right[rows, lanes] = jnp.concatenate([one[24:], two[24:]], axis=0).astype(BF16)

    for n in range(2):
        acc = lax.dot_general(right[384 * n : 384 * (n + 1), :], left[...], NT, preferred_element_type=F32)
        for b in range(16):
            for low in range(2):
                for k in range(3):
                    p[k, 32 * n + 2 * b + low] = acc[
                        24 * b + 8 * k : 24 * b + 8 * k + 8, LANES * low : LANES * (low + 1)
                    ].astype(BF16)

    for n in (1, 3):
        send_on(n)
    for k in range(3):
        pltpu.make_async_copy(p.at[k, me], p_in.at[k, me], p_recv.at[k]).start()
        for hop in HOPS:
            device, chip = chip_at(row, col, hop)
            pltpu.make_async_remote_copy(
                src_ref=p.at[k, chip],
                dst_ref=p_in.at[k, me],
                send_sem=p_send.at[k],
                recv_sem=p_recv.at[k],
                device_id=device,
                device_id_type=MESH,
            ).start()

    for s in range(8):
        wait_bytes(g_in.at[s], g_recv.at[s])

    @pl.loop(0, 2)
    def _(n):
        for u in range(11):
            j = 11 * n + u
            pairs = jnp.concatenate([g_in[s, j].astype(F32) for s in range(8)], axis=0).astype(BF16)
            gates[j] = sigmoid(jnp.dot(pairs, gate_weight_ref[...], preferred_element_type=F32))

    gains[...] = jnp.broadcast_to(out_gain_ref[...], (128, 128)).T
    ws[...] = out_weight_ref[...].astype(F32)
    ours = pl.ds(pl.multiple_of(HALF * half, HALF), HALF)
    theirs = pl.ds(pl.multiple_of(HALF - HALF * half, HALF), HALF)
    gain = jnp.concatenate([gains[ours, :], gains[theirs, :]], axis=0)
    gain = jnp.concatenate([gain, gain], axis=1)
    out_weight = jnp.concatenate([ws[ours, :], ws[theirs, :]], axis=0).astype(BF16)

    for k, (start, stop) in enumerate(GROUPS):
        wait_bytes(p_in.at[k], p_recv.at[k])
        swap = pltpu.make_async_remote_copy(
            src_ref=p_in.at[k, :, :, pl.ds(pl.multiple_of(128 - 128 * half, 128), 256)],
            dst_ref=p_sib.at[k],
            send_sem=sib_send.at[k],
            recv_sem=sib_recv.at[k],
            device_id=sibling,
            device_id_type=MESH,
        )
        swap.start()
        for t in range(2):
            lanes = pl.ds(pl.multiple_of(128 * half + 128 * t, 128), 128)
            p32[t, 0:512, :] = p_in[k, :, :, lanes].astype(F32).reshape(512, 128)
        swap.wait()
        for t in range(2):
            p32[t, 512:1024, :] = p_sib[k, :, :, 128 * t : 128 * (t + 1)].astype(F32).reshape(512, 128)
        for j in range(start, stop):
            u = j - start
            q = jnp.concatenate([p32[t, pl.ds(u, CHANNELS, stride=8), :] for t in range(2)], axis=1)
            center = q - jnp.mean(q, axis=0, keepdims=True)
            spread = jnp.mean(center * center, axis=0, keepdims=True)
            hidden = (center * lax.rsqrt(spread + 1e-05) * gain).astype(BF16)
            mixed[u] = lax.dot_general(hidden, out_weight, TN, preferred_element_type=F32)
            update = gates[j] * mixed[u, pl.ds(pl.multiple_of(64 * half, 64), 192), :]
            for s in range(8):
                packed[u, 22 * s : 22 * s + 24, :] = update[24 * s : 24 * s + 24]
            out[j] = packed[u, 0:COLS, :].astype(BF16)
        group = pl.ds(start, stop - start)
        pltpu.make_async_copy(out.at[group], out_ref.at[group], out_sem.at[k]).start()

    for k, (start, stop) in enumerate(GROUPS):
        group = pl.ds(start, stop - start)
        pltpu.make_async_copy(out.at[group], out_ref.at[group], out_sem.at[k]).wait()
    wait_bytes(lr.at[pl.ds(0, 63)], lr_send)
    for k in range(3):
        wait_bytes(p.at[k, pl.ds(0, 63)], p_send.at[k])
    for v, _ in relays + owners[1:]:
        wait_bytes(g.at[v], g_send.at[v])
    for s in range(4):
        wait_bytes(g_relay.at[s], relay_send.at[s])

    @pl.when(jnp.logical_not(is_own))
    def _():
        wait_bytes(g.at[owners[0][0]], g_send.at[owners[0][0]])


def fused(*args):
    vmem = pl.BlockSpec(memory_space=pltpu.VMEM)
    return pl.pallas_call(
        kernel,
        out_shape=jax.ShapeDtypeStruct((ROWS, COLS, 128), BF16),
        in_specs=[pl.BlockSpec(memory_space=pl.ANY)] + [vmem] * 5,
        out_specs=pl.BlockSpec(memory_space=pl.ANY),
        scratch_shapes=[
            pltpu.VMEM((ROWS, COLS, 128), BF16),
            pltpu.VMEM((ROWS, COLS, 128), BF16),
            pltpu.VMEM((512, 128), F32),
            pltpu.VMEM((ROWS, 128, 128), BF16),
            pltpu.VMEM((ROWS, 256, 128), BF16),
            pltpu.VMEM((3, HALF * 48, 128), F32),
            pltpu.VMEM((COLS * ROWS_PAD, 128), F32),
            pltpu.VMEM((64, 48, LANES), BF16),
            pltpu.VMEM((8, ROWS, ROWS_PAD, 128), BF16),
            pltpu.VMEM((4, ROWS, ROWS_PAD, 128), BF16),
            pltpu.VMEM((64, 48, LANES), BF16),
            pltpu.VMEM((8, ROWS, ROWS_PAD, 128), BF16),
            pltpu.VMEM((768, 768), BF16),
            pltpu.VMEM((768, 768), BF16),
            pltpu.VMEM((3, 64, 8, LANES), BF16),
            pltpu.VMEM((3, 64, 8, LANES), BF16),
            pltpu.VMEM((3, 64, 8, 256), BF16),
            pltpu.VMEM((2, CHANNELS * 8, 128), F32),
            pltpu.VMEM((ROWS, 192, 128), F32),
            pltpu.VMEM((128, 128), F32),
            pltpu.VMEM((128, 128), F32),
            pltpu.VMEM((8, 256, 128), F32),
            pltpu.VMEM((8, 184, 128), F32),
            pltpu.VMEM((ROWS, COLS, 128), BF16),
            pltpu.SemaphoreType.DMA,
            pltpu.SemaphoreType.DMA((2,)),
            pltpu.SemaphoreType.DMA((2,)),
            pltpu.SemaphoreType.DMA,
            pltpu.SemaphoreType.DMA((16,)),
            pltpu.SemaphoreType.DMA((8,)),
            pltpu.SemaphoreType.DMA((8,)),
            pltpu.SemaphoreType.DMA((4,)),
            pltpu.SemaphoreType.DMA((4,)),
            pltpu.SemaphoreType.DMA((3,)),
            pltpu.SemaphoreType.DMA((3,)),
            pltpu.SemaphoreType.DMA((3,)),
            pltpu.SemaphoreType.DMA((3,)),
            pltpu.SemaphoreType.DMA((3,)),
        ],
        compiler_params=pltpu.CompilerParams(
            collective_id=0, has_side_effects=True, vmem_limit_bytes=VMEM_LIMIT
        ),
        name="triangle_update",
    )(*args)


def copy_kernel(src_ref, dst_ref, sems):
    copies = [pltpu.make_async_copy(src_ref.at[i], dst_ref.at[i], sems.at[i]) for i in range(ROWS)]
    for copy in copies:
        copy.start()
    for copy in copies:
        copy.wait()


def copy_out(x):
    return pl.pallas_call(
        copy_kernel,
        out_shape=jax.ShapeDtypeStruct(x.shape, x.dtype),
        in_specs=[pl.BlockSpec(memory_space=pl.ANY)],
        out_specs=pl.BlockSpec(memory_space=pl.ANY),
        scratch_shapes=[pltpu.SemaphoreType.DMA((ROWS,))],
        name="copy_out",
    )(x)


def body(pair_map, in_gain, project_weight, gate_weight, out_gain, out_weight):
    update = fused(
        pair_map, in_gain.reshape(1, 128), project_weight, gate_weight, out_gain.reshape(1, 128), out_weight
    )
    return copy_out(update)


def solution(mesh):
    return jax.shard_map(
        body,
        mesh=mesh,
        in_specs=(P("row", "col", None), P(), P(), P(), P(), P()),
        out_specs=P("row", "col", None),
        check_vma=False,
    )
```

```python
import functools

import jax
import jax.numpy as jnp
from jax import lax
from jax.experimental import pallas as pl
from jax.experimental.pallas import tpu as pltpu
from jax.sharding import PartitionSpec as P

MESH = pl.DeviceIdType.MESH
F32 = jnp.float32
BF16 = jnp.bfloat16
VMEM_LIMIT = 56 * 2**20

ROWS = 22
ROWS_PAD = 24
COLS = 176
CHANNELS = 128
HALF = 64
LANES = 384
BLOCKS = 32
NT = (((1,), (1,)), ((), ()))
TN = (((0,), (0,)), ((), ()))


def sigmoid(x):
    return 0.5 * jnp.tanh(0.5 * x) + 0.5


def place():
    row = lax.axis_index("row")
    col = lax.axis_index("col")
    return row, col


def chip_at(row, col, hop):
    z, y, x = row // 8, ((row // 4) % 2) * 2 + col // 2, row % 4
    z, y, x = (z + hop[0]) % 4, (y + hop[1]) % 4, (x + hop[2]) % 4
    row2 = z * 8 + (y // 2) * 4 + x
    low = y % 2
    return {"row": row2, "col": low * 2 + col % 2}, row2 * 2 + low


def hop_order():
    left = [(a, b, c) for a in range(4) for b in range(4) for c in range(4)][1:]
    use = [0] * 6
    order = []

    def after(hop):
        then = list(use)
        for axis, step in enumerate(hop):
            then[2 * axis] += (0, 2, 2, 0)[step]
            then[2 * axis + 1] += (0, 0, 2, 2)[step]
        return then

    def score(hop):
        then = after(hop)
        return max(then) - min(then), sum(v * v for v in then), (hop[0] * 37 + hop[1] * 11 + hop[2] * 5) % 17

    while left:
        best = min(left, key=score)
        use = after(best)
        left.remove(best)
        order.append(best)
    return order


HOPS = hop_order()
GROUPS = ((0, 8), (8, 16), (16, 22))


def wait_bytes(ref, sem):
    pltpu.make_async_copy(ref, ref, sem).wait()


def kernel(
    own_ref, gain_ref, weight_ref, gate_weight_ref, out_gain_ref, out_weight_ref, out_ref,
    own, wt, main, rest, main32, rest32, g32, lr, g, g_relay, lr_in, g_in, left, right, p, p_in, p_sib, p32, gates, gains, ws, mixed, packed,
    own_sem, map_send, map_recv, lr_send, lr_recv, g_send, g_recv, relay_send, relay_recv, p_send, p_recv, sib_send, sib_recv,
):
    row, col = place()
    half = col % 2
    me = row * 2 + col // 2
    sibling = {"row": row, "col": col + 1 - 2 * half}
    barrier = pltpu.get_barrier_semaphore()

    def signal(device):
        pl.semaphore_signal(barrier, inc=1, device_id=device, device_id_type=MESH)

    z, y_hi, x = row // 8, (row // 4) % 2, row % 4
    base = 8 * col + 4 * y_hi
    other = (z + 2) % 4
    owners, relays = [], []
    for n in range(4):
        x2 = (x + n) % 4
        owners.append((4 * y_hi + x2, {"row": base + x2, "col": z}))
        relays.append((4 - 4 * y_hi + x2, {"row": base + x2, "col": other}))
    forward = {"row": row + 4 - 8 * y_hi, "col": (col + 2) % 4}
    is_own = z == col

    signal(sibling)
    for hop in HOPS:
        device, _ = chip_at(row, col, hop)
        signal(device)
        signal({"row": device["row"], "col": device["col"] + 1 - 2 * half})

    own_copy = pltpu.make_async_copy(own_ref, own, own_sem)
    own_copy.start()

    wt[...] = weight_ref[...].astype(F32).T
    parts = [wt[pl.ds(pl.multiple_of(128 * n + HALF * half, HALF), HALF), :] for n in range(4)]
    weight = jnp.concatenate(parts, axis=0).astype(BF16)
    weight_all = wt[...].astype(BF16)
    ones = jnp.full((128, 128), 1.0 / 128, BF16)
    rest[:, 96:128, :] = jnp.zeros((ROWS, 32, 128), BF16)
    for pad in (22, 23, 46, 47):
        main32[pl.ds(pad, CHANNELS, stride=48), :] = jnp.zeros((CHANNELS, 128), F32)
        rest32[pl.ds(pad, HALF, stride=48), :] = jnp.zeros((HALF, 128), F32)
    for pad in (22, 23):
        g32[pl.ds(pad, COLS, stride=ROWS_PAD), :] = jnp.zeros((COLS, 128), F32)

    own_copy.wait()

    @pl.loop(0, 2)
    def _(n):
        for u in range(11):
            i = 11 * n + u
            v = own[i]
            center = v.astype(F32) - jnp.dot(v, ones, preferred_element_type=F32)
            spread = jnp.dot((center * center).astype(BF16), ones, preferred_element_type=F32)
            y = center * lax.rsqrt(spread + 1e-05) * gain_ref[...]
            main[i] = y[0:128].astype(BF16)
            rest[i, 0:48, :] = y[128:176].astype(BF16)
            g32[pl.ds(i, COLS, stride=ROWS_PAD), :] = y

    def factors(target, rows, n, weights, normed):
        projected = lax.dot_general(weights, normed.reshape(256, 128), NT, preferred_element_type=F32)
        one = sigmoid(projected[0:rows]) * projected[rows : 2 * rows]
        two = sigmoid(projected[2 * rows : 3 * rows]) * projected[3 * rows :]
        for u in range(2):
            lanes = slice(128 * u, 128 * (u + 1))
            target[pl.ds(2 * n + u, rows, stride=48), :] = one[:, lanes]
            target[pl.ds(24 + 2 * n + u, rows, stride=48), :] = two[:, lanes]

    for n in range(11):
        factors(main32, CHANNELS, n, weight_all, main[2 * n : 2 * n + 2])

    pl.semaphore_wait(barrier, 127)

    swap_rest = pltpu.make_async_remote_copy(
        src_ref=rest.at[:, pl.ds(0, 48), :],
        dst_ref=rest.at[:, pl.ds(48, 48), :],
        send_sem=map_send,
        recv_sem=map_recv,
        device_id=sibling,
        device_id_type=MESH,
    )
    swap_rest.start()

    def pack(source, channel):
        return source[pl.ds(pl.multiple_of(channel * 48, 48), 48), :].astype(BF16)

    def send_main(device, channel):
        lr[channel] = pack(main32, channel)
        pltpu.make_async_remote_copy(
            src_ref=lr.at[channel],
            dst_ref=lr_in.at[me, half],
            send_sem=lr_send.at[0],
            recv_sem=lr_recv.at[row // 2],
            device_id=device,
            device_id_type=MESH,
        ).start()

    for hop in HOPS:
        device, chip = chip_at(row, col, hop)
        send_main(device, HALF * half + chip)
        send_main({"row": device["row"], "col": device["col"] + 1 - 2 * half}, HALF - HALF * half + chip)
    send_main(sibling, HALF - HALF * half + me)
    lr[HALF * half + me] = pack(main32, HALF * half + me)
    pltpu.make_async_copy(lr.at[HALF * half + me], lr_in.at[me, half], lr_recv.at[row // 2]).start()

    swap_rest.wait()
    for n in range(11):
        factors(rest32, HALF, n, weight, rest[2 * n : 2 * n + 2])
    for hop in HOPS:
        device, chip = chip_at(row, col, hop)
        lr[CHANNELS + chip] = pack(rest32, chip)
        pltpu.make_async_remote_copy(
            src_ref=lr.at[CHANNELS + chip],
            dst_ref=lr_in.at[me, 2],
            send_sem=lr_send.at[1],
            recv_sem=lr_recv.at[row // 2],
            device_id=device,
            device_id_type=MESH,
        ).start()
    lr[CHANNELS + me] = pack(rest32, me)
    pltpu.make_async_copy(lr.at[CHANNELS + me], lr_in.at[me, 2], lr_recv.at[row // 2]).start()

    def pack_pairs(v):
        for n in range(2):
            rows = pl.ds(pl.multiple_of((22 * v + 11 * n) * ROWS_PAD, 8), 11 * ROWS_PAD)
            g[v, pl.ds(11 * n, 11)] = g32[rows, :].reshape(11, ROWS_PAD, 128).astype(BF16)

    for n in range(4):
        v, device = relays[n]
        pack_pairs(v)
        pltpu.make_async_remote_copy(
            src_ref=g.at[v],
            dst_ref=g_relay.at[x],
            send_sem=g_send.at[v],
            recv_sem=relay_recv.at[x],
            device_id=device,
            device_id_type=MESH,
        ).start()

        m = (n + 1) % 4
        v, device = owners[m]
        pack_pairs(v)

        def send_pairs():
            pltpu.make_async_remote_copy(
                src_ref=g.at[v],
                dst_ref=g_in.at[row % 8],
                send_sem=g_send.at[v],
                recv_sem=g_recv.at[row % 8],
                device_id=device,
                device_id_type=MESH,
            ).start()

        if m == 0:

            @pl.when(is_own)
            def _():
                pltpu.make_async_copy(g.at[v], g_in.at[v], g_recv.at[v]).start()

            pl.when(jnp.logical_not(is_own))(send_pairs)
        else:
            send_pairs()

    def send_on(n):
        s = (x + 4 - n) % 4
        wait_bytes(g_relay.at[s], relay_recv.at[s])
        pltpu.make_async_remote_copy(
            src_ref=g_relay.at[s],
            dst_ref=g_in.at[4 * y_hi + s],
            send_sem=relay_send.at[s],
            recv_sem=g_recv.at[4 * y_hi + s],
            device_id=forward,
            device_id_type=MESH,
        ).start()

    @pl.loop(0, BLOCKS // 2)
    def _(n):
        b = (row // 2 + n) % 16
        wait_bytes(lr_in.at[pl.ds(pl.multiple_of(4 * b, 4), 4)], lr_recv.at[b])
        for low in range(2):
            for t in range(3):
                one = lr_in[4 * b + low, t].astype(F32)
                two = lr_in[4 * b + 2 + low, t].astype(F32)
                rows = pl.ds(pl.multiple_of(48 * b, 48), 48)
                lanes = slice(LANES * low + 128 * t, LANES * low + 128 * (t + 1))
                left[rows, lanes] = jnp.concatenate([one[:24], two[:24]], axis=0).astype(BF16)
                right[rows, lanes] = jnp.concatenate([one[24:], two[24:]], axis=0).astype(BF16)

    for n in range(2):
        acc = lax.dot_general(right[384 * n : 384 * (n + 1), :], left[...], NT, preferred_element_type=F32)
        for b in range(16):
            for low in range(2):
                for k in range(3):
                    p[k, 32 * n + 2 * b + low] = acc[
                        24 * b + 8 * k : 24 * b + 8 * k + 8, LANES * low : LANES * (low + 1)
                    ].astype(BF16)

    for k in range(3):
        pltpu.make_async_copy(p.at[k, me], p_in.at[k, me], p_recv.at[k]).start()
        for hop in HOPS:
            device, chip = chip_at(row, col, hop)
            pltpu.make_async_remote_copy(
                src_ref=p.at[k, chip],
                dst_ref=p_in.at[k, me],
                send_sem=p_send.at[k],
                recv_sem=p_recv.at[k],
                device_id=device,
                device_id_type=MESH,
            ).start()
        if k == 0:
            for n in range(4):
                send_on(n)

    for s in range(8):
        wait_bytes(g_in.at[s], g_recv.at[s])

    @pl.loop(0, 2)
    def _(n):
        for u in range(11):
            j = 11 * n + u
            pairs = jnp.concatenate([g_in[s, j].astype(F32) for s in range(8)], axis=0).astype(BF16)
            gates[j] = sigmoid(jnp.dot(pairs, gate_weight_ref[...], preferred_element_type=F32))

    gains[...] = jnp.broadcast_to(out_gain_ref[...], (128, 128)).T
    ws[...] = out_weight_ref[...].astype(F32)
    ours = pl.ds(pl.multiple_of(HALF * half, HALF), HALF)
    theirs = pl.ds(pl.multiple_of(HALF - HALF * half, HALF), HALF)
    gain = jnp.concatenate([gains[ours, :], gains[theirs, :]], axis=0)
    gain = jnp.concatenate([gain, gain], axis=1)
    out_weight = jnp.concatenate([ws[ours, :], ws[theirs, :]], axis=0).astype(BF16)

    for k, (start, stop) in enumerate(GROUPS):
        wait_bytes(p_in.at[k], p_recv.at[k])
        swap = pltpu.make_async_remote_copy(
            src_ref=p_in.at[k, :, :, pl.ds(pl.multiple_of(128 - 128 * half, 128), 256)],
            dst_ref=p_sib.at[k],
            send_sem=sib_send.at[k],
            recv_sem=sib_recv.at[k],
            device_id=sibling,
            device_id_type=MESH,
        )
        swap.start()
        for t in range(2):
            lanes = pl.ds(pl.multiple_of(128 * half + 128 * t, 128), 128)
            p32[t, 0:512, :] = p_in[k, :, :, lanes].astype(F32).reshape(512, 128)
        swap.wait()
        for t in range(2):
            p32[t, 512:1024, :] = p_sib[k, :, :, 128 * t : 128 * (t + 1)].astype(F32).reshape(512, 128)
        for j in range(start, stop):
            u = j - start
            q = jnp.concatenate([p32[t, pl.ds(u, CHANNELS, stride=8), :] for t in range(2)], axis=1)
            center = q - jnp.mean(q, axis=0, keepdims=True)
            spread = jnp.mean(center * center, axis=0, keepdims=True)
            hidden = (center * lax.rsqrt(spread + 1e-05) * gain).astype(BF16)
            mixed[u] = lax.dot_general(hidden, out_weight, TN, preferred_element_type=F32)
            update = gates[j] * mixed[u, pl.ds(pl.multiple_of(64 * half, 64), 192), :]
            for s in range(8):
                packed[u, 22 * s : 22 * s + 24, :] = update[24 * s : 24 * s + 24]
            out_ref[j] = packed[u, 0:COLS, :].astype(BF16)

    wait_bytes(lr.at[pl.ds(0, 127)], lr_send.at[0])
    wait_bytes(lr.at[pl.ds(0, 63)], lr_send.at[1])
    for k in range(3):
        wait_bytes(p.at[k, pl.ds(0, 63)], p_send.at[k])
    for v, _ in relays + owners[1:]:
        wait_bytes(g.at[v], g_send.at[v])
    for s in range(4):
        wait_bytes(g_relay.at[s], relay_send.at[s])

    @pl.when(jnp.logical_not(is_own))
    def _():
        wait_bytes(g.at[owners[0][0]], g_send.at[owners[0][0]])


def fused(*args):
    vmem = pl.BlockSpec(memory_space=pltpu.VMEM)
    return pl.pallas_call(
        kernel,
        out_shape=jax.ShapeDtypeStruct((ROWS, COLS, 128), BF16),
        in_specs=[pl.BlockSpec(memory_space=pl.ANY)] + [vmem] * 5,
        out_specs=vmem,
        scratch_shapes=[
            pltpu.VMEM((ROWS, COLS, 128), BF16),
            pltpu.VMEM((512, 128), F32),
            pltpu.VMEM((ROWS, 128, 128), BF16),
            pltpu.VMEM((ROWS, 128, 128), BF16),
            pltpu.VMEM((CHANNELS * 48, 128), F32),
            pltpu.VMEM((HALF * 48, 128), F32),
            pltpu.VMEM((COLS * ROWS_PAD, 128), F32),
            pltpu.VMEM((CHANNELS + HALF, 48, 128), BF16),
            pltpu.VMEM((8, ROWS, ROWS_PAD, 128), BF16),
            pltpu.VMEM((4, ROWS, ROWS_PAD, 128), BF16),
            pltpu.VMEM((64, 3, 48, 128), BF16),
            pltpu.VMEM((8, ROWS, ROWS_PAD, 128), BF16),
            pltpu.VMEM((768, 768), BF16),
            pltpu.VMEM((768, 768), BF16),
            pltpu.VMEM((3, 64, 8, LANES), BF16),
            pltpu.VMEM((3, 64, 8, LANES), BF16),
            pltpu.VMEM((3, 64, 8, 256), BF16),
            pltpu.VMEM((2, CHANNELS * 8, 128), F32),
            pltpu.VMEM((ROWS, 192, 128), F32),
            pltpu.VMEM((128, 128), F32),
            pltpu.VMEM((128, 128), F32),
            pltpu.VMEM((8, 256, 128), F32),
            pltpu.VMEM((8, 184, 128), F32),
            pltpu.SemaphoreType.DMA,
            pltpu.SemaphoreType.DMA,
            pltpu.SemaphoreType.DMA,
            pltpu.SemaphoreType.DMA((2,)),
            pltpu.SemaphoreType.DMA((16,)),
            pltpu.SemaphoreType.DMA((8,)),
            pltpu.SemaphoreType.DMA((8,)),
            pltpu.SemaphoreType.DMA((4,)),
            pltpu.SemaphoreType.DMA((4,)),
            pltpu.SemaphoreType.DMA((3,)),
            pltpu.SemaphoreType.DMA((3,)),
            pltpu.SemaphoreType.DMA((3,)),
            pltpu.SemaphoreType.DMA((3,)),
        ],
        compiler_params=pltpu.CompilerParams(
            collective_id=0, has_side_effects=True, vmem_limit_bytes=VMEM_LIMIT
        ),
        name="triangle_update",
    )(*args)


def copy_kernel(src_ref, dst_ref, sems):
    copies = [pltpu.make_async_copy(src_ref.at[i], dst_ref.at[i], sems.at[i]) for i in range(ROWS)]
    for copy in copies:
        copy.start()
    for copy in copies:
        copy.wait()


def copy_out(x):
    return pl.pallas_call(
        copy_kernel,
        out_shape=jax.ShapeDtypeStruct(x.shape, x.dtype),
        in_specs=[pl.BlockSpec(memory_space=pltpu.VMEM)],
        out_specs=pl.BlockSpec(memory_space=pl.ANY),
        scratch_shapes=[pltpu.SemaphoreType.DMA((ROWS,))],
        name="copy_out",
    )(x)


def body(pair_map, in_gain, project_weight, gate_weight, out_gain, out_weight):
    update = fused(
        pair_map, in_gain.reshape(1, 128), project_weight, gate_weight, out_gain.reshape(1, 128), out_weight
    )
    return copy_out(update)


def solution(mesh):
    return jax.shard_map(
        body,
        mesh=mesh,
        in_specs=(P("row", "col", None), P(), P(), P(), P(), P()),
        out_specs=P("row", "col", None),
        check_vma=False,
    )
```

```python
import functools

import jax
import jax.numpy as jnp
from jax import lax
from jax.experimental import pallas as pl
from jax.experimental.pallas import tpu as pltpu
from jax.sharding import PartitionSpec as P

MESH = pl.DeviceIdType.MESH
F32 = jnp.float32
BF16 = jnp.bfloat16
VMEM_LIMIT = 56 * 2**20

ROWS = 22
ROWS_PAD = 24
COLS = 176
CHANNELS = 128
HALF = 64
LANES = 384
BLOCKS = 32
NT = (((1,), (1,)), ((), ()))
TN = (((0,), (0,)), ((), ()))


def sigmoid(x):
    return 0.5 * jnp.tanh(0.5 * x) + 0.5


def place():
    row = lax.axis_index("row")
    col = lax.axis_index("col")
    return row, col


def chip_at(row, col, hop):
    z, y, x = row // 8, ((row // 4) % 2) * 2 + col // 2, row % 4
    z, y, x = (z + hop[0]) % 4, (y + hop[1]) % 4, (x + hop[2]) % 4
    row2 = z * 8 + (y // 2) * 4 + x
    low = y % 2
    return {"row": row2, "col": low * 2 + col % 2}, row2 * 2 + low


def hop_order():
    left = [(a, b, c) for a in range(4) for b in range(4) for c in range(4)][1:]
    use = [0] * 6
    order = []

    def after(hop):
        then = list(use)
        for axis, step in enumerate(hop):
            then[2 * axis] += (0, 2, 2, 0)[step]
            then[2 * axis + 1] += (0, 0, 2, 2)[step]
        return then

    def score(hop):
        then = after(hop)
        return max(then) - min(then), sum(v * v for v in then), (hop[0] * 37 + hop[1] * 11 + hop[2] * 5) % 17

    while left:
        best = min(left, key=score)
        use = after(best)
        left.remove(best)
        order.append(best)
    return order


HOPS = hop_order()
GROUPS = ((0, 8), (8, 16), (16, 22))


def wait_bytes(ref, sem):
    pltpu.make_async_copy(ref, ref, sem).wait()


def kernel(
    own_ref, gain_ref, weight_ref, gate_weight_ref, out_gain_ref, out_weight_ref, out_ref,
    own, wt, main, rest, main32, rest32, g32, lr, g, g_relay, lr_in, g_in, left, right, p, p_in, p_sib, p32, gates, gains, ws, mixed, packed,
    own_sem, map_send, map_recv, lr_send, lr_recv, g_send, g_recv, relay_send, relay_recv, p_send, p_recv, sib_send, sib_recv,
):
    row, col = place()
    half = col % 2
    me = row * 2 + col // 2
    sibling = {"row": row, "col": col + 1 - 2 * half}
    barrier = pltpu.get_barrier_semaphore()

    def signal(device):
        pl.semaphore_signal(barrier, inc=1, device_id=device, device_id_type=MESH)

    z, y_hi, x = row // 8, (row // 4) % 2, row % 4
    base = 8 * col + 4 * y_hi
    other = (z + 2) % 4
    owners, relays = [], []
    for n in range(4):
        x2 = (x + n) % 4
        owners.append((4 * y_hi + x2, {"row": base + x2, "col": z}))
        relays.append((4 - 4 * y_hi + x2, {"row": base + x2, "col": other}))
    forward = {"row": row + 4 - 8 * y_hi, "col": (col + 2) % 4}
    is_own = z == col

    signal(sibling)
    for hop in HOPS:
        device, _ = chip_at(row, col, hop)
        signal(device)
        signal({"row": device["row"], "col": device["col"] + 1 - 2 * half})

    own_copy = pltpu.make_async_copy(own_ref, own, own_sem)
    own_copy.start()

    wt[...] = weight_ref[...].astype(F32).T
    parts = [wt[pl.ds(pl.multiple_of(128 * n + HALF * half, HALF), HALF), :] for n in range(4)]
    weight = jnp.concatenate(parts, axis=0).astype(BF16)
    weight_all = wt[...].astype(BF16)
    ones = jnp.full((128, 128), 1.0 / 128, BF16)
    rest[:, 96:128, :] = jnp.zeros((ROWS, 32, 128), BF16)
    for pad in (22, 23, 46, 47):
        main32[pl.ds(pad, CHANNELS, stride=48), :] = jnp.zeros((CHANNELS, 128), F32)
        rest32[pl.ds(pad, HALF, stride=48), :] = jnp.zeros((HALF, 128), F32)
    for pad in (22, 23):
        g32[pl.ds(pad, COLS, stride=ROWS_PAD), :] = jnp.zeros((COLS, 128), F32)

    own_copy.wait()

    @pl.loop(0, 2)
    def _(n):
        for u in range(11):
            i = 11 * n + u
            v = own[i]
            center = v.astype(F32) - jnp.dot(v, ones, preferred_element_type=F32)
            spread = jnp.dot((center * center).astype(BF16), ones, preferred_element_type=F32)
            y = center * lax.rsqrt(spread + 1e-05) * gain_ref[...]
            main[i] = y[0:128].astype(BF16)
            rest[i, 0:48, :] = y[128:176].astype(BF16)
            g32[pl.ds(i, COLS, stride=ROWS_PAD), :] = y

    def factors(target, rows, n, weights, normed):
        projected = lax.dot_general(weights, normed.reshape(256, 128), NT, preferred_element_type=F32)
        one = sigmoid(projected[0:rows]) * projected[rows : 2 * rows]
        two = sigmoid(projected[2 * rows : 3 * rows]) * projected[3 * rows :]
        for u in range(2):
            lanes = slice(128 * u, 128 * (u + 1))
            target[pl.ds(2 * n + u, rows, stride=48), :] = one[:, lanes]
            target[pl.ds(24 + 2 * n + u, rows, stride=48), :] = two[:, lanes]

    def pack_pairs(v):
        for n in range(2):
            rows = pl.ds(pl.multiple_of((22 * v + 11 * n) * ROWS_PAD, 8), 11 * ROWS_PAD)
            g[v, pl.ds(11 * n, 11)] = g32[rows, :].reshape(11, ROWS_PAD, 128).astype(BF16)

    def send_pairs(n):
        v, device = relays[n]
        pltpu.make_async_remote_copy(
            src_ref=g.at[v],
            dst_ref=g_relay.at[x],
            send_sem=g_send.at[v],
            recv_sem=relay_recv.at[x],
            device_id=device,
            device_id_type=MESH,
        ).start()

        m = (n + 2) % 4
        v2, device2 = owners[m]

        def send_direct():
            pltpu.make_async_remote_copy(
                src_ref=g.at[v2],
                dst_ref=g_in.at[row % 8],
                send_sem=g_send.at[v2],
                recv_sem=g_recv.at[row % 8],
                device_id=device2,
                device_id_type=MESH,
            ).start()

        if m == 0:

            @pl.when(is_own)
            def _():
                pltpu.make_async_copy(g.at[v2], g_in.at[v2], g_recv.at[v2]).start()

            pl.when(jnp.logical_not(is_own))(send_direct)
        else:
            send_direct()

    def send_on(n):
        s = (x + 4 - n) % 4
        wait_bytes(g_relay.at[s], relay_recv.at[s])
        pltpu.make_async_remote_copy(
            src_ref=g_relay.at[s],
            dst_ref=g_in.at[4 * y_hi + s],
            send_sem=relay_send.at[s],
            recv_sem=g_recv.at[4 * y_hi + s],
            device_id=forward,
            device_id_type=MESH,
        ).start()

    for n in (0, 1):
        pack_pairs(relays[n][0])
        pack_pairs(owners[(n + 2) % 4][0])

    for n in range(11):
        factors(main32, CHANNELS, n, weight_all, main[2 * n : 2 * n + 2])

    pl.semaphore_wait(barrier, 127)

    swap_rest = pltpu.make_async_remote_copy(
        src_ref=rest.at[:, pl.ds(0, 48), :],
        dst_ref=rest.at[:, pl.ds(48, 48), :],
        send_sem=map_send,
        recv_sem=map_recv,
        device_id=sibling,
        device_id_type=MESH,
    )
    swap_rest.start()
    send_pairs(0)

    def pack(source, channel):
        return source[pl.ds(pl.multiple_of(channel * 48, 48), 48), :].astype(BF16)

    def send_main(device, channel):
        lr[channel] = pack(main32, channel)
        pltpu.make_async_remote_copy(
            src_ref=lr.at[channel],
            dst_ref=lr_in.at[me, half],
            send_sem=lr_send.at[0],
            recv_sem=lr_recv.at[row // 2],
            device_id=device,
            device_id_type=MESH,
        ).start()

    for hop in HOPS:
        device, chip = chip_at(row, col, hop)
        send_main(device, HALF * half + chip)
        send_main({"row": device["row"], "col": device["col"] + 1 - 2 * half}, HALF - HALF * half + chip)
    send_main(sibling, HALF - HALF * half + me)
    lr[HALF * half + me] = pack(main32, HALF * half + me)
    pltpu.make_async_copy(lr.at[HALF * half + me], lr_in.at[me, half], lr_recv.at[row // 2]).start()

    send_pairs(1)
    swap_rest.wait()
    for n in range(11):
        factors(rest32, HALF, n, weight, rest[2 * n : 2 * n + 2])
    for hop in HOPS:
        device, chip = chip_at(row, col, hop)
        lr[CHANNELS + chip] = pack(rest32, chip)
        pltpu.make_async_remote_copy(
            src_ref=lr.at[CHANNELS + chip],
            dst_ref=lr_in.at[me, 2],
            send_sem=lr_send.at[1],
            recv_sem=lr_recv.at[row // 2],
            device_id=device,
            device_id_type=MESH,
        ).start()
    lr[CHANNELS + me] = pack(rest32, me)
    pltpu.make_async_copy(lr.at[CHANNELS + me], lr_in.at[me, 2], lr_recv.at[row // 2]).start()

    send_on(0)
    for n in (2, 3):
        pack_pairs(relays[n][0])
        pack_pairs(owners[(n + 2) % 4][0])
        send_pairs(n)

    def take(n):
        b = (row // 2 + n) % 16
        wait_bytes(lr_in.at[pl.ds(pl.multiple_of(4 * b, 4), 4)], lr_recv.at[b])
        rows = pl.ds(pl.multiple_of(48 * b, 48), 48)
        for low in range(2):
            for t in range(3):
                one = lr_in[4 * b + low, t].astype(F32)
                two = lr_in[4 * b + 2 + low, t].astype(F32)
                lanes = slice(LANES * low + 128 * t, LANES * low + 128 * (t + 1))
                left[rows, lanes] = jnp.concatenate([one[:24], two[:24]], axis=0).astype(BF16)
                for k in range(3):
                    part = slice(24 + 8 * k, 32 + 8 * k)
                    right[pl.ds(pl.multiple_of(256 * k + 16 * b, 16), 16), lanes] = jnp.concatenate(
                        [one[part], two[part]], axis=0
                    ).astype(BF16)

    pl.loop(0, 8)(take)
    send_on(1)
    pl.loop(8, 16)(take)

    for k in range(3):
        acc = lax.dot_general(right[256 * k : 256 * (k + 1), :], left[...], NT, preferred_element_type=F32)
        for r in range(BLOCKS):
            for low in range(2):
                p[k, 2 * r + low] = acc[8 * r : 8 * r + 8, LANES * low : LANES * (low + 1)].astype(BF16)
        pltpu.make_async_copy(p.at[k, me], p_in.at[k, me], p_recv.at[k]).start()
        for hop in HOPS:
            device, chip = chip_at(row, col, hop)
            pltpu.make_async_remote_copy(
                src_ref=p.at[k, chip],
                dst_ref=p_in.at[k, me],
                send_sem=p_send.at[k],
                recv_sem=p_recv.at[k],
                device_id=device,
                device_id_type=MESH,
            ).start()
        if k < 2:
            send_on(k + 2)

    for s in range(8):
        wait_bytes(g_in.at[s], g_recv.at[s])

    @pl.loop(0, 2)
    def _(n):
        for u in range(11):
            j = 11 * n + u
            pairs = jnp.concatenate([g_in[s, j].astype(F32) for s in range(8)], axis=0).astype(BF16)
            gates[j] = sigmoid(jnp.dot(pairs, gate_weight_ref[...], preferred_element_type=F32))

    gains[...] = jnp.broadcast_to(out_gain_ref[...], (128, 128)).T
    ws[...] = out_weight_ref[...].astype(F32)
    ours = pl.ds(pl.multiple_of(HALF * half, HALF), HALF)
    theirs = pl.ds(pl.multiple_of(HALF - HALF * half, HALF), HALF)
    gain = jnp.concatenate([gains[ours, :], gains[theirs, :]], axis=0)
    gain = jnp.concatenate([gain, gain], axis=1)
    out_weight = jnp.concatenate([ws[ours, :], ws[theirs, :]], axis=0).astype(BF16)

    for k, (start, stop) in enumerate(GROUPS):
        wait_bytes(p_in.at[k], p_recv.at[k])
        swap = pltpu.make_async_remote_copy(
            src_ref=p_in.at[k, :, :, pl.ds(pl.multiple_of(128 - 128 * half, 128), 256)],
            dst_ref=p_sib.at[k],
            send_sem=sib_send.at[k],
            recv_sem=sib_recv.at[k],
            device_id=sibling,
            device_id_type=MESH,
        )
        swap.start()
        for t in range(2):
            lanes = pl.ds(pl.multiple_of(128 * half + 128 * t, 128), 128)
            p32[t, 0:512, :] = p_in[k, :, :, lanes].astype(F32).reshape(512, 128)
        swap.wait()
        for t in range(2):
            p32[t, 512:1024, :] = p_sib[k, :, :, 128 * t : 128 * (t + 1)].astype(F32).reshape(512, 128)
        for j in range(start, stop):
            u = j - start
            q = jnp.concatenate([p32[t, pl.ds(u, CHANNELS, stride=8), :] for t in range(2)], axis=1)
            center = q - jnp.mean(q, axis=0, keepdims=True)
            spread = jnp.mean(center * center, axis=0, keepdims=True)
            hidden = (center * lax.rsqrt(spread + 1e-05) * gain).astype(BF16)
            mixed[u] = lax.dot_general(hidden, out_weight, TN, preferred_element_type=F32)
            update = gates[j] * mixed[u, pl.ds(pl.multiple_of(64 * half, 64), 192), :]
            for s in range(8):
                packed[u, 22 * s : 22 * s + 24, :] = update[24 * s : 24 * s + 24]
            out_ref[j] = packed[u, 0:COLS, :].astype(BF16)

    wait_bytes(lr.at[pl.ds(0, 127)], lr_send.at[0])
    wait_bytes(lr.at[pl.ds(0, 63)], lr_send.at[1])
    for k in range(3):
        wait_bytes(p.at[k, pl.ds(0, 63)], p_send.at[k])
    for v, _ in relays + owners[1:]:
        wait_bytes(g.at[v], g_send.at[v])
    for s in range(4):
        wait_bytes(g_relay.at[s], relay_send.at[s])

    @pl.when(jnp.logical_not(is_own))
    def _():
        wait_bytes(g.at[owners[0][0]], g_send.at[owners[0][0]])


def fused(*args):
    vmem = pl.BlockSpec(memory_space=pltpu.VMEM)
    return pl.pallas_call(
        kernel,
        out_shape=jax.ShapeDtypeStruct((ROWS, COLS, 128), BF16),
        in_specs=[pl.BlockSpec(memory_space=pl.ANY)] + [vmem] * 5,
        out_specs=vmem,
        scratch_shapes=[
            pltpu.VMEM((ROWS, COLS, 128), BF16),
            pltpu.VMEM((512, 128), F32),
            pltpu.VMEM((ROWS, 128, 128), BF16),
            pltpu.VMEM((ROWS, 128, 128), BF16),
            pltpu.VMEM((CHANNELS * 48, 128), F32),
            pltpu.VMEM((HALF * 48, 128), F32),
            pltpu.VMEM((COLS * ROWS_PAD, 128), F32),
            pltpu.VMEM((CHANNELS + HALF, 48, 128), BF16),
            pltpu.VMEM((8, ROWS, ROWS_PAD, 128), BF16),
            pltpu.VMEM((4, ROWS, ROWS_PAD, 128), BF16),
            pltpu.VMEM((64, 3, 48, 128), BF16),
            pltpu.VMEM((8, ROWS, ROWS_PAD, 128), BF16),
            pltpu.VMEM((768, 768), BF16),
            pltpu.VMEM((768, 768), BF16),
            pltpu.VMEM((3, 64, 8, LANES), BF16),
            pltpu.VMEM((3, 64, 8, LANES), BF16),
            pltpu.VMEM((3, 64, 8, 256), BF16),
            pltpu.VMEM((2, CHANNELS * 8, 128), F32),
            pltpu.VMEM((ROWS, 192, 128), F32),
            pltpu.VMEM((128, 128), F32),
            pltpu.VMEM((128, 128), F32),
            pltpu.VMEM((8, 256, 128), F32),
            pltpu.VMEM((8, 184, 128), F32),
            pltpu.SemaphoreType.DMA,
            pltpu.SemaphoreType.DMA,
            pltpu.SemaphoreType.DMA,
            pltpu.SemaphoreType.DMA((2,)),
            pltpu.SemaphoreType.DMA((16,)),
            pltpu.SemaphoreType.DMA((8,)),
            pltpu.SemaphoreType.DMA((8,)),
            pltpu.SemaphoreType.DMA((4,)),
            pltpu.SemaphoreType.DMA((4,)),
            pltpu.SemaphoreType.DMA((3,)),
            pltpu.SemaphoreType.DMA((3,)),
            pltpu.SemaphoreType.DMA((3,)),
            pltpu.SemaphoreType.DMA((3,)),
        ],
        compiler_params=pltpu.CompilerParams(
            collective_id=0, has_side_effects=True, vmem_limit_bytes=VMEM_LIMIT
        ),
        name="triangle_update",
    )(*args)


def copy_kernel(src_ref, dst_ref, held, in_sems, out_sems):
    ins = [pltpu.make_async_copy(src_ref.at[i], held.at[i], in_sems.at[i]) for i in range(ROWS)]
    outs = [pltpu.make_async_copy(held.at[i], dst_ref.at[i], out_sems.at[i]) for i in range(ROWS)]
    for copy in ins:
        copy.start()
    for i in range(ROWS):
        ins[i].wait()
        outs[i].start()
    for copy in outs:
        copy.wait()


def copy_out(x):
    return pl.pallas_call(
        copy_kernel,
        out_shape=jax.ShapeDtypeStruct(x.shape, x.dtype),
        in_specs=[pl.BlockSpec(memory_space=pl.ANY)],
        out_specs=pl.BlockSpec(memory_space=pl.ANY),
        scratch_shapes=[
            pltpu.VMEM(x.shape, x.dtype),
            pltpu.SemaphoreType.DMA((ROWS,)),
            pltpu.SemaphoreType.DMA((ROWS,)),
        ],
        name="copy_out",
    )(x)


def body(pair_map, in_gain, project_weight, gate_weight, out_gain, out_weight):
    update = fused(
        pair_map, in_gain.reshape(1, 128), project_weight, gate_weight, out_gain.reshape(1, 128), out_weight
    )
    return copy_out(update)


def solution(mesh):
    return jax.shard_map(
        body,
        mesh=mesh,
        in_specs=(P("row", "col", None), P(), P(), P(), P(), P()),
        out_specs=P("row", "col", None),
        check_vma=False,
    )
```

```python
import functools

import jax
import jax.numpy as jnp
from jax import lax
from jax.experimental import pallas as pl
from jax.experimental.pallas import tpu as pltpu
from jax.sharding import PartitionSpec as P

MESH = pl.DeviceIdType.MESH
F32 = jnp.float32
BF16 = jnp.bfloat16
VMEM_LIMIT = 56 * 2**20

ROWS = 22
ROWS_PAD = 24
COLS = 176
CHANNELS = 128
HALF = 64
LANES = 384
BLOCKS = 32
NT = (((1,), (1,)), ((), ()))
TN = (((0,), (0,)), ((), ()))


def sigmoid(x):
    return 0.5 * jnp.tanh(0.5 * x) + 0.5


def place():
    row = lax.axis_index("row")
    col = lax.axis_index("col")
    return row, col


def chip_at(row, col, hop):
    z, y, x = row // 8, ((row // 4) % 2) * 2 + col // 2, row % 4
    z, y, x = (z + hop[0]) % 4, (y + hop[1]) % 4, (x + hop[2]) % 4
    row2 = z * 8 + (y // 2) * 4 + x
    low = y % 2
    return {"row": row2, "col": low * 2 + col % 2}, row2 * 2 + low


def hop_order():
    left = [(a, b, c) for a in range(4) for b in range(4) for c in range(4)][1:]
    use = [0] * 6
    order = []

    def after(hop):
        then = list(use)
        for axis, step in enumerate(hop):
            then[2 * axis] += (0, 2, 2, 0)[step]
            then[2 * axis + 1] += (0, 0, 2, 2)[step]
        return then

    def score(hop):
        then = after(hop)
        return max(then) - min(then), sum(v * v for v in then), (hop[0] * 37 + hop[1] * 11 + hop[2] * 5) % 17

    while left:
        best = min(left, key=score)
        use = after(best)
        left.remove(best)
        order.append(best)
    return order


HOPS = hop_order()
GROUPS = ((0, 8), (8, 16), (16, 22))


def wait_bytes(ref, sem):
    pltpu.make_async_copy(ref, ref, sem).wait()


def kernel(
    own_ref, gain_ref, weight_ref, gate_weight_ref, out_gain_ref, out_weight_ref, out_ref,
    own, wt, main, rest, main32, rest32, g32, lr_a, lr_b, g, g_relay, lr_a_in, lr_b_in, g_in, left, right, p, p_in, p_sib, p32, gates, gains, ws, mixed, packed,
    own_sem, map_send, map_recv, lr_send, lr_a_recv, lr_b_recv, g_send, g_recv, relay_send, relay_recv, p_send, p_recv, sib_send, sib_recv,
):
    row, col = place()
    half = col % 2
    me = row * 2 + col // 2
    sibling = {"row": row, "col": col + 1 - 2 * half}
    barrier = pltpu.get_barrier_semaphore()

    def signal(device):
        pl.semaphore_signal(barrier, inc=1, device_id=device, device_id_type=MESH)

    z, y_hi, x = row // 8, (row // 4) % 2, row % 4
    base = 8 * col + 4 * y_hi
    other = (z + 2) % 4
    owners, relays = [], []
    for n in range(4):
        x2 = (x + n) % 4
        owners.append((4 * y_hi + x2, {"row": base + x2, "col": z}))
        relays.append((4 - 4 * y_hi + x2, {"row": base + x2, "col": other}))
    forward = {"row": row + 4 - 8 * y_hi, "col": (col + 2) % 4}
    is_own = z == col

    signal(sibling)
    for hop in HOPS:
        device, _ = chip_at(row, col, hop)
        signal(device)
        signal({"row": device["row"], "col": device["col"] + 1 - 2 * half})

    own_copy = pltpu.make_async_copy(own_ref, own, own_sem)
    own_copy.start()

    wt[...] = weight_ref[...].astype(F32).T
    parts = [wt[pl.ds(pl.multiple_of(128 * n + HALF * half, HALF), HALF), :] for n in range(4)]
    weight = jnp.concatenate(parts, axis=0).astype(BF16)
    weight_all = wt[...].astype(BF16)
    ones = jnp.full((128, 128), 1.0 / 128, BF16)
    rest[:, 96:128, :] = jnp.zeros((ROWS, 32, 128), BF16)
    for pad in (22, 23, 46, 47):
        main32[pl.ds(pad, CHANNELS, stride=48), :] = jnp.zeros((CHANNELS, 128), F32)
        rest32[pl.ds(pad, HALF, stride=48), :] = jnp.zeros((HALF, 128), F32)
    for pad in (22, 23):
        g32[pl.ds(pad, COLS, stride=ROWS_PAD), :] = jnp.zeros((COLS, 128), F32)

    own_copy.wait()

    @pl.loop(0, 2)
    def _(n):
        for u in range(11):
            i = 11 * n + u
            v = own[i]
            center = v.astype(F32) - jnp.dot(v, ones, preferred_element_type=F32)
            spread = jnp.dot((center * center).astype(BF16), ones, preferred_element_type=F32)
            y = center * lax.rsqrt(spread + 1e-05) * gain_ref[...]
            main[i] = y[0:128].astype(BF16)
            rest[i, 0:48, :] = y[128:176].astype(BF16)
            g32[pl.ds(i, COLS, stride=ROWS_PAD), :] = y

    def factors(target, rows, n, weights, normed):
        projected = lax.dot_general(weights, normed.reshape(256, 128), NT, preferred_element_type=F32)
        one = sigmoid(projected[0:rows]) * projected[rows : 2 * rows]
        two = sigmoid(projected[2 * rows : 3 * rows]) * projected[3 * rows :]
        for u in range(2):
            lanes = slice(128 * u, 128 * (u + 1))
            target[pl.ds(2 * n + u, rows, stride=48), :] = one[:, lanes]
            target[pl.ds(24 + 2 * n + u, rows, stride=48), :] = two[:, lanes]

    def pack_pairs(v):
        for n in range(2):
            rows = pl.ds(pl.multiple_of((22 * v + 11 * n) * ROWS_PAD, 8), 11 * ROWS_PAD)
            g[v, pl.ds(11 * n, 11)] = g32[rows, :].reshape(11, ROWS_PAD, 128).astype(BF16)

    def send_pairs(n):
        v, device = relays[n]
        pltpu.make_async_remote_copy(
            src_ref=g.at[v],
            dst_ref=g_relay.at[x],
            send_sem=g_send.at[v],
            recv_sem=relay_recv.at[x],
            device_id=device,
            device_id_type=MESH,
        ).start()

        m = (n + 2) % 4
        v2, device2 = owners[m]

        def send_direct():
            pltpu.make_async_remote_copy(
                src_ref=g.at[v2],
                dst_ref=g_in.at[row % 8],
                send_sem=g_send.at[v2],
                recv_sem=g_recv.at[row % 8],
                device_id=device2,
                device_id_type=MESH,
            ).start()

        if m == 0:

            @pl.when(is_own)
            def _():
                pltpu.make_async_copy(g.at[v2], g_in.at[v2], g_recv.at[v2]).start()

            pl.when(jnp.logical_not(is_own))(send_direct)
        else:
            send_direct()

    def send_on(n):
        s = (x + 4 - n) % 4
        wait_bytes(g_relay.at[s], relay_recv.at[s])
        pltpu.make_async_remote_copy(
            src_ref=g_relay.at[s],
            dst_ref=g_in.at[4 * y_hi + s],
            send_sem=relay_send.at[s],
            recv_sem=g_recv.at[4 * y_hi + s],
            device_id=forward,
            device_id_type=MESH,
        ).start()

    for n in (0, 1):
        pack_pairs(relays[n][0])
        pack_pairs(owners[(n + 2) % 4][0])

    for n in range(11):
        factors(main32, CHANNELS, n, weight_all, main[2 * n : 2 * n + 2])

    pl.semaphore_wait(barrier, 127)

    swap_rest = pltpu.make_async_remote_copy(
        src_ref=rest.at[:, pl.ds(0, 48), :],
        dst_ref=rest.at[:, pl.ds(48, 48), :],
        send_sem=map_send,
        recv_sem=map_recv,
        device_id=sibling,
        device_id_type=MESH,
    )
    swap_rest.start()

    parts = ((lr_a, lr_a_in, 0, 32, lr_a_recv), (lr_b, lr_b_in, 32, 16, lr_b_recv))

    def send_factors(part, source, channel, slot, device, kind):
        buffer, landing, start, rows, recv = parts[part]
        index = channel if kind < 2 else CHANNELS + channel
        buffer[index] = source[pl.ds(pl.multiple_of(channel * 48 + start, 16), rows), :].astype(BF16)
        if device is None:
            pltpu.make_async_copy(buffer.at[index], landing.at[me, slot], recv.at[row // 2]).start()
        else:
            pltpu.make_async_remote_copy(
                src_ref=buffer.at[index],
                dst_ref=landing.at[me, slot],
                send_sem=lr_send.at[part],
                recv_sem=recv.at[row // 2],
                device_id=device,
                device_id_type=MESH,
            ).start()

    def send_main(part):
        for hop in HOPS:
            device, chip = chip_at(row, col, hop)
            send_factors(part, main32, HALF * half + chip, half, device, 0)
            across = {"row": device["row"], "col": device["col"] + 1 - 2 * half}
            send_factors(part, main32, HALF - HALF * half + chip, half, across, 1)
        send_factors(part, main32, HALF - HALF * half + me, half, sibling, 1)
        send_factors(part, main32, HALF * half + me, half, None, 0)

    def send_rest(part):
        for hop in HOPS:
            device, chip = chip_at(row, col, hop)
            send_factors(part, rest32, chip, 2, device, 2)
        send_factors(part, rest32, me, 2, None, 2)

    send_main(0)
    send_pairs(0)
    send_pairs(1)
    swap_rest.wait()
    for n in range(11):
        factors(rest32, HALF, n, weight, rest[2 * n : 2 * n + 2])
    send_rest(0)
    for n in (2, 3):
        pack_pairs(relays[n][0])
        pack_pairs(owners[(n + 2) % 4][0])
        send_pairs(n)
    send_main(1)
    send_rest(1)

    def landed(part, n):
        b = (row // 2 + n) % 16
        landing, recv = parts[part][1], parts[part][4]
        wait_bytes(landing.at[pl.ds(pl.multiple_of(4 * b, 4), 4)], recv.at[b])
        for low in range(2):
            for t in range(3):
                one = landing[4 * b + low, t].astype(F32)
                two = landing[4 * b + 2 + low, t].astype(F32)
                yield b, slice(LANES * low + 128 * t, LANES * low + 128 * (t + 1)), one, two

    def take_right(b, k, lanes, one, two):
        rows = pl.ds(pl.multiple_of(256 * k + 16 * b, 16), 16)
        right[rows, lanes] = jnp.concatenate([one, two], axis=0).astype(BF16)

    def take_first(n):
        for b, lanes, one, two in landed(0, n):
            rows = pl.ds(pl.multiple_of(48 * b, 48), 48)
            left[rows, lanes] = jnp.concatenate([one[:24], two[:24]], axis=0).astype(BF16)
            take_right(b, 0, lanes, one[24:], two[24:])

    def take_second(n):
        for b, lanes, one, two in landed(1, n):
            take_right(b, 1, lanes, one[:8], two[:8])
            take_right(b, 2, lanes, one[8:], two[8:])

    def send_products(k):
        acc = lax.dot_general(right[256 * k : 256 * (k + 1), :], left[...], NT, preferred_element_type=F32)
        for r in range(BLOCKS):
            for low in range(2):
                p[k, 2 * r + low] = acc[8 * r : 8 * r + 8, LANES * low : LANES * (low + 1)].astype(BF16)
        pltpu.make_async_copy(p.at[k, me], p_in.at[k, me], p_recv.at[k]).start()
        for hop in HOPS:
            device, chip = chip_at(row, col, hop)
            pltpu.make_async_remote_copy(
                src_ref=p.at[k, chip],
                dst_ref=p_in.at[k, me],
                send_sem=p_send.at[k],
                recv_sem=p_recv.at[k],
                device_id=device,
                device_id_type=MESH,
            ).start()

    pl.loop(0, 8)(take_first)
    send_on(0)
    send_on(1)
    pl.loop(8, 16)(take_first)
    send_products(0)
    send_on(2)
    send_on(3)
    pl.loop(0, 16)(take_second)
    send_products(1)
    send_products(2)

    for s in range(8):
        wait_bytes(g_in.at[s], g_recv.at[s])

    @pl.loop(0, 2)
    def _(n):
        for u in range(11):
            j = 11 * n + u
            pairs = jnp.concatenate([g_in[s, j].astype(F32) for s in range(8)], axis=0).astype(BF16)
            gates[j] = sigmoid(jnp.dot(pairs, gate_weight_ref[...], preferred_element_type=F32))

    gains[...] = jnp.broadcast_to(out_gain_ref[...], (128, 128)).T
    ws[...] = out_weight_ref[...].astype(F32)
    ours = pl.ds(pl.multiple_of(HALF * half, HALF), HALF)
    theirs = pl.ds(pl.multiple_of(HALF - HALF * half, HALF), HALF)
    gain = jnp.concatenate([gains[ours, :], gains[theirs, :]], axis=0)
    gain = jnp.concatenate([gain, gain], axis=1)
    out_weight = jnp.concatenate([ws[ours, :], ws[theirs, :]], axis=0).astype(BF16)

    for k, (start, stop) in enumerate(GROUPS):
        wait_bytes(p_in.at[k], p_recv.at[k])
        swap = pltpu.make_async_remote_copy(
            src_ref=p_in.at[k, :, :, pl.ds(pl.multiple_of(128 - 128 * half, 128), 256)],
            dst_ref=p_sib.at[k],
            send_sem=sib_send.at[k],
            recv_sem=sib_recv.at[k],
            device_id=sibling,
            device_id_type=MESH,
        )
        swap.start()
        for t in range(2):
            lanes = pl.ds(pl.multiple_of(128 * half + 128 * t, 128), 128)
            p32[t, 0:512, :] = p_in[k, :, :, lanes].astype(F32).reshape(512, 128)
        swap.wait()
        for t in range(2):
            p32[t, 512:1024, :] = p_sib[k, :, :, 128 * t : 128 * (t + 1)].astype(F32).reshape(512, 128)
        for j in range(start, stop):
            u = j - start
            q = jnp.concatenate([p32[t, pl.ds(u, CHANNELS, stride=8), :] for t in range(2)], axis=1)
            center = q - jnp.mean(q, axis=0, keepdims=True)
            spread = jnp.mean(center * center, axis=0, keepdims=True)
            hidden = (center * lax.rsqrt(spread + 1e-05) * gain).astype(BF16)
            mixed[u] = lax.dot_general(hidden, out_weight, TN, preferred_element_type=F32)
            update = gates[j] * mixed[u, pl.ds(pl.multiple_of(64 * half, 64), 192), :]
            for s in range(8):
                packed[u, 22 * s : 22 * s + 24, :] = update[24 * s : 24 * s + 24]
            out_ref[j] = packed[u, 0:COLS, :].astype(BF16)

    wait_bytes(lr_a.at[pl.ds(0, 190)], lr_send.at[0])
    wait_bytes(lr_b.at[pl.ds(0, 190)], lr_send.at[1])
    for k in range(3):
        wait_bytes(p.at[k, pl.ds(0, 63)], p_send.at[k])
    for v, _ in relays + owners[1:]:
        wait_bytes(g.at[v], g_send.at[v])
    for s in range(4):
        wait_bytes(g_relay.at[s], relay_send.at[s])

    @pl.when(jnp.logical_not(is_own))
    def _():
        wait_bytes(g.at[owners[0][0]], g_send.at[owners[0][0]])


def fused(*args):
    vmem = pl.BlockSpec(memory_space=pltpu.VMEM)
    return pl.pallas_call(
        kernel,
        out_shape=jax.ShapeDtypeStruct((ROWS, COLS, 128), BF16),
        in_specs=[pl.BlockSpec(memory_space=pl.ANY)] + [vmem] * 5,
        out_specs=vmem,
        scratch_shapes=[
            pltpu.VMEM((ROWS, COLS, 128), BF16),
            pltpu.VMEM((512, 128), F32),
            pltpu.VMEM((ROWS, 128, 128), BF16),
            pltpu.VMEM((ROWS, 128, 128), BF16),
            pltpu.VMEM((CHANNELS * 48, 128), F32),
            pltpu.VMEM((HALF * 48, 128), F32),
            pltpu.VMEM((COLS * ROWS_PAD, 128), F32),
            pltpu.VMEM((CHANNELS + HALF, 32, 128), BF16),
            pltpu.VMEM((CHANNELS + HALF, 16, 128), BF16),
            pltpu.VMEM((8, ROWS, ROWS_PAD, 128), BF16),
            pltpu.VMEM((4, ROWS, ROWS_PAD, 128), BF16),
            pltpu.VMEM((64, 3, 32, 128), BF16),
            pltpu.VMEM((64, 3, 16, 128), BF16),
            pltpu.VMEM((8, ROWS, ROWS_PAD, 128), BF16),
            pltpu.VMEM((768, 768), BF16),
            pltpu.VMEM((768, 768), BF16),
            pltpu.VMEM((3, 64, 8, LANES), BF16),
            pltpu.VMEM((3, 64, 8, LANES), BF16),
            pltpu.VMEM((3, 64, 8, 256), BF16),
            pltpu.VMEM((2, CHANNELS * 8, 128), F32),
            pltpu.VMEM((ROWS, 192, 128), F32),
            pltpu.VMEM((128, 128), F32),
            pltpu.VMEM((128, 128), F32),
            pltpu.VMEM((8, 256, 128), F32),
            pltpu.VMEM((8, 184, 128), F32),
            pltpu.SemaphoreType.DMA,
            pltpu.SemaphoreType.DMA,
            pltpu.SemaphoreType.DMA,
            pltpu.SemaphoreType.DMA((2,)),
            pltpu.SemaphoreType.DMA((16,)),
            pltpu.SemaphoreType.DMA((16,)),
            pltpu.SemaphoreType.DMA((8,)),
            pltpu.SemaphoreType.DMA((8,)),
            pltpu.SemaphoreType.DMA((4,)),
            pltpu.SemaphoreType.DMA((4,)),
            pltpu.SemaphoreType.DMA((3,)),
            pltpu.SemaphoreType.DMA((3,)),
            pltpu.SemaphoreType.DMA((3,)),
            pltpu.SemaphoreType.DMA((3,)),
        ],
        compiler_params=pltpu.CompilerParams(
            collective_id=0, has_side_effects=True, vmem_limit_bytes=VMEM_LIMIT
        ),
        name="triangle_update",
    )(*args)


def copy_kernel(src_ref, dst_ref, held, in_sems, out_sems):
    ins = [pltpu.make_async_copy(src_ref.at[i], held.at[i], in_sems.at[i]) for i in range(ROWS)]
    outs = [pltpu.make_async_copy(held.at[i], dst_ref.at[i], out_sems.at[i]) for i in range(ROWS)]
    for copy in ins:
        copy.start()
    for i in range(ROWS):
        ins[i].wait()
        outs[i].start()
    for copy in outs:
        copy.wait()


def copy_out(x):
    return pl.pallas_call(
        copy_kernel,
        out_shape=jax.ShapeDtypeStruct(x.shape, x.dtype),
        in_specs=[pl.BlockSpec(memory_space=pl.ANY)],
        out_specs=pl.BlockSpec(memory_space=pl.ANY),
        scratch_shapes=[
            pltpu.VMEM(x.shape, x.dtype),
            pltpu.SemaphoreType.DMA((ROWS,)),
            pltpu.SemaphoreType.DMA((ROWS,)),
        ],
        name="copy_out",
    )(x)


def body(pair_map, in_gain, project_weight, gate_weight, out_gain, out_weight):
    update = fused(
        pair_map, in_gain.reshape(1, 128), project_weight, gate_weight, out_gain.reshape(1, 128), out_weight
    )
    return copy_out(update)


def solution(mesh):
    return jax.shard_map(
        body,
        mesh=mesh,
        in_specs=(P("row", "col", None), P(), P(), P(), P(), P()),
        out_specs=P("row", "col", None),
        check_vma=False,
    )
```

```python
import functools

import jax
import jax.numpy as jnp
from jax import lax
from jax.experimental import pallas as pl
from jax.experimental.pallas import tpu as pltpu
from jax.sharding import PartitionSpec as P

MESH = pl.DeviceIdType.MESH
F32 = jnp.float32
BF16 = jnp.bfloat16
VMEM_LIMIT = 56 * 2**20

ROWS = 22
ROWS_PAD = 24
COLS = 176
CHANNELS = 128
HALF = 64
LANES = 384
BLOCKS = 32
NT = (((1,), (1,)), ((), ()))
TN = (((0,), (0,)), ((), ()))


def sigmoid(x):
    return 0.5 * jnp.tanh(0.5 * x) + 0.5


def place():
    row = lax.axis_index("row")
    col = lax.axis_index("col")
    return row, col


def chip_at(row, col, hop):
    z, y, x = row // 8, ((row // 4) % 2) * 2 + col // 2, row % 4
    z, y, x = (z + hop[0]) % 4, (y + hop[1]) % 4, (x + hop[2]) % 4
    row2 = z * 8 + (y // 2) * 4 + x
    low = y % 2
    return {"row": row2, "col": low * 2 + col % 2}, row2 * 2 + low


def hop_order():
    left = [(a, b, c) for a in range(4) for b in range(4) for c in range(4)][1:]
    use = [0] * 6
    order = []

    def after(hop):
        then = list(use)
        for axis, step in enumerate(hop):
            then[2 * axis] += (0, 2, 2, 0)[step]
            then[2 * axis + 1] += (0, 0, 2, 2)[step]
        return then

    def score(hop):
        then = after(hop)
        return max(then) - min(then), sum(v * v for v in then), (hop[0] * 37 + hop[1] * 11 + hop[2] * 5) % 17

    while left:
        best = min(left, key=score)
        use = after(best)
        left.remove(best)
        order.append(best)
    return order


HOPS = hop_order()
GROUPS = ((0, 8), (8, 16), (16, 22))


def wait_bytes(ref, sem):
    pltpu.make_async_copy(ref, ref, sem).wait()


def kernel(
    own_ref, gain_ref, weight_ref, gate_weight_ref, out_gain_ref, out_weight_ref, out_ref,
    own, wt, main, rest, main32, rest32, g32, lr_a, lr_b, g, g_relay, lr_a_in, lr_b_in, g_in, left, right, p, p_in, p_sib, p32, gates, gains, ws, mixed, packed,
    own_sem, map_send, map_recv, lr_send, lr_a_recv, lr_b_recv, g_send, g_recv, relay_send, relay_recv, p_send, p_recv, sib_send, sib_recv,
):
    row, col = place()
    half = col % 2
    me = row * 2 + col // 2
    sibling = {"row": row, "col": col + 1 - 2 * half}
    barrier = pltpu.get_barrier_semaphore()

    def signal(device):
        pl.semaphore_signal(barrier, inc=1, device_id=device, device_id_type=MESH)

    z, y_hi, x = row // 8, (row // 4) % 2, row % 4
    base = 8 * col + 4 * y_hi
    other = (z + 2) % 4
    owners, relays = [], []
    for n in range(4):
        x2 = (x + n) % 4
        owners.append((4 * y_hi + x2, {"row": base + x2, "col": z}))
        relays.append((4 - 4 * y_hi + x2, {"row": base + x2, "col": other}))
    forward = {"row": row + 4 - 8 * y_hi, "col": (col + 2) % 4}
    is_own = z == col

    signal(sibling)
    for hop in HOPS:
        device, _ = chip_at(row, col, hop)
        signal(device)
        signal({"row": device["row"], "col": device["col"] + 1 - 2 * half})

    own_copy = pltpu.make_async_copy(own_ref, own, own_sem)
    own_copy.start()

    wt[...] = weight_ref[...].astype(F32).T
    parts = [wt[pl.ds(pl.multiple_of(128 * n + HALF * half, HALF), HALF), :] for n in range(4)]
    weight = jnp.concatenate(parts, axis=0).astype(BF16)
    weight_all = wt[...].astype(BF16)
    ones = jnp.full((128, 128), 1.0 / 128, BF16)
    rest[:, 96:128, :] = jnp.zeros((ROWS, 32, 128), BF16)
    for pad in (22, 23, 46, 47):
        main32[pl.ds(pad, CHANNELS, stride=48), :] = jnp.zeros((CHANNELS, 128), F32)
        rest32[pl.ds(pad, HALF, stride=48), :] = jnp.zeros((HALF, 128), F32)
    for pad in (22, 23):
        g32[pl.ds(pad, COLS, stride=ROWS_PAD), :] = jnp.zeros((COLS, 128), F32)

    own_copy.wait()

    @pl.loop(0, 2)
    def _(n):
        for u in range(11):
            i = 11 * n + u
            v = own[i]
            center = v.astype(F32) - jnp.dot(v, ones, preferred_element_type=F32)
            spread = jnp.dot((center * center).astype(BF16), ones, preferred_element_type=F32)
            y = center * lax.rsqrt(spread + 1e-05) * gain_ref[...]
            main[i] = y[0:128].astype(BF16)
            rest[i, 0:48, :] = y[128:176].astype(BF16)
            g32[pl.ds(i, COLS, stride=ROWS_PAD), :] = y

    def factors(target, rows, n, weights, normed):
        projected = lax.dot_general(weights, normed.reshape(256, 128), NT, preferred_element_type=F32)
        one = sigmoid(projected[0:rows]) * projected[rows : 2 * rows]
        two = sigmoid(projected[2 * rows : 3 * rows]) * projected[3 * rows :]
        for u in range(2):
            lanes = slice(128 * u, 128 * (u + 1))
            target[pl.ds(2 * n + u, rows, stride=48), :] = one[:, lanes]
            target[pl.ds(24 + 2 * n + u, rows, stride=48), :] = two[:, lanes]

    def pack_pairs(v):
        for n in range(2):
            rows = pl.ds(pl.multiple_of((22 * v + 11 * n) * ROWS_PAD, 8), 11 * ROWS_PAD)
            g[v, pl.ds(11 * n, 11)] = g32[rows, :].reshape(11, ROWS_PAD, 128).astype(BF16)

    def send_pairs(step):
        n, rows = step // 2, pl.ds(11 * (step % 2), 11)
        v, device = relays[n]
        pltpu.make_async_remote_copy(
            src_ref=g.at[v, rows],
            dst_ref=g_relay.at[x, rows],
            send_sem=g_send.at[v],
            recv_sem=relay_recv.at[x, step % 2],
            device_id=device,
            device_id_type=MESH,
        ).start()

        m = (n + 2) % 4
        v2, device2 = owners[m]

        def send_direct():
            pltpu.make_async_remote_copy(
                src_ref=g.at[v2, rows],
                dst_ref=g_in.at[row % 8, rows],
                send_sem=g_send.at[v2],
                recv_sem=g_recv.at[row % 8],
                device_id=device2,
                device_id_type=MESH,
            ).start()

        if m == 0:

            @pl.when(is_own)
            def _():
                pltpu.make_async_copy(g.at[v2, rows], g_in.at[v2, rows], g_recv.at[v2]).start()

            pl.when(jnp.logical_not(is_own))(send_direct)
        else:
            send_direct()

    def send_on(step):
        s, rows = (x + 4 - step // 2) % 4, pl.ds(11 * (step % 2), 11)
        wait_bytes(g_relay.at[s, rows], relay_recv.at[s, step % 2])
        pltpu.make_async_remote_copy(
            src_ref=g_relay.at[s, rows],
            dst_ref=g_in.at[4 * y_hi + s, rows],
            send_sem=relay_send.at[s],
            recv_sem=g_recv.at[4 * y_hi + s],
            device_id=forward,
            device_id_type=MESH,
        ).start()

    for n in (0, 1):
        pack_pairs(relays[n][0])
        pack_pairs(owners[(n + 2) % 4][0])

    for n in range(11):
        factors(main32, CHANNELS, n, weight_all, main[2 * n : 2 * n + 2])

    pl.semaphore_wait(barrier, 127)

    swap_rest = pltpu.make_async_remote_copy(
        src_ref=rest.at[:, pl.ds(0, 48), :],
        dst_ref=rest.at[:, pl.ds(48, 48), :],
        send_sem=map_send,
        recv_sem=map_recv,
        device_id=sibling,
        device_id_type=MESH,
    )
    swap_rest.start()

    parts = ((lr_a, lr_a_in, 0, 32, lr_a_recv), (lr_b, lr_b_in, 32, 16, lr_b_recv))

    def send_factors(part, source, channel, slot, device, kind):
        buffer, landing, start, rows, recv = parts[part]
        index = channel if kind < 2 else CHANNELS + channel
        buffer[index] = source[pl.ds(pl.multiple_of(channel * 48 + start, 16), rows), :].astype(BF16)
        if device is None:
            pltpu.make_async_copy(buffer.at[index], landing.at[me, slot], recv.at[row // 2]).start()
        else:
            pltpu.make_async_remote_copy(
                src_ref=buffer.at[index],
                dst_ref=landing.at[me, slot],
                send_sem=lr_send.at[part],
                recv_sem=recv.at[row // 2],
                device_id=device,
                device_id_type=MESH,
            ).start()

    def send_main(part, start, stop):
        for hop in HOPS[start:stop]:
            device, chip = chip_at(row, col, hop)
            send_factors(part, main32, HALF * half + chip, half, device, 0)
            across = {"row": device["row"], "col": device["col"] + 1 - 2 * half}
            send_factors(part, main32, HALF - HALF * half + chip, half, across, 1)
        if start == 0:
            send_factors(part, main32, HALF - HALF * half + me, half, sibling, 1)
            send_factors(part, main32, HALF * half + me, half, None, 0)

    def send_rest(part, start, stop):
        for hop in HOPS[start:stop]:
            device, chip = chip_at(row, col, hop)
            send_factors(part, rest32, chip, 2, device, 2)
        if start == 0:
            send_factors(part, rest32, me, 2, None, 2)

    for step in range(8):
        send_pairs(step)
        if step < 4:
            send_main(0, 16 * step, 16 * step + 16)
        elif step < 6:
            send_rest(0, 32 * (step - 4), 32 * (step - 3))
        elif step == 6:
            send_main(1, 0, 63)
        else:
            send_rest(1, 0, 63)
        if step == 0:
            for n in (2, 3):
                pack_pairs(relays[n][0])
                pack_pairs(owners[(n + 2) % 4][0])
        if step == 1:
            swap_rest.wait()
            for n in range(11):
                factors(rest32, HALF, n, weight, rest[2 * n : 2 * n + 2])
        if step >= 2:
            send_on(step - 2)

    def landed(part, n):
        b = (row // 2 + n) % 16
        landing, recv = parts[part][1], parts[part][4]
        wait_bytes(landing.at[pl.ds(pl.multiple_of(4 * b, 4), 4)], recv.at[b])
        for low in range(2):
            for t in range(3):
                one = landing[4 * b + low, t].astype(F32)
                two = landing[4 * b + 2 + low, t].astype(F32)
                yield b, slice(LANES * low + 128 * t, LANES * low + 128 * (t + 1)), one, two

    def take_right(b, k, lanes, one, two):
        rows = pl.ds(pl.multiple_of(256 * k + 16 * b, 16), 16)
        right[rows, lanes] = jnp.concatenate([one, two], axis=0).astype(BF16)

    def take_first(n):
        for b, lanes, one, two in landed(0, n):
            rows = pl.ds(pl.multiple_of(48 * b, 48), 48)
            left[rows, lanes] = jnp.concatenate([one[:24], two[:24]], axis=0).astype(BF16)
            take_right(b, 0, lanes, one[24:], two[24:])

    def take_second(n):
        for b, lanes, one, two in landed(1, n):
            take_right(b, 1, lanes, one[:8], two[:8])
            take_right(b, 2, lanes, one[8:], two[8:])

    def send_products(k):
        acc = lax.dot_general(right[256 * k : 256 * (k + 1), :], left[...], NT, preferred_element_type=F32)
        for r in range(BLOCKS):
            for low in range(2):
                p[k, 2 * r + low] = acc[8 * r : 8 * r + 8, LANES * low : LANES * (low + 1)].astype(BF16)
        pltpu.make_async_copy(p.at[k, me], p_in.at[k, me], p_recv.at[k]).start()
        for hop in HOPS:
            device, chip = chip_at(row, col, hop)
            pltpu.make_async_remote_copy(
                src_ref=p.at[k, chip],
                dst_ref=p_in.at[k, me],
                send_sem=p_send.at[k],
                recv_sem=p_recv.at[k],
                device_id=device,
                device_id_type=MESH,
            ).start()

    pl.loop(0, 8)(take_first)
    send_on(6)
    pl.loop(8, 16)(take_first)
    send_on(7)
    send_products(0)
    pl.loop(0, 16)(take_second)
    send_products(1)
    send_products(2)

    for s in range(8):
        wait_bytes(g_in.at[s], g_recv.at[s])

    @pl.loop(0, 2)
    def _(n):
        for u in range(11):
            j = 11 * n + u
            pairs = jnp.concatenate([g_in[s, j].astype(F32) for s in range(8)], axis=0).astype(BF16)
            gates[j] = sigmoid(jnp.dot(pairs, gate_weight_ref[...], preferred_element_type=F32))

    gains[...] = jnp.broadcast_to(out_gain_ref[...], (128, 128)).T
    ws[...] = out_weight_ref[...].astype(F32)
    ours = pl.ds(pl.multiple_of(HALF * half, HALF), HALF)
    theirs = pl.ds(pl.multiple_of(HALF - HALF * half, HALF), HALF)
    gain = jnp.concatenate([gains[ours, :], gains[theirs, :]], axis=0)
    gain = jnp.concatenate([gain, gain], axis=1)
    out_weight = jnp.concatenate([ws[ours, :], ws[theirs, :]], axis=0).astype(BF16)

    for k, (start, stop) in enumerate(GROUPS):
        wait_bytes(p_in.at[k], p_recv.at[k])
        swap = pltpu.make_async_remote_copy(
            src_ref=p_in.at[k, :, :, pl.ds(pl.multiple_of(128 - 128 * half, 128), 256)],
            dst_ref=p_sib.at[k],
            send_sem=sib_send.at[k],
            recv_sem=sib_recv.at[k],
            device_id=sibling,
            device_id_type=MESH,
        )
        swap.start()
        for t in range(2):
            lanes = pl.ds(pl.multiple_of(128 * half + 128 * t, 128), 128)
            p32[t, 0:512, :] = p_in[k, :, :, lanes].astype(F32).reshape(512, 128)
        swap.wait()
        for t in range(2):
            p32[t, 512:1024, :] = p_sib[k, :, :, 128 * t : 128 * (t + 1)].astype(F32).reshape(512, 128)
        for j in range(start, stop):
            u = j - start
            q = jnp.concatenate([p32[t, pl.ds(u, CHANNELS, stride=8), :] for t in range(2)], axis=1)
            center = q - jnp.mean(q, axis=0, keepdims=True)
            spread = jnp.mean(center * center, axis=0, keepdims=True)
            hidden = (center * lax.rsqrt(spread + 1e-05) * gain).astype(BF16)
            mixed[u] = lax.dot_general(hidden, out_weight, TN, preferred_element_type=F32)
            update = gates[j] * mixed[u, pl.ds(pl.multiple_of(64 * half, 64), 192), :]
            for s in range(8):
                packed[u, 22 * s : 22 * s + 24, :] = update[24 * s : 24 * s + 24]
            out_ref[j] = packed[u, 0:COLS, :].astype(BF16)

    wait_bytes(lr_a.at[pl.ds(0, 190)], lr_send.at[0])
    wait_bytes(lr_b.at[pl.ds(0, 190)], lr_send.at[1])
    for k in range(3):
        wait_bytes(p.at[k, pl.ds(0, 63)], p_send.at[k])
    for v, _ in relays + owners[1:]:
        wait_bytes(g.at[v], g_send.at[v])
    for s in range(4):
        wait_bytes(g_relay.at[s], relay_send.at[s])

    @pl.when(jnp.logical_not(is_own))
    def _():
        wait_bytes(g.at[owners[0][0]], g_send.at[owners[0][0]])


def fused(*args):
    vmem = pl.BlockSpec(memory_space=pltpu.VMEM)
    return pl.pallas_call(
        kernel,
        out_shape=jax.ShapeDtypeStruct((ROWS, COLS, 128), BF16),
        in_specs=[pl.BlockSpec(memory_space=pl.ANY)] + [vmem] * 5,
        out_specs=vmem,
        scratch_shapes=[
            pltpu.VMEM((ROWS, COLS, 128), BF16),
            pltpu.VMEM((512, 128), F32),
            pltpu.VMEM((ROWS, 128, 128), BF16),
            pltpu.VMEM((ROWS, 128, 128), BF16),
            pltpu.VMEM((CHANNELS * 48, 128), F32),
            pltpu.VMEM((HALF * 48, 128), F32),
            pltpu.VMEM((COLS * ROWS_PAD, 128), F32),
            pltpu.VMEM((CHANNELS + HALF, 32, 128), BF16),
            pltpu.VMEM((CHANNELS + HALF, 16, 128), BF16),
            pltpu.VMEM((8, ROWS, ROWS_PAD, 128), BF16),
            pltpu.VMEM((4, ROWS, ROWS_PAD, 128), BF16),
            pltpu.VMEM((64, 3, 32, 128), BF16),
            pltpu.VMEM((64, 3, 16, 128), BF16),
            pltpu.VMEM((8, ROWS, ROWS_PAD, 128), BF16),
            pltpu.VMEM((768, 768), BF16),
            pltpu.VMEM((768, 768), BF16),
            pltpu.VMEM((3, 64, 8, LANES), BF16),
            pltpu.VMEM((3, 64, 8, LANES), BF16),
            pltpu.VMEM((3, 64, 8, 256), BF16),
            pltpu.VMEM((2, CHANNELS * 8, 128), F32),
            pltpu.VMEM((ROWS, 192, 128), F32),
            pltpu.VMEM((128, 128), F32),
            pltpu.VMEM((128, 128), F32),
            pltpu.VMEM((8, 256, 128), F32),
            pltpu.VMEM((8, 184, 128), F32),
            pltpu.SemaphoreType.DMA,
            pltpu.SemaphoreType.DMA,
            pltpu.SemaphoreType.DMA,
            pltpu.SemaphoreType.DMA((2,)),
            pltpu.SemaphoreType.DMA((16,)),
            pltpu.SemaphoreType.DMA((16,)),
            pltpu.SemaphoreType.DMA((8,)),
            pltpu.SemaphoreType.DMA((8,)),
            pltpu.SemaphoreType.DMA((4,)),
            pltpu.SemaphoreType.DMA((4, 2)),
            pltpu.SemaphoreType.DMA((3,)),
            pltpu.SemaphoreType.DMA((3,)),
            pltpu.SemaphoreType.DMA((3,)),
            pltpu.SemaphoreType.DMA((3,)),
        ],
        compiler_params=pltpu.CompilerParams(
            collective_id=0, has_side_effects=True, vmem_limit_bytes=VMEM_LIMIT
        ),
        name="triangle_update",
    )(*args)


def copy_kernel(src_ref, dst_ref, held, in_sems, out_sems):
    ins = [pltpu.make_async_copy(src_ref.at[i], held.at[i], in_sems.at[i]) for i in range(ROWS)]
    outs = [pltpu.make_async_copy(held.at[i], dst_ref.at[i], out_sems.at[i]) for i in range(ROWS)]
    for copy in ins:
        copy.start()
    for i in range(ROWS):
        ins[i].wait()
        outs[i].start()
    for copy in outs:
        copy.wait()


def copy_out(x):
    return pl.pallas_call(
        copy_kernel,
        out_shape=jax.ShapeDtypeStruct(x.shape, x.dtype),
        in_specs=[pl.BlockSpec(memory_space=pl.ANY)],
        out_specs=pl.BlockSpec(memory_space=pl.ANY),
        scratch_shapes=[
            pltpu.VMEM(x.shape, x.dtype),
            pltpu.SemaphoreType.DMA((ROWS,)),
            pltpu.SemaphoreType.DMA((ROWS,)),
        ],
        name="copy_out",
    )(x)


def body(pair_map, in_gain, project_weight, gate_weight, out_gain, out_weight):
    update = fused(
        pair_map, in_gain.reshape(1, 128), project_weight, gate_weight, out_gain.reshape(1, 128), out_weight
    )
    return copy_out(update)


def solution(mesh):
    return jax.shard_map(
        body,
        mesh=mesh,
        in_specs=(P("row", "col", None), P(), P(), P(), P(), P()),
        out_specs=P("row", "col", None),
        check_vma=False,
    )
```

```python
import functools

import jax
import jax.numpy as jnp
from jax import lax
from jax.experimental import pallas as pl
from jax.experimental.pallas import tpu as pltpu
from jax.sharding import PartitionSpec as P

MESH = pl.DeviceIdType.MESH
F32 = jnp.float32
BF16 = jnp.bfloat16
VMEM_LIMIT = 56 * 2**20

ROWS = 22
ROWS_PAD = 24
COLS = 176
CHANNELS = 128
HALF = 64
LANES = 384
BLOCKS = 32
NT = (((1,), (1,)), ((), ()))
TN = (((0,), (0,)), ((), ()))


def sigmoid(x):
    return 0.5 * jnp.tanh(0.5 * x) + 0.5


def place():
    row = lax.axis_index("row")
    col = lax.axis_index("col")
    return row, col


def chip_at(row, col, hop):
    z, y, x = row // 8, ((row // 4) % 2) * 2 + col // 2, row % 4
    z, y, x = (z + hop[0]) % 4, (y + hop[1]) % 4, (x + hop[2]) % 4
    row2 = z * 8 + (y // 2) * 4 + x
    low = y % 2
    return {"row": row2, "col": low * 2 + col % 2}, row2 * 2 + low


def hop_order():
    left = [(a, b, c) for a in range(4) for b in range(4) for c in range(4)][1:]
    use = [0] * 6
    order = []

    def after(hop):
        then = list(use)
        for axis, step in enumerate(hop):
            then[2 * axis] += (0, 2, 2, 0)[step]
            then[2 * axis + 1] += (0, 0, 2, 2)[step]
        return then

    def score(hop):
        then = after(hop)
        return max(then) - min(then), sum(v * v for v in then), (hop[0] * 37 + hop[1] * 11 + hop[2] * 5) % 17

    while left:
        best = min(left, key=score)
        use = after(best)
        left.remove(best)
        order.append(best)
    return order


HOPS = hop_order()
GROUPS = ((0, 8), (8, 16), (16, 22))


def wait_bytes(ref, sem):
    pltpu.make_async_copy(ref, ref, sem).wait()


def kernel(
    own_ref, gain_hbm, weight_hbm, gate_weight_hbm, out_gain_hbm, out_weight_hbm, out_ref,
    gain_ref, weight_ref, gate_weight_ref, out_gain_ref, out_weight_ref,
    own, wt, main, rest, main32, rest32, g32, lr_a, lr_b, g, g_relay, lr_a_in, lr_b_in, g_in, left, right, p, p_in, p_sib, p32, gates, gains, ws, mixed, packed,
    load_sems, map_send, map_recv, lr_send, lr_a_recv, lr_b_recv, g_send, g_recv, relay_send, relay_recv, p_send, p_recv, sib_send, sib_recv,
):
    row, col = place()
    half = col % 2
    me = row * 2 + col // 2
    sibling = {"row": row, "col": col + 1 - 2 * half}
    barrier = pltpu.get_barrier_semaphore()

    def signal(device):
        pl.semaphore_signal(barrier, inc=1, device_id=device, device_id_type=MESH)

    z, y_hi, x = row // 8, (row // 4) % 2, row % 4
    base = 8 * col + 4 * y_hi
    other = (z + 2) % 4
    owners, relays = [], []
    for n in range(4):
        x2 = (x + n) % 4
        owners.append((4 * y_hi + x2, {"row": base + x2, "col": z}))
        relays.append((4 - 4 * y_hi + x2, {"row": base + x2, "col": other}))
    forward = {"row": row + 4 - 8 * y_hi, "col": (col + 2) % 4}
    is_own = z == col

    for hop in sorted(HOPS, key=lambda hop: -sum(min(v, 4 - v) for v in hop)):
        device, _ = chip_at(row, col, hop)
        signal(device)
        signal({"row": device["row"], "col": device["col"] + 1 - 2 * half})
    signal(sibling)

    loads = [
        pltpu.make_async_copy(src, dst, load_sems.at[n])
        for n, (src, dst) in enumerate(
            (
                (own_ref, own),
                (gain_hbm, gain_ref),
                (weight_hbm, weight_ref),
                (gate_weight_hbm, gate_weight_ref),
                (out_gain_hbm, out_gain_ref),
                (out_weight_hbm, out_weight_ref),
            )
        )
    ]
    for load in loads:
        load.start()

    for load in loads[1:]:
        load.wait()
    wt[...] = weight_ref[...].astype(F32).T
    parts = [wt[pl.ds(pl.multiple_of(128 * n + HALF * half, HALF), HALF), :] for n in range(4)]
    weight = jnp.concatenate(parts, axis=0).astype(BF16)
    weight_all = wt[...].astype(BF16)
    ones = jnp.full((128, 128), 1.0 / 128, BF16)
    rest[:, 96:128, :] = jnp.zeros((ROWS, 32, 128), BF16)
    for pad in (22, 23, 46, 47):
        main32[pl.ds(pad, CHANNELS, stride=48), :] = jnp.zeros((CHANNELS, 128), F32)
        rest32[pl.ds(pad, HALF, stride=48), :] = jnp.zeros((HALF, 128), F32)
    for pad in (22, 23):
        g32[pl.ds(pad, COLS, stride=ROWS_PAD), :] = jnp.zeros((COLS, 128), F32)

    loads[0].wait()

    @pl.loop(0, 2)
    def _(n):
        for u in range(11):
            i = 11 * n + u
            v = own[i]
            center = v.astype(F32) - jnp.dot(v, ones, preferred_element_type=F32)
            spread = jnp.dot((center * center).astype(BF16), ones, preferred_element_type=F32)
            y = center * lax.rsqrt(spread + 1e-05) * gain_ref[...]
            main[i] = y[0:128].astype(BF16)
            rest[i, 0:48, :] = y[128:176].astype(BF16)
            g32[pl.ds(i, COLS, stride=ROWS_PAD), :] = y

    def factors(target, rows, n, weights, normed):
        projected = lax.dot_general(weights, normed.reshape(256, 128), NT, preferred_element_type=F32)
        one = sigmoid(projected[0:rows]) * projected[rows : 2 * rows]
        two = sigmoid(projected[2 * rows : 3 * rows]) * projected[3 * rows :]
        for u in range(2):
            lanes = slice(128 * u, 128 * (u + 1))
            target[pl.ds(2 * n + u, rows, stride=48), :] = one[:, lanes]
            target[pl.ds(24 + 2 * n + u, rows, stride=48), :] = two[:, lanes]

    def pack_pairs(v):
        for n in range(2):
            rows = pl.ds(pl.multiple_of((22 * v + 11 * n) * ROWS_PAD, 8), 11 * ROWS_PAD)
            g[v, pl.ds(11 * n, 11)] = g32[rows, :].reshape(11, ROWS_PAD, 128).astype(BF16)

    def send_pairs(step):
        n, rows = step // 2, pl.ds(11 * (step % 2), 11)
        v, device = relays[n]
        pltpu.make_async_remote_copy(
            src_ref=g.at[v, rows],
            dst_ref=g_relay.at[x, rows],
            send_sem=g_send.at[v],
            recv_sem=relay_recv.at[x, step % 2],
            device_id=device,
            device_id_type=MESH,
        ).start()

        m = (n + 2) % 4
        v2, device2 = owners[m]

        def send_direct():
            pltpu.make_async_remote_copy(
                src_ref=g.at[v2, rows],
                dst_ref=g_in.at[row % 8, rows],
                send_sem=g_send.at[v2],
                recv_sem=g_recv.at[row % 8],
                device_id=device2,
                device_id_type=MESH,
            ).start()

        if m == 0:

            @pl.when(is_own)
            def _():
                pltpu.make_async_copy(g.at[v2, rows], g_in.at[v2, rows], g_recv.at[v2]).start()

            pl.when(jnp.logical_not(is_own))(send_direct)
        else:
            send_direct()

    def send_on(step):
        s, rows = (x + 4 - step // 2) % 4, pl.ds(11 * (step % 2), 11)
        wait_bytes(g_relay.at[s, rows], relay_recv.at[s, step % 2])
        pltpu.make_async_remote_copy(
            src_ref=g_relay.at[s, rows],
            dst_ref=g_in.at[4 * y_hi + s, rows],
            send_sem=relay_send.at[s],
            recv_sem=g_recv.at[4 * y_hi + s],
            device_id=forward,
            device_id_type=MESH,
        ).start()

    for n in (0, 1):
        pack_pairs(relays[n][0])
        pack_pairs(owners[(n + 2) % 4][0])

    pl.semaphore_wait(barrier, 127)

    swap_rest = pltpu.make_async_remote_copy(
        src_ref=rest.at[:, pl.ds(0, 48), :],
        dst_ref=rest.at[:, pl.ds(48, 48), :],
        send_sem=map_send,
        recv_sem=map_recv,
        device_id=sibling,
        device_id_type=MESH,
    )
    swap_rest.start()
    send_pairs(0)
    send_pairs(1)
    for n in (2, 3):
        pack_pairs(relays[n][0])
        pack_pairs(owners[(n + 2) % 4][0])

    for n in range(11):
        factors(main32, CHANNELS, n, weight_all, main[2 * n : 2 * n + 2])


    parts = ((lr_a, lr_a_in, 0, 40, lr_a_recv), (lr_b, lr_b_in, 40, 8, lr_b_recv))

    def send_factors(part, source, channel, slot, device, kind):
        buffer, landing, start, rows, recv = parts[part]
        index = channel if kind < 2 else CHANNELS + channel
        buffer[index] = source[pl.ds(pl.multiple_of(channel * 48 + start, 8), rows), :].astype(BF16)
        if device is None:
            pltpu.make_async_copy(buffer.at[index], landing.at[me, slot], recv.at[row // 2]).start()
        else:
            pltpu.make_async_remote_copy(
                src_ref=buffer.at[index],
                dst_ref=landing.at[me, slot],
                send_sem=lr_send.at[part],
                recv_sem=recv.at[row // 2],
                device_id=device,
                device_id_type=MESH,
            ).start()

    def send_main(part, start, stop):
        for hop in HOPS[start:stop]:
            device, chip = chip_at(row, col, hop)
            send_factors(part, main32, HALF * half + chip, half, device, 0)
            across = {"row": device["row"], "col": device["col"] + 1 - 2 * half}
            send_factors(part, main32, HALF - HALF * half + chip, half, across, 1)
        if start == 0:
            send_factors(part, main32, HALF - HALF * half + me, half, sibling, 1)
            send_factors(part, main32, HALF * half + me, half, None, 0)

    def send_rest(part, start, stop):
        for hop in HOPS[start:stop]:
            device, chip = chip_at(row, col, hop)
            send_factors(part, rest32, chip, 2, device, 2)
        if start == 0:
            send_factors(part, rest32, me, 2, None, 2)

    for step in range(8):
        if step >= 2:
            send_pairs(step)
        if step < 4:
            send_main(0, 16 * step, 16 * step + 16)
        elif step < 6:
            send_rest(0, 32 * (step - 4), 32 * (step - 3))
        elif step == 6:
            send_main(1, 0, 63)
        else:
            send_rest(1, 0, 63)
        if step == 1:
            swap_rest.wait()
            for n in range(11):
                factors(rest32, HALF, n, weight, rest[2 * n : 2 * n + 2])
        if step >= 2:
            send_on(step - 2)

    def landed(part, n):
        b = (row // 2 + n) % 16
        landing, recv = parts[part][1], parts[part][4]
        wait_bytes(landing.at[pl.ds(pl.multiple_of(4 * b, 4), 4)], recv.at[b])
        for low in range(2):
            for t in range(3):
                one = landing[4 * b + low, t].astype(F32)
                two = landing[4 * b + 2 + low, t].astype(F32)
                yield b, slice(LANES * low + 128 * t, LANES * low + 128 * (t + 1)), one, two

    def take_right(b, k, lanes, one, two):
        rows = pl.ds(pl.multiple_of(256 * k + 16 * b, 16), 16)
        right[rows, lanes] = jnp.concatenate([one, two], axis=0).astype(BF16)

    def take_first(n):
        for b, lanes, one, two in landed(0, n):
            rows = pl.ds(pl.multiple_of(48 * b, 48), 48)
            left[rows, lanes] = jnp.concatenate([one[:24], two[:24]], axis=0).astype(BF16)
            take_right(b, 0, lanes, one[24:32], two[24:32])
            take_right(b, 1, lanes, one[32:], two[32:])

    def take_second(n):
        for b, lanes, one, two in landed(1, n):
            take_right(b, 2, lanes, one, two)

    def send_products(k):
        acc = lax.dot_general(right[256 * k : 256 * (k + 1), :], left[...], NT, preferred_element_type=F32)
        for r in range(BLOCKS):
            for low in range(2):
                p[k, 2 * r + low] = acc[8 * r : 8 * r + 8, LANES * low : LANES * (low + 1)].astype(BF16)
        pltpu.make_async_copy(p.at[k, me], p_in.at[k, me], p_recv.at[k]).start()
        for hop in HOPS:
            device, chip = chip_at(row, col, hop)
            pltpu.make_async_remote_copy(
                src_ref=p.at[k, chip],
                dst_ref=p_in.at[k, me],
                send_sem=p_send.at[k],
                recv_sem=p_recv.at[k],
                device_id=device,
                device_id_type=MESH,
            ).start()

    pl.loop(0, 8)(take_first)
    send_on(6)
    pl.loop(8, 16)(take_first)
    send_on(7)
    send_products(0)
    send_products(1)
    pl.loop(0, 16)(take_second)
    send_products(2)

    for s in range(8):
        wait_bytes(g_in.at[s], g_recv.at[s])

    @pl.loop(0, 2)
    def _(n):
        for u in range(11):
            j = 11 * n + u
            pairs = jnp.concatenate([g_in[s, j].astype(F32) for s in range(8)], axis=0).astype(BF16)
            gates[j] = sigmoid(jnp.dot(pairs, gate_weight_ref[...], preferred_element_type=F32))

    gains[...] = jnp.broadcast_to(out_gain_ref[...], (128, 128)).T
    ws[...] = out_weight_ref[...].astype(F32)
    ours = pl.ds(pl.multiple_of(HALF * half, HALF), HALF)
    theirs = pl.ds(pl.multiple_of(HALF - HALF * half, HALF), HALF)
    gain = jnp.concatenate([gains[ours, :], gains[theirs, :]], axis=0)
    gain = jnp.concatenate([gain, gain], axis=1)
    out_weight = jnp.concatenate([ws[ours, :], ws[theirs, :]], axis=0).astype(BF16)

    for k, (start, stop) in enumerate(GROUPS):
        wait_bytes(p_in.at[k], p_recv.at[k])
        swap = pltpu.make_async_remote_copy(
            src_ref=p_in.at[k, :, :, pl.ds(pl.multiple_of(128 - 128 * half, 128), 256)],
            dst_ref=p_sib.at[k],
            send_sem=sib_send.at[k],
            recv_sem=sib_recv.at[k],
            device_id=sibling,
            device_id_type=MESH,
        )
        swap.start()
        for t in range(2):
            lanes = pl.ds(pl.multiple_of(128 * half + 128 * t, 128), 128)
            p32[t, 0:512, :] = p_in[k, :, :, lanes].astype(F32).reshape(512, 128)
        swap.wait()
        for t in range(2):
            p32[t, 512:1024, :] = p_sib[k, :, :, 128 * t : 128 * (t + 1)].astype(F32).reshape(512, 128)
        for j in range(start, stop):
            u = j - start
            q = jnp.concatenate([p32[t, pl.ds(u, CHANNELS, stride=8), :] for t in range(2)], axis=1)
            center = q - jnp.mean(q, axis=0, keepdims=True)
            spread = jnp.mean(center * center, axis=0, keepdims=True)
            hidden = (center * lax.rsqrt(spread + 1e-05) * gain).astype(BF16)
            mixed[u] = lax.dot_general(hidden, out_weight, TN, preferred_element_type=F32)
            update = gates[j] * mixed[u, pl.ds(pl.multiple_of(64 * half, 64), 192), :]
            for s in range(8):
                packed[u, 22 * s : 22 * s + 24, :] = update[24 * s : 24 * s + 24]
            out_ref[j] = packed[u, 0:COLS, :].astype(BF16)

    wait_bytes(lr_a.at[pl.ds(0, 190)], lr_send.at[0])
    wait_bytes(lr_b.at[pl.ds(0, 190)], lr_send.at[1])
    for k in range(3):
        wait_bytes(p.at[k, pl.ds(0, 63)], p_send.at[k])
    for v, _ in relays + owners[1:]:
        wait_bytes(g.at[v], g_send.at[v])
    for s in range(4):
        wait_bytes(g_relay.at[s], relay_send.at[s])

    @pl.when(jnp.logical_not(is_own))
    def _():
        wait_bytes(g.at[owners[0][0]], g_send.at[owners[0][0]])


def fused(*args):
    vmem = pl.BlockSpec(memory_space=pltpu.VMEM)
    return pl.pallas_call(
        kernel,
        out_shape=pltpu.VMEM((ROWS, COLS, 128), BF16),
        in_specs=[pl.BlockSpec(memory_space=pl.ANY)] * 6,
        out_specs=vmem,
        scratch_shapes=[
            pltpu.VMEM((1, 128), F32),
            pltpu.VMEM((128, 512), BF16),
            pltpu.VMEM((128, 128), BF16),
            pltpu.VMEM((1, 128), F32),
            pltpu.VMEM((128, 128), BF16),
            pltpu.VMEM((ROWS, COLS, 128), BF16),
            pltpu.VMEM((512, 128), F32),
            pltpu.VMEM((ROWS, 128, 128), BF16),
            pltpu.VMEM((ROWS, 128, 128), BF16),
            pltpu.VMEM((CHANNELS * 48, 128), F32),
            pltpu.VMEM((HALF * 48, 128), F32),
            pltpu.VMEM((COLS * ROWS_PAD, 128), F32),
            pltpu.VMEM((CHANNELS + HALF, 40, 128), BF16),
            pltpu.VMEM((CHANNELS + HALF, 8, 128), BF16),
            pltpu.VMEM((8, ROWS, ROWS_PAD, 128), BF16),
            pltpu.VMEM((4, ROWS, ROWS_PAD, 128), BF16),
            pltpu.VMEM((64, 3, 40, 128), BF16),
            pltpu.VMEM((64, 3, 8, 128), BF16),
            pltpu.VMEM((8, ROWS, ROWS_PAD, 128), BF16),
            pltpu.VMEM((768, 768), BF16),
            pltpu.VMEM((768, 768), BF16),
            pltpu.VMEM((3, 64, 8, LANES), BF16),
            pltpu.VMEM((3, 64, 8, LANES), BF16),
            pltpu.VMEM((3, 64, 8, 256), BF16),
            pltpu.VMEM((2, CHANNELS * 8, 128), F32),
            pltpu.VMEM((ROWS, 192, 128), F32),
            pltpu.VMEM((128, 128), F32),
            pltpu.VMEM((128, 128), F32),
            pltpu.VMEM((8, 256, 128), F32),
            pltpu.VMEM((8, 184, 128), F32),
            pltpu.SemaphoreType.DMA((6,)),
            pltpu.SemaphoreType.DMA,
            pltpu.SemaphoreType.DMA,
            pltpu.SemaphoreType.DMA((2,)),
            pltpu.SemaphoreType.DMA((16,)),
            pltpu.SemaphoreType.DMA((16,)),
            pltpu.SemaphoreType.DMA((8,)),
            pltpu.SemaphoreType.DMA((8,)),
            pltpu.SemaphoreType.DMA((4,)),
            pltpu.SemaphoreType.DMA((4, 2)),
            pltpu.SemaphoreType.DMA((3,)),
            pltpu.SemaphoreType.DMA((3,)),
            pltpu.SemaphoreType.DMA((3,)),
            pltpu.SemaphoreType.DMA((3,)),
        ],
        compiler_params=pltpu.CompilerParams(
            collective_id=0, has_side_effects=True, vmem_limit_bytes=VMEM_LIMIT
        ),
        name="triangle_update",
    )(*args)


def copy_kernel(src_ref, dst_ref, sems):
    copies = [pltpu.make_async_copy(src_ref.at[i], dst_ref.at[i], sems.at[i]) for i in range(ROWS)]
    for copy in copies:
        copy.start()
    for copy in copies:
        copy.wait()


def copy_out(x):
    return pl.pallas_call(
        copy_kernel,
        out_shape=jax.ShapeDtypeStruct(x.shape, x.dtype),
        in_specs=[pl.BlockSpec(memory_space=pltpu.VMEM)],
        out_specs=pl.BlockSpec(memory_space=pl.ANY),
        scratch_shapes=[pltpu.SemaphoreType.DMA((ROWS,))],
        name="copy_out",
    )(x)


def body(pair_map, in_gain, project_weight, gate_weight, out_gain, out_weight):
    update = fused(
        pair_map, in_gain.reshape(1, 128), project_weight, gate_weight, out_gain.reshape(1, 128), out_weight
    )
    return copy_out(update)


def solution(mesh):
    return jax.shard_map(
        body,
        mesh=mesh,
        in_specs=(P("row", "col", None), P(), P(), P(), P(), P()),
        out_specs=P("row", "col", None),
        check_vma=False,
    )
```

```python
import functools

import jax
import jax.numpy as jnp
from jax import lax
from jax.experimental import pallas as pl
from jax.experimental.pallas import tpu as pltpu
from jax.sharding import PartitionSpec as P

MESH = pl.DeviceIdType.MESH
F32 = jnp.float32
BF16 = jnp.bfloat16
VMEM_LIMIT = 56 * 2**20

ROWS = 22
ROWS_PAD = 24
COLS = 176
CHANNELS = 128
HALF = 64
LANES = 384
BLOCKS = 32
NT = (((1,), (1,)), ((), ()))
TN = (((0,), (0,)), ((), ()))


def sigmoid(x):
    return 0.5 * jnp.tanh(0.5 * x) + 0.5


def place():
    row = lax.axis_index("row")
    col = lax.axis_index("col")
    return row, col


def chip_at(row, col, hop):
    z, y, x = row // 8, ((row // 4) % 2) * 2 + col // 2, row % 4
    z, y, x = (z + hop[0]) % 4, (y + hop[1]) % 4, (x + hop[2]) % 4
    row2 = z * 8 + (y // 2) * 4 + x
    low = y % 2
    return {"row": row2, "col": low * 2 + col % 2}, row2 * 2 + low


def hop_order():
    left = [(a, b, c) for a in range(4) for b in range(4) for c in range(4)][1:]
    use = [0] * 6
    order = []

    def after(hop):
        then = list(use)
        for axis, step in enumerate(hop):
            then[2 * axis] += (0, 2, 2, 0)[step]
            then[2 * axis + 1] += (0, 0, 2, 2)[step]
        return then

    def score(hop):
        then = after(hop)
        return max(then) - min(then), sum(v * v for v in then), (hop[0] * 37 + hop[1] * 11 + hop[2] * 5) % 17

    while left:
        best = min(left, key=score)
        use = after(best)
        left.remove(best)
        order.append(best)
    return order


HOPS = hop_order()
GROUPS = (
    [(u, u) for u in range(8)],
    [(u, 8 + u) for u in range(8)],
    [(0, 18), (1, 19), (2, 20), (3, 21), (6, 16), (7, 17)],
)


def right_row(j):
    return 24 + j if j < 16 else 6 + j if j < 18 else 22 + j


def wait_bytes(ref, sem):
    pltpu.make_async_copy(ref, ref, sem).wait()


def kernel(
    own_ref, gain_hbm, weight_hbm, gate_weight_hbm, out_gain_hbm, out_weight_hbm, out_ref,
    gain_ref, weight_ref, gate_weight_ref, out_gain_ref, out_weight_ref,
    own, wt, main, rest, main32, rest32, g32, lr_a, lr_r, lr_b, g, g_relay, lr_a_in, lr_r_in, lr_b_in, g_in, left, right, p, p_in, p_sib, p32, gates, gains, ws, mixed, packed,
    load_sems, map_send, map_recv, lr_send, lr_a_recv, lr_r_recv, lr_b_recv, g_send, g_recv, relay_send, relay_recv, p_send, p_recv, sib_send, sib_recv,
):
    row, col = place()
    half = col % 2
    me = row * 2 + col // 2
    sibling = {"row": row, "col": col + 1 - 2 * half}
    barrier = pltpu.get_barrier_semaphore()

    def signal(device):
        pl.semaphore_signal(barrier, inc=1, device_id=device, device_id_type=MESH)

    z, y_hi, x = row // 8, (row // 4) % 2, row % 4
    base = 8 * col + 4 * y_hi
    other = (z + 2) % 4
    owners, relays = [], []
    for n in range(4):
        x2 = (x + n) % 4
        owners.append((4 * y_hi + x2, {"row": base + x2, "col": z}))
        relays.append((4 - 4 * y_hi + x2, {"row": base + x2, "col": other}))
    forward = {"row": row + 4 - 8 * y_hi, "col": (col + 2) % 4}
    is_own = z == col

    for hop in sorted(HOPS, key=lambda hop: -sum(min(v, 4 - v) for v in hop)):
        device, _ = chip_at(row, col, hop)
        signal(device)
        signal({"row": device["row"], "col": device["col"] + 1 - 2 * half})
    signal(sibling)

    loads = [
        pltpu.make_async_copy(src, dst, load_sems.at[n])
        for n, (src, dst) in enumerate(
            (
                (own_ref, own),
                (gain_hbm, gain_ref),
                (weight_hbm, weight_ref),
                (gate_weight_hbm, gate_weight_ref),
                (out_gain_hbm, out_gain_ref),
                (out_weight_hbm, out_weight_ref),
            )
        )
    ]
    for load in loads:
        load.start()

    for load in loads[1:]:
        load.wait()
    wt[...] = weight_ref[...].astype(F32).T
    parts = [wt[pl.ds(pl.multiple_of(128 * n + HALF * half, HALF), HALF), :] for n in range(4)]
    weight = jnp.concatenate(parts, axis=0).astype(BF16)
    weight_all = wt[...].astype(BF16)
    ones = jnp.full((128, 128), 1.0 / 128, BF16)
    rest[:, 96:128, :] = jnp.zeros((ROWS, 32, 128), BF16)
    for pad in (44, 45, 46, 47):
        main32[pl.ds(pad, CHANNELS, stride=48), :] = jnp.zeros((CHANNELS, 128), F32)
        rest32[pl.ds(pad, HALF, stride=48), :] = jnp.zeros((HALF, 128), F32)
    for pad in (22, 23):
        g32[pl.ds(pad, COLS, stride=ROWS_PAD), :] = jnp.zeros((COLS, 128), F32)

    loads[0].wait()

    @pl.loop(0, 2)
    def _(n):
        for u in range(11):
            i = 11 * n + u
            v = own[i]
            center = v.astype(F32) - jnp.dot(v, ones, preferred_element_type=F32)
            spread = jnp.dot((center * center).astype(BF16), ones, preferred_element_type=F32)
            y = center * lax.rsqrt(spread + 1e-05) * gain_ref[...]
            main[i] = y[0:128].astype(BF16)
            rest[i, 0:48, :] = y[128:176].astype(BF16)
            g32[pl.ds(i, COLS, stride=ROWS_PAD), :] = y

    def factors(target, rows, n, weights, normed):
        projected = lax.dot_general(weights, normed.reshape(256, 128), NT, preferred_element_type=F32)
        one = sigmoid(projected[0:rows]) * projected[rows : 2 * rows]
        two = sigmoid(projected[2 * rows : 3 * rows]) * projected[3 * rows :]
        for u in range(2):
            lanes = slice(128 * u, 128 * (u + 1))
            target[pl.ds(2 * n + u, rows, stride=48), :] = one[:, lanes]
            target[pl.ds(right_row(2 * n + u), rows, stride=48), :] = two[:, lanes]

    def pack_pairs(v):
        for n in range(2):
            rows = pl.ds(pl.multiple_of((22 * v + 11 * n) * ROWS_PAD, 8), 11 * ROWS_PAD)
            g[v, pl.ds(11 * n, 11)] = g32[rows, :].reshape(11, ROWS_PAD, 128).astype(BF16)

    def send_pairs(step):
        n, rows = step // 2, pl.ds(11 * (step % 2), 11)
        v, device = relays[n]
        pltpu.make_async_remote_copy(
            src_ref=g.at[v, rows],
            dst_ref=g_relay.at[x, rows],
            send_sem=g_send.at[v],
            recv_sem=relay_recv.at[x, step % 2],
            device_id=device,
            device_id_type=MESH,
        ).start()

        m = (n + 2) % 4
        v2, device2 = owners[m]

        def send_direct():
            pltpu.make_async_remote_copy(
                src_ref=g.at[v2, rows],
                dst_ref=g_in.at[row % 8, rows],
                send_sem=g_send.at[v2],
                recv_sem=g_recv.at[row % 8],
                device_id=device2,
                device_id_type=MESH,
            ).start()

        if m == 0:

            @pl.when(is_own)
            def _():
                pltpu.make_async_copy(g.at[v2, rows], g_in.at[v2, rows], g_recv.at[v2]).start()

            pl.when(jnp.logical_not(is_own))(send_direct)
        else:
            send_direct()

    def send_on(step):
        s, rows = (x + 4 - step // 2) % 4, pl.ds(11 * (step % 2), 11)
        wait_bytes(g_relay.at[s, rows], relay_recv.at[s, step % 2])
        pltpu.make_async_remote_copy(
            src_ref=g_relay.at[s, rows],
            dst_ref=g_in.at[4 * y_hi + s, rows],
            send_sem=relay_send.at[s],
            recv_sem=g_recv.at[4 * y_hi + s],
            device_id=forward,
            device_id_type=MESH,
        ).start()

    for n in (0, 1):
        pack_pairs(relays[n][0])
        pack_pairs(owners[(n + 2) % 4][0])

    pl.semaphore_wait(barrier, 127)

    swap_rest = pltpu.make_async_remote_copy(
        src_ref=rest.at[:, pl.ds(0, 48), :],
        dst_ref=rest.at[:, pl.ds(48, 48), :],
        send_sem=map_send,
        recv_sem=map_recv,
        device_id=sibling,
        device_id_type=MESH,
    )
    swap_rest.start()
    send_pairs(0)
    send_pairs(1)
    for n in (2, 3):
        pack_pairs(relays[n][0])
        pack_pairs(owners[(n + 2) % 4][0])

    for n in range(11):
        factors(main32, CHANNELS, n, weight_all, main[2 * n : 2 * n + 2])


    lane = lax.broadcasted_iota(jnp.int32, (8, 128), 1)
    place8 = lax.broadcasted_iota(jnp.int32, (8, 128), 0)

    def rows_of(source, channel, start, count):
        return source[pl.ds(pl.multiple_of(channel * 48 + start, 8), count), :]

    def send(buffer, index, target, recv, device, part):
        if device is None:
            pltpu.make_async_copy(buffer.at[index], target, recv.at[row // 2]).start()
        else:
            pltpu.make_async_remote_copy(
                src_ref=buffer.at[index],
                dst_ref=target,
                send_sem=lr_send.at[part],
                recv_sem=recv.at[row // 2],
                device_id=device,
                device_id_type=MESH,
            ).start()

    def send_first(chip, same, device):
        channel = chip + (HALF * half if same else HALF - HALF * half)
        lr_a[channel] = rows_of(main32, channel, 0, 40).astype(BF16)
        send(lr_a, channel, lr_a_in.at[me, half], lr_a_recv, device, 0)

    def send_rest(chip, device):
        held = rows_of(rest32, chip, 0, 40)
        full = [
            jnp.where(lane < 96, held[8 * q : 8 * q + 8], pltpu.roll(held[32:40], 96 - 32 * q, 1)) for q in range(3)
        ]
        lr_r[chip] = jnp.concatenate(full + [held[24:32]], axis=0).astype(BF16)
        send(lr_r, chip, lr_r_in.at[me], lr_r_recv, device, 1)

    def send_second(chip, same, device):
        channel = chip + (HALF * half if same else HALF - HALF * half)
        held = rows_of(main32, channel, 40, 8)
        if same:
            held = jnp.where(place8 < 4, held, pltpu.roll(rows_of(rest32, chip, 40, 8), 4, 0))
        lr_b[channel] = held.astype(BF16)
        send(lr_b, channel, lr_b_in.at[me, half], lr_b_recv, device, 2)

    def send_both(send_one, start, stop):
        for hop in HOPS[start:stop]:
            device, chip = chip_at(row, col, hop)
            send_one(chip, True, device)
            send_one(chip, False, {"row": device["row"], "col": device["col"] + 1 - 2 * half})
        if start == 0:
            send_one(me, False, sibling)
            send_one(me, True, None)

    for step in range(8):
        if step >= 2:
            send_pairs(step)
        if step < 4:
            send_both(send_first, 16 * step, 16 * step + 16)
        elif step < 6:
            for hop in HOPS[32 * (step - 4) : 32 * (step - 3)]:
                device, chip = chip_at(row, col, hop)
                send_rest(chip, device)
            if step == 4:
                send_rest(me, None)
        else:
            send_both(send_second, 32 * (step - 6), 32 * (step - 5))
        if step == 1:
            swap_rest.wait()
            for n in range(11):
                factors(rest32, HALF, n, weight, rest[2 * n : 2 * n + 2])
        if step >= 2:
            send_on(step - 2)

    def group(n):
        b = (row // 2 + n) % 16
        return b, pl.ds(pl.multiple_of(4 * b, 4), 4)

    def take_right(b, k, lanes, one, two):
        rows = pl.ds(pl.multiple_of(256 * k + 16 * b, 16), 16)
        right[rows, lanes] = jnp.concatenate([one, two], axis=0).astype(BF16)

    def tiles(b):
        for low in range(2):
            for t in range(3):
                yield 4 * b + low, t, slice(LANES * low + 128 * t, LANES * low + 128 * (t + 1))

    def first_rows(chip, t):
        if t < 2:
            return lr_a_in[chip, t].astype(F32)
        held = lr_r_in[chip].astype(F32)
        last = [pltpu.roll(held[8 * q : 8 * q + 8], 32 + 32 * q, 1) for q in range(3)]
        last = jnp.where(lane < 32, last[0], jnp.where(lane < 64, last[1], last[2]))
        rows = [held[8 * q : 8 * q + 8] for q in range(4)] + [last]
        return jnp.concatenate([jnp.where(lane < 96, v, 0.0) for v in rows], axis=0)

    def second_rows(chip, t):
        if t < 2:
            early, late = lr_a_in[chip, t, 16:32].astype(F32)[:8], lr_b_in[chip, t].astype(F32)
        else:
            early = jnp.where(lane < 96, lr_r_in[chip, 16:32].astype(F32)[:8], 0.0)
            late = pltpu.roll(lr_b_in[chip, half].astype(F32), 4, 0)
        return jnp.where(place8 < 6, late, early)

    def take_first(n):
        b, chips = group(n)
        wait_bytes(lr_a_in.at[chips], lr_a_recv.at[b])
        wait_bytes(lr_r_in.at[chips], lr_r_recv.at[b])
        for chip, t, lanes in tiles(b):
            one, two = first_rows(chip, t), first_rows(chip + 2, t)
            rows = pl.ds(pl.multiple_of(48 * b, 48), 48)
            left[rows, lanes] = jnp.concatenate([one[:24], two[:24]], axis=0).astype(BF16)
            take_right(b, 0, lanes, one[24:32], two[24:32])
            take_right(b, 1, lanes, one[32:], two[32:])

    def take_second(n):
        b, chips = group(n)
        wait_bytes(lr_b_in.at[chips], lr_b_recv.at[b])
        for chip, t, lanes in tiles(b):
            take_right(b, 2, lanes, second_rows(chip, t), second_rows(chip + 2, t))

    def send_products(k):
        acc = lax.dot_general(right[256 * k : 256 * (k + 1), :], left[...], NT, preferred_element_type=F32)
        for r in range(BLOCKS):
            for low in range(2):
                p[k, 2 * r + low] = acc[8 * r : 8 * r + 8, LANES * low : LANES * (low + 1)].astype(BF16)
        pltpu.make_async_copy(p.at[k, me], p_in.at[k, me], p_recv.at[k]).start()
        for hop in HOPS:
            device, chip = chip_at(row, col, hop)
            pltpu.make_async_remote_copy(
                src_ref=p.at[k, chip],
                dst_ref=p_in.at[k, me],
                send_sem=p_send.at[k],
                recv_sem=p_recv.at[k],
                device_id=device,
                device_id_type=MESH,
            ).start()

    pl.loop(0, 8)(take_first)
    send_on(6)
    pl.loop(8, 16)(take_first)
    send_on(7)
    send_products(0)
    send_products(1)
    pl.loop(0, 16)(take_second)
    send_products(2)

    for s in range(8):
        wait_bytes(g_in.at[s], g_recv.at[s])

    @pl.loop(0, 2)
    def _(n):
        for u in range(11):
            j = 11 * n + u
            pairs = jnp.concatenate([g_in[s, j].astype(F32) for s in range(8)], axis=0).astype(BF16)
            gates[j] = sigmoid(jnp.dot(pairs, gate_weight_ref[...], preferred_element_type=F32))

    gains[...] = jnp.broadcast_to(out_gain_ref[...], (128, 128)).T
    ws[...] = out_weight_ref[...].astype(F32)
    ours = pl.ds(pl.multiple_of(HALF * half, HALF), HALF)
    theirs = pl.ds(pl.multiple_of(HALF - HALF * half, HALF), HALF)
    gain = jnp.concatenate([gains[ours, :], gains[theirs, :]], axis=0)
    gain = jnp.concatenate([gain, gain], axis=1)
    out_weight = jnp.concatenate([ws[ours, :], ws[theirs, :]], axis=0).astype(BF16)

    for k, members in enumerate(GROUPS):
        wait_bytes(p_in.at[k], p_recv.at[k])
        swap = pltpu.make_async_remote_copy(
            src_ref=p_in.at[k, :, :, pl.ds(pl.multiple_of(128 - 128 * half, 128), 256)],
            dst_ref=p_sib.at[k],
            send_sem=sib_send.at[k],
            recv_sem=sib_recv.at[k],
            device_id=sibling,
            device_id_type=MESH,
        )
        swap.start()
        for t in range(2):
            lanes = pl.ds(pl.multiple_of(128 * half + 128 * t, 128), 128)
            p32[t, 0:512, :] = p_in[k, :, :, lanes].astype(F32).reshape(512, 128)
        swap.wait()
        for t in range(2):
            p32[t, 512:1024, :] = p_sib[k, :, :, 128 * t : 128 * (t + 1)].astype(F32).reshape(512, 128)
        for u, j in members:
            q = jnp.concatenate([p32[t, pl.ds(u, CHANNELS, stride=8), :] for t in range(2)], axis=1)
            center = q - jnp.mean(q, axis=0, keepdims=True)
            spread = jnp.mean(center * center, axis=0, keepdims=True)
            hidden = (center * lax.rsqrt(spread + 1e-05) * gain).astype(BF16)
            mixed[u] = lax.dot_general(hidden, out_weight, TN, preferred_element_type=F32)
            update = gates[j] * mixed[u, pl.ds(pl.multiple_of(64 * half, 64), 192), :]
            for s in range(8):
                packed[u, 22 * s : 22 * s + 24, :] = update[24 * s : 24 * s + 24]
            out_ref[j] = packed[u, 0:COLS, :].astype(BF16)

    wait_bytes(lr_a.at[pl.ds(0, 127)], lr_send.at[0])
    wait_bytes(lr_r.at[pl.ds(0, 63)], lr_send.at[1])
    wait_bytes(lr_b.at[pl.ds(0, 127)], lr_send.at[2])
    for k in range(3):
        wait_bytes(p.at[k, pl.ds(0, 63)], p_send.at[k])
    for v, _ in relays + owners[1:]:
        wait_bytes(g.at[v], g_send.at[v])
    for s in range(4):
        wait_bytes(g_relay.at[s], relay_send.at[s])

    @pl.when(jnp.logical_not(is_own))
    def _():
        wait_bytes(g.at[owners[0][0]], g_send.at[owners[0][0]])


def fused(*args):
    vmem = pl.BlockSpec(memory_space=pltpu.VMEM)
    return pl.pallas_call(
        kernel,
        out_shape=pltpu.VMEM((ROWS, COLS, 128), BF16),
        in_specs=[pl.BlockSpec(memory_space=pl.ANY)] * 6,
        out_specs=vmem,
        scratch_shapes=[
            pltpu.VMEM((1, 128), F32),
            pltpu.VMEM((128, 512), BF16),
            pltpu.VMEM((128, 128), BF16),
            pltpu.VMEM((1, 128), F32),
            pltpu.VMEM((128, 128), BF16),
            pltpu.VMEM((ROWS, COLS, 128), BF16),
            pltpu.VMEM((512, 128), F32),
            pltpu.VMEM((ROWS, 128, 128), BF16),
            pltpu.VMEM((ROWS, 128, 128), BF16),
            pltpu.VMEM((CHANNELS * 48, 128), F32),
            pltpu.VMEM((HALF * 48, 128), F32),
            pltpu.VMEM((COLS * ROWS_PAD, 128), F32),
            pltpu.VMEM((CHANNELS, 40, 128), BF16),
            pltpu.VMEM((HALF, 32, 128), BF16),
            pltpu.VMEM((CHANNELS, 8, 128), BF16),
            pltpu.VMEM((8, ROWS, ROWS_PAD, 128), BF16),
            pltpu.VMEM((4, ROWS, ROWS_PAD, 128), BF16),
            pltpu.VMEM((64, 2, 40, 128), BF16),
            pltpu.VMEM((64, 32, 128), BF16),
            pltpu.VMEM((64, 2, 8, 128), BF16),
            pltpu.VMEM((8, ROWS, ROWS_PAD, 128), BF16),
            pltpu.VMEM((768, 768), BF16),
            pltpu.VMEM((768, 768), BF16),
            pltpu.VMEM((3, 64, 8, LANES), BF16),
            pltpu.VMEM((3, 64, 8, LANES), BF16),
            pltpu.VMEM((3, 64, 8, 256), BF16),
            pltpu.VMEM((2, CHANNELS * 8, 128), F32),
            pltpu.VMEM((ROWS, 192, 128), F32),
            pltpu.VMEM((128, 128), F32),
            pltpu.VMEM((128, 128), F32),
            pltpu.VMEM((8, 256, 128), F32),
            pltpu.VMEM((8, 184, 128), F32),
            pltpu.SemaphoreType.DMA((6,)),
            pltpu.SemaphoreType.DMA,
            pltpu.SemaphoreType.DMA,
            pltpu.SemaphoreType.DMA((3,)),
            pltpu.SemaphoreType.DMA((16,)),
            pltpu.SemaphoreType.DMA((16,)),
            pltpu.SemaphoreType.DMA((16,)),
            pltpu.SemaphoreType.DMA((8,)),
            pltpu.SemaphoreType.DMA((8,)),
            pltpu.SemaphoreType.DMA((4,)),
            pltpu.SemaphoreType.DMA((4, 2)),
            pltpu.SemaphoreType.DMA((3,)),
            pltpu.SemaphoreType.DMA((3,)),
            pltpu.SemaphoreType.DMA((3,)),
            pltpu.SemaphoreType.DMA((3,)),
        ],
        compiler_params=pltpu.CompilerParams(
            collective_id=0, has_side_effects=True, vmem_limit_bytes=VMEM_LIMIT
        ),
        name="triangle_update",
    )(*args)


def copy_kernel(src_ref, dst_ref, sems):
    copies = [pltpu.make_async_copy(src_ref.at[i], dst_ref.at[i], sems.at[i]) for i in range(ROWS)]
    for copy in copies:
        copy.start()
    for copy in copies:
        copy.wait()


def copy_out(x):
    return pl.pallas_call(
        copy_kernel,
        out_shape=jax.ShapeDtypeStruct(x.shape, x.dtype),
        in_specs=[pl.BlockSpec(memory_space=pltpu.VMEM)],
        out_specs=pl.BlockSpec(memory_space=pl.ANY),
        scratch_shapes=[pltpu.SemaphoreType.DMA((ROWS,))],
        name="copy_out",
    )(pltpu.with_memory_space_constraint(x, pltpu.VMEM))


def body(pair_map, in_gain, project_weight, gate_weight, out_gain, out_weight):
    update = fused(
        pair_map, in_gain.reshape(1, 128), project_weight, gate_weight, out_gain.reshape(1, 128), out_weight
    )
    return copy_out(update)


def solution(mesh):
    return jax.shard_map(
        body,
        mesh=mesh,
        in_specs=(P("row", "col", None), P(), P(), P(), P(), P()),
        out_specs=P("row", "col", None),
        check_vma=False,
    )
```

```python
import functools

import jax
import jax.numpy as jnp
from jax import lax
from jax.experimental import pallas as pl
from jax.experimental.pallas import tpu as pltpu
from jax.sharding import PartitionSpec as P

MESH = pl.DeviceIdType.MESH
F32 = jnp.float32
BF16 = jnp.bfloat16
VMEM_LIMIT = 56 * 2**20

ROWS = 22
ROWS_PAD = 24
COLS = 176
CHANNELS = 128
HALF = 64
LANES = 384
BLOCKS = 32
NT = (((1,), (1,)), ((), ()))
TN = (((0,), (0,)), ((), ()))


def sigmoid(x):
    return 0.5 * jnp.tanh(0.5 * x) + 0.5


def place():
    row = lax.axis_index("row")
    col = lax.axis_index("col")
    return row, col


def chip_at(row, col, hop):
    z, y, x = row // 8, ((row // 4) % 2) * 2 + col // 2, row % 4
    z, y, x = (z + hop[0]) % 4, (y + hop[1]) % 4, (x + hop[2]) % 4
    row2 = z * 8 + (y // 2) * 4 + x
    low = y % 2
    return {"row": row2, "col": low * 2 + col % 2}, row2 * 2 + low


HOP_ORDER = (
    42, 4, 46, 58, 16, 1, 43, 41, 3, 48, 26, 12, 38, 54, 28, 34, 8, 59, 17, 45, 7,
    30, 52, 47, 5, 13, 39, 62, 20, 2, 40, 15, 37, 22, 60, 10, 32, 19, 57, 51, 25, 27,
    49, 61, 23, 6, 44, 50, 24, 29, 55, 18, 56, 63, 21, 11, 33, 36, 14, 53, 31, 35, 9,
)
HOPS = [(n // 16, n // 4 % 4, n % 4) for n in HOP_ORDER]
GROUPS = (
    [(u, u) for u in range(8)],
    [(u, 8 + u) for u in range(8)],
    [(0, 18), (1, 19), (2, 20), (3, 21), (6, 16), (7, 17)],
)


def right_row(j):
    return 24 + j if j < 16 else 6 + j if j < 18 else 22 + j


def wait_bytes(ref, sem):
    pltpu.make_async_copy(ref, ref, sem).wait()


def kernel(
    own_ref, gain_hbm, weight_hbm, gate_weight_hbm, out_gain_hbm, out_weight_hbm, out_ref,
    gain_ref, weight_ref, gate_weight_ref, out_gain_ref, out_weight_ref,
    own, wt, main, rest, main32, rest32, g32, lr_a, lr_r, lr_b, g, g_relay, lr_a_in, lr_r_in, lr_b_in, g_in, left, right, p, p_in, p_sib, p32, gates, gains, ws, mixed, packed,
    load_sems, map_send, map_recv, lr_send, lr_a_recv, lr_r_recv, lr_b_recv, g_send, g_recv, relay_send, relay_recv, p_send, p_recv, sib_send, sib_recv,
):
    row, col = place()
    half = col % 2
    me = row * 2 + col // 2
    sibling = {"row": row, "col": col + 1 - 2 * half}
    barrier = pltpu.get_barrier_semaphore()

    def signal(device):
        pl.semaphore_signal(barrier, inc=1, device_id=device, device_id_type=MESH)

    z, y_hi, x = row // 8, (row // 4) % 2, row % 4
    base = 8 * col + 4 * y_hi
    other = (z + 2) % 4
    owners, relays = [], []
    for n in range(4):
        x2 = (x + n) % 4
        owners.append((4 * y_hi + x2, {"row": base + x2, "col": z}))
        relays.append((4 - 4 * y_hi + x2, {"row": base + x2, "col": other}))
    forward = {"row": row + 4 - 8 * y_hi, "col": (col + 2) % 4}
    is_own = z == col

    for hop in sorted(HOPS, key=lambda hop: -sum(min(v, 4 - v) for v in hop)):
        device, _ = chip_at(row, col, hop)
        signal(device)
        signal({"row": device["row"], "col": device["col"] + 1 - 2 * half})
    signal(sibling)

    loads = [
        pltpu.make_async_copy(src, dst, load_sems.at[n])
        for n, (src, dst) in enumerate(
            (
                (own_ref, own),
                (gain_hbm, gain_ref),
                (weight_hbm, weight_ref),
                (gate_weight_hbm, gate_weight_ref),
                (out_gain_hbm, out_gain_ref),
                (out_weight_hbm, out_weight_ref),
            )
        )
    ]
    for load in loads:
        load.start()

    for load in loads[1:]:
        load.wait()
    wt[...] = weight_ref[...].astype(F32).T
    parts = [wt[pl.ds(pl.multiple_of(128 * n + HALF * half, HALF), HALF), :] for n in range(4)]
    weight = jnp.concatenate(parts, axis=0).astype(BF16)
    weight_all = wt[...].astype(BF16)
    ones = jnp.full((128, 128), 1.0 / 128, BF16)
    rest[:, 96:128, :] = jnp.zeros((ROWS, 32, 128), BF16)
    for pad in (44, 45, 46, 47):
        main32[pl.ds(pad, CHANNELS, stride=48), :] = jnp.zeros((CHANNELS, 128), F32)
        rest32[pl.ds(pad, HALF, stride=48), :] = jnp.zeros((HALF, 128), F32)
    for pad in (22, 23):
        g32[pl.ds(pad, COLS, stride=ROWS_PAD), :] = jnp.zeros((COLS, 128), F32)

    loads[0].wait()

    @pl.loop(0, 2)
    def _(n):
        for u in range(11):
            i = 11 * n + u
            v = own[i]
            center = v.astype(F32) - jnp.dot(v, ones, preferred_element_type=F32)
            spread = jnp.dot((center * center).astype(BF16), ones, preferred_element_type=F32)
            y = center * lax.rsqrt(spread + 1e-05) * gain_ref[...]
            main[i] = y[0:128].astype(BF16)
            rest[i, 0:48, :] = y[128:176].astype(BF16)
            g32[pl.ds(i, COLS, stride=ROWS_PAD), :] = y

    def factors(target, rows, n, weights, normed):
        projected = lax.dot_general(weights, normed.reshape(256, 128), NT, preferred_element_type=F32)
        one = sigmoid(projected[0:rows]) * projected[rows : 2 * rows]
        two = sigmoid(projected[2 * rows : 3 * rows]) * projected[3 * rows :]
        for u in range(2):
            lanes = slice(128 * u, 128 * (u + 1))
            target[pl.ds(2 * n + u, rows, stride=48), :] = one[:, lanes]
            target[pl.ds(right_row(2 * n + u), rows, stride=48), :] = two[:, lanes]

    def pack_pairs(v):
        for n in range(2):
            rows = pl.ds(pl.multiple_of((22 * v + 11 * n) * ROWS_PAD, 8), 11 * ROWS_PAD)
            g[v, pl.ds(11 * n, 11)] = g32[rows, :].reshape(11, ROWS_PAD, 128).astype(BF16)

    def send_pairs(step):
        n, rows = step // 2, pl.ds(11 * (step % 2), 11)
        v, device = relays[n]
        pltpu.make_async_remote_copy(
            src_ref=g.at[v, rows],
            dst_ref=g_relay.at[x, rows],
            send_sem=g_send.at[v],
            recv_sem=relay_recv.at[x, step % 2],
            device_id=device,
            device_id_type=MESH,
        ).start()

        m = (n + 2) % 4
        v2, device2 = owners[m]

        def send_direct():
            pltpu.make_async_remote_copy(
                src_ref=g.at[v2, rows],
                dst_ref=g_in.at[row % 8, rows],
                send_sem=g_send.at[v2],
                recv_sem=g_recv.at[row % 8],
                device_id=device2,
                device_id_type=MESH,
            ).start()

        if m == 0:

            @pl.when(is_own)
            def _():
                pltpu.make_async_copy(g.at[v2, rows], g_in.at[v2, rows], g_recv.at[v2]).start()

            pl.when(jnp.logical_not(is_own))(send_direct)
        else:
            send_direct()

    def send_on(step):
        s, rows = (x + 4 - step // 2) % 4, pl.ds(11 * (step % 2), 11)
        wait_bytes(g_relay.at[s, rows], relay_recv.at[s, step % 2])
        pltpu.make_async_remote_copy(
            src_ref=g_relay.at[s, rows],
            dst_ref=g_in.at[4 * y_hi + s, rows],
            send_sem=relay_send.at[s],
            recv_sem=g_recv.at[4 * y_hi + s],
            device_id=forward,
            device_id_type=MESH,
        ).start()

    for n in (0, 1):
        pack_pairs(relays[n][0])
        pack_pairs(owners[(n + 2) % 4][0])

    pl.semaphore_wait(barrier, 127)

    swap_rest = pltpu.make_async_remote_copy(
        src_ref=rest.at[:, pl.ds(0, 48), :],
        dst_ref=rest.at[:, pl.ds(48, 48), :],
        send_sem=map_send,
        recv_sem=map_recv,
        device_id=sibling,
        device_id_type=MESH,
    )
    swap_rest.start()
    send_pairs(0)
    send_pairs(1)
    for n in (2, 3):
        pack_pairs(relays[n][0])
        pack_pairs(owners[(n + 2) % 4][0])

    for n in range(11):
        factors(main32, CHANNELS, n, weight_all, main[2 * n : 2 * n + 2])


    lane = lax.broadcasted_iota(jnp.int32, (8, 128), 1)
    place8 = lax.broadcasted_iota(jnp.int32, (8, 128), 0)

    def rows_of(source, channel, start, count):
        return source[pl.ds(pl.multiple_of(channel * 48 + start, 8), count), :]

    def send(buffer, index, target, recv, device, part):
        if device is None:
            pltpu.make_async_copy(buffer.at[index], target, recv.at[row // 2]).start()
        else:
            pltpu.make_async_remote_copy(
                src_ref=buffer.at[index],
                dst_ref=target,
                send_sem=lr_send.at[part],
                recv_sem=recv.at[row // 2],
                device_id=device,
                device_id_type=MESH,
            ).start()

    def send_first(chip, same, device):
        channel = chip + (HALF * half if same else HALF - HALF * half)
        lr_a[channel] = rows_of(main32, channel, 0, 40).astype(BF16)
        send(lr_a, channel, lr_a_in.at[me, half], lr_a_recv, device, 0)

    def send_rest(chip, device):
        held = rows_of(rest32, chip, 0, 40)
        full = [
            jnp.where(lane < 96, held[8 * q : 8 * q + 8], pltpu.roll(held[32:40], 96 - 32 * q, 1)) for q in range(3)
        ]
        lr_r[chip] = jnp.concatenate(full + [held[24:32]], axis=0).astype(BF16)
        send(lr_r, chip, lr_r_in.at[me], lr_r_recv, device, 1)

    def send_second(chip, same, device):
        channel = chip + (HALF * half if same else HALF - HALF * half)
        held = rows_of(main32, channel, 40, 8)
        if same:
            held = jnp.where(place8 < 4, held, pltpu.roll(rows_of(rest32, chip, 40, 8), 4, 0))
        lr_b[channel] = held.astype(BF16)
        send(lr_b, channel, lr_b_in.at[me, half], lr_b_recv, device, 2)

    def send_both(send_one, start, stop):
        for hop in HOPS[start:stop]:
            device, chip = chip_at(row, col, hop)
            send_one(chip, True, device)
            send_one(chip, False, {"row": device["row"], "col": device["col"] + 1 - 2 * half})
        if start == 0:
            send_one(me, False, sibling)
            send_one(me, True, None)

    for step in range(8):
        if step >= 2:
            send_pairs(step)
        if step < 4:
            send_both(send_first, 16 * step, 16 * step + 16)
        elif step < 6:
            for hop in HOPS[32 * (step - 4) : 32 * (step - 3)]:
                device, chip = chip_at(row, col, hop)
                send_rest(chip, device)
            if step == 4:
                send_rest(me, None)
        else:
            send_both(send_second, 32 * (step - 6), 32 * (step - 5))
        if step == 1:
            swap_rest.wait()
            for n in range(11):
                factors(rest32, HALF, n, weight, rest[2 * n : 2 * n + 2])
        if step >= 1:
            send_on(step - 1)

    def group(n):
        b = (row // 2 + n) % 16
        return b, pl.ds(pl.multiple_of(4 * b, 4), 4)

    def take_right(b, k, lanes, one, two):
        rows = pl.ds(pl.multiple_of(256 * k + 16 * b, 16), 16)
        right[rows, lanes] = jnp.concatenate([one, two], axis=0).astype(BF16)

    def tiles(b):
        for low in range(2):
            for t in range(3):
                yield 4 * b + low, t, slice(LANES * low + 128 * t, LANES * low + 128 * (t + 1))

    def first_rows(chip, t):
        if t < 2:
            return lr_a_in[chip, t].astype(F32)
        held = lr_r_in[chip].astype(F32)
        last = [pltpu.roll(held[8 * q : 8 * q + 8], 32 + 32 * q, 1) for q in range(3)]
        last = jnp.where(lane < 32, last[0], jnp.where(lane < 64, last[1], last[2]))
        rows = [held[8 * q : 8 * q + 8] for q in range(4)] + [last]
        return jnp.concatenate([jnp.where(lane < 96, v, 0.0) for v in rows], axis=0)

    def second_rows(chip, t):
        if t < 2:
            early, late = lr_a_in[chip, t, 16:32].astype(F32)[:8], lr_b_in[chip, t].astype(F32)
        else:
            early = jnp.where(lane < 96, lr_r_in[chip, 16:32].astype(F32)[:8], 0.0)
            late = pltpu.roll(lr_b_in[chip, half].astype(F32), 4, 0)
        return jnp.where(place8 < 6, late, early)

    def take_first(n):
        b, chips = group(n)
        wait_bytes(lr_a_in.at[chips], lr_a_recv.at[b])
        wait_bytes(lr_r_in.at[chips], lr_r_recv.at[b])
        for chip, t, lanes in tiles(b):
            one, two = first_rows(chip, t), first_rows(chip + 2, t)
            rows = pl.ds(pl.multiple_of(48 * b, 48), 48)
            left[rows, lanes] = jnp.concatenate([one[:24], two[:24]], axis=0).astype(BF16)
            take_right(b, 0, lanes, one[24:32], two[24:32])
            take_right(b, 1, lanes, one[32:], two[32:])

    def take_second(n):
        b, chips = group(n)
        wait_bytes(lr_b_in.at[chips], lr_b_recv.at[b])
        for chip, t, lanes in tiles(b):
            take_right(b, 2, lanes, second_rows(chip, t), second_rows(chip + 2, t))

    def send_products(k):
        acc = lax.dot_general(right[256 * k : 256 * (k + 1), :], left[...], NT, preferred_element_type=F32)
        for r in range(BLOCKS):
            for low in range(2):
                p[k, 2 * r + low] = acc[8 * r : 8 * r + 8, LANES * low : LANES * (low + 1)].astype(BF16)
        pltpu.make_async_copy(p.at[k, me], p_in.at[k, me], p_recv.at[k]).start()
        for hop in HOPS:
            device, chip = chip_at(row, col, hop)
            pltpu.make_async_remote_copy(
                src_ref=p.at[k, chip],
                dst_ref=p_in.at[k, me],
                send_sem=p_send.at[k],
                recv_sem=p_recv.at[k],
                device_id=device,
                device_id_type=MESH,
            ).start()

    pl.loop(0, 8)(take_first)
    send_on(7)
    pl.loop(8, 16)(take_first)
    send_products(0)
    send_products(1)
    pl.loop(0, 16)(take_second)
    send_products(2)

    for s in range(8):
        wait_bytes(g_in.at[s], g_recv.at[s])

    @pl.loop(0, 2)
    def _(n):
        for u in range(11):
            j = 11 * n + u
            pairs = jnp.concatenate([g_in[s, j].astype(F32) for s in range(8)], axis=0).astype(BF16)
            gates[j] = sigmoid(jnp.dot(pairs, gate_weight_ref[...], preferred_element_type=F32))

    gains[...] = jnp.broadcast_to(out_gain_ref[...], (128, 128)).T
    ws[...] = out_weight_ref[...].astype(F32)
    ours = pl.ds(pl.multiple_of(HALF * half, HALF), HALF)
    theirs = pl.ds(pl.multiple_of(HALF - HALF * half, HALF), HALF)
    gain = jnp.concatenate([gains[ours, :], gains[theirs, :]], axis=0)
    gain = jnp.concatenate([gain, gain], axis=1)
    out_weight = jnp.concatenate([ws[ours, :], ws[theirs, :]], axis=0).astype(BF16)

    for k, members in enumerate(GROUPS):
        wait_bytes(p_in.at[k], p_recv.at[k])
        swap = pltpu.make_async_remote_copy(
            src_ref=p_in.at[k, :, :, pl.ds(pl.multiple_of(128 - 128 * half, 128), 256)],
            dst_ref=p_sib.at[k],
            send_sem=sib_send.at[k],
            recv_sem=sib_recv.at[k],
            device_id=sibling,
            device_id_type=MESH,
        )
        swap.start()
        for t in range(2):
            lanes = pl.ds(pl.multiple_of(128 * half + 128 * t, 128), 128)
            p32[t, 0:512, :] = p_in[k, :, :, lanes].astype(F32).reshape(512, 128)
        swap.wait()
        for t in range(2):
            p32[t, 512:1024, :] = p_sib[k, :, :, 128 * t : 128 * (t + 1)].astype(F32).reshape(512, 128)
        for u, j in members:
            q = jnp.concatenate([p32[t, pl.ds(u, CHANNELS, stride=8), :] for t in range(2)], axis=1)
            center = q - jnp.mean(q, axis=0, keepdims=True)
            spread = jnp.mean(center * center, axis=0, keepdims=True)
            hidden = (center * lax.rsqrt(spread + 1e-05) * gain).astype(BF16)
            mixed[u] = lax.dot_general(hidden, out_weight, TN, preferred_element_type=F32)
            update = gates[j] * mixed[u, pl.ds(pl.multiple_of(64 * half, 64), 192), :]
            for s in range(8):
                packed[u, 22 * s : 22 * s + 24, :] = update[24 * s : 24 * s + 24]
            out_ref[j] = packed[u, 0:COLS, :].astype(BF16)

    wait_bytes(lr_a.at[pl.ds(0, 127)], lr_send.at[0])
    wait_bytes(lr_r.at[pl.ds(0, 63)], lr_send.at[1])
    wait_bytes(lr_b.at[pl.ds(0, 127)], lr_send.at[2])
    for k in range(3):
        wait_bytes(p.at[k, pl.ds(0, 63)], p_send.at[k])
    for v, _ in relays + owners[1:]:
        wait_bytes(g.at[v], g_send.at[v])
    for s in range(4):
        wait_bytes(g_relay.at[s], relay_send.at[s])

    @pl.when(jnp.logical_not(is_own))
    def _():
        wait_bytes(g.at[owners[0][0]], g_send.at[owners[0][0]])


def fused(*args):
    vmem = pl.BlockSpec(memory_space=pltpu.VMEM)
    return pl.pallas_call(
        kernel,
        out_shape=pltpu.VMEM((ROWS, COLS, 128), BF16),
        in_specs=[pl.BlockSpec(memory_space=pl.ANY)] * 6,
        out_specs=vmem,
        scratch_shapes=[
            pltpu.VMEM((1, 128), F32),
            pltpu.VMEM((128, 512), BF16),
            pltpu.VMEM((128, 128), BF16),
            pltpu.VMEM((1, 128), F32),
            pltpu.VMEM((128, 128), BF16),
            pltpu.VMEM((ROWS, COLS, 128), BF16),
            pltpu.VMEM((512, 128), F32),
            pltpu.VMEM((ROWS, 128, 128), BF16),
            pltpu.VMEM((ROWS, 128, 128), BF16),
            pltpu.VMEM((CHANNELS * 48, 128), F32),
            pltpu.VMEM((HALF * 48, 128), F32),
            pltpu.VMEM((COLS * ROWS_PAD, 128), F32),
            pltpu.VMEM((CHANNELS, 40, 128), BF16),
            pltpu.VMEM((HALF, 32, 128), BF16),
            pltpu.VMEM((CHANNELS, 8, 128), BF16),
            pltpu.VMEM((8, ROWS, ROWS_PAD, 128), BF16),
            pltpu.VMEM((4, ROWS, ROWS_PAD, 128), BF16),
            pltpu.VMEM((64, 2, 40, 128), BF16),
            pltpu.VMEM((64, 32, 128), BF16),
            pltpu.VMEM((64, 2, 8, 128), BF16),
            pltpu.VMEM((8, ROWS, ROWS_PAD, 128), BF16),
            pltpu.VMEM((768, 768), BF16),
            pltpu.VMEM((768, 768), BF16),
            pltpu.VMEM((3, 64, 8, LANES), BF16),
            pltpu.VMEM((3, 64, 8, LANES), BF16),
            pltpu.VMEM((3, 64, 8, 256), BF16),
            pltpu.VMEM((2, CHANNELS * 8, 128), F32),
            pltpu.VMEM((ROWS, 192, 128), F32),
            pltpu.VMEM((128, 128), F32),
            pltpu.VMEM((128, 128), F32),
            pltpu.VMEM((8, 256, 128), F32),
            pltpu.VMEM((8, 184, 128), F32),
            pltpu.SemaphoreType.DMA((6,)),
            pltpu.SemaphoreType.DMA,
            pltpu.SemaphoreType.DMA,
            pltpu.SemaphoreType.DMA((3,)),
            pltpu.SemaphoreType.DMA((16,)),
            pltpu.SemaphoreType.DMA((16,)),
            pltpu.SemaphoreType.DMA((16,)),
            pltpu.SemaphoreType.DMA((8,)),
            pltpu.SemaphoreType.DMA((8,)),
            pltpu.SemaphoreType.DMA((4,)),
            pltpu.SemaphoreType.DMA((4, 2)),
            pltpu.SemaphoreType.DMA((3,)),
            pltpu.SemaphoreType.DMA((3,)),
            pltpu.SemaphoreType.DMA((3,)),
            pltpu.SemaphoreType.DMA((3,)),
        ],
        compiler_params=pltpu.CompilerParams(
            collective_id=0, has_side_effects=True, vmem_limit_bytes=VMEM_LIMIT
        ),
        name="triangle_update",
    )(*args)


def copy_kernel(src_ref, dst_ref, sems):
    copies = [pltpu.make_async_copy(src_ref.at[i], dst_ref.at[i], sems.at[i]) for i in range(ROWS)]
    for copy in copies:
        copy.start()
    for copy in copies:
        copy.wait()


def copy_out(x):
    return pl.pallas_call(
        copy_kernel,
        out_shape=jax.ShapeDtypeStruct(x.shape, x.dtype),
        in_specs=[pl.BlockSpec(memory_space=pltpu.VMEM)],
        out_specs=pl.BlockSpec(memory_space=pl.ANY),
        scratch_shapes=[pltpu.SemaphoreType.DMA((ROWS,))],
        name="copy_out",
    )(pltpu.with_memory_space_constraint(x, pltpu.VMEM))


def body(pair_map, in_gain, project_weight, gate_weight, out_gain, out_weight):
    update = fused(
        pair_map, in_gain.reshape(1, 128), project_weight, gate_weight, out_gain.reshape(1, 128), out_weight
    )
    return copy_out(update)


def solution(mesh):
    return jax.shard_map(
        body,
        mesh=mesh,
        in_specs=(P("row", "col", None), P(), P(), P(), P(), P()),
        out_specs=P("row", "col", None),
        check_vma=False,
    )
```

```python
import functools

import jax
import jax.numpy as jnp
from jax import lax
from jax.experimental import pallas as pl
from jax.experimental.pallas import tpu as pltpu
from jax.sharding import PartitionSpec as P

MESH = pl.DeviceIdType.MESH
F32 = jnp.float32
BF16 = jnp.bfloat16
VMEM_LIMIT = 56 * 2**20

ROWS = 22
ROWS_PAD = 24
COLS = 176
CHANNELS = 128
HALF = 64
LANES = 384
BLOCKS = 32
NT = (((1,), (1,)), ((), ()))
TN = (((0,), (0,)), ((), ()))


def sigmoid(x):
    return 0.5 * jnp.tanh(0.5 * x) + 0.5


def place():
    row = lax.axis_index("row")
    col = lax.axis_index("col")
    return row, col


def chip_at(row, col, hop):
    z, y, x = row // 8, ((row // 4) % 2) * 2 + col // 2, row % 4
    z, y, x = (z + hop[0]) % 4, (y + hop[1]) % 4, (x + hop[2]) % 4
    row2 = z * 8 + (y // 2) * 4 + x
    low = y % 2
    return {"row": row2, "col": low * 2 + col % 2}, row2 * 2 + low


HOP_ORDER = (
    42, 4, 46, 58, 16, 1, 43, 41, 3, 48, 26, 12, 38, 54, 28, 34, 8, 59, 17, 45, 7,
    30, 52, 47, 5, 13, 39, 62, 20, 2, 40, 15, 37, 22, 60, 10, 32, 19, 57, 51, 25, 27,
    49, 61, 23, 6, 44, 50, 24, 29, 55, 18, 56, 63, 21, 11, 33, 36, 14, 53, 31, 35, 9,
)
HOPS = [(n // 16, n // 4 % 4, n % 4) for n in HOP_ORDER]
GROUPS = (
    [(u, u) for u in range(8)],
    [(u, 8 + u) for u in range(8)],
    [(0, 18), (1, 19), (2, 20), (3, 21), (6, 16), (7, 17)],
)


def right_row(j):
    return 24 + j if j < 16 else 6 + j if j < 18 else 22 + j


def wait_bytes(ref, sem):
    pltpu.make_async_copy(ref, ref, sem).wait()


def kernel(
    own_ref, gain_hbm, weight_hbm, gate_weight_hbm, out_gain_hbm, out_weight_hbm, out_ref,
    gain_ref, weight_ref, gate_weight_ref, out_gain_ref, out_weight_ref,
    own, wt, main, rest, main32, rest32, g32, lr_a, lr_r, lr_b, g, g_relay, lr_a_in, lr_r_in, lr_b_in, g_in, left, right, p, p_in, p_sib, p32, gates, gains, ws, mixed, packed,
    load_sems, map_send, map_recv, lr_send, lr_a_recv, lr_r_recv, lr_b_recv, g_send, g_recv, relay_send, relay_recv, p_send, p_recv, sib_send, sib_recv,
):
    row, col = place()
    half = col % 2
    me = row * 2 + col // 2
    sibling = {"row": row, "col": col + 1 - 2 * half}
    barrier = pltpu.get_barrier_semaphore()

    def signal(device):
        pl.semaphore_signal(barrier, inc=1, device_id=device, device_id_type=MESH)

    z, y_hi, x = row // 8, (row // 4) % 2, row % 4
    base = 8 * col + 4 * y_hi
    other = (z + 2) % 4
    owners, relays = [], []
    for n in range(4):
        x2 = (x + n) % 4
        owners.append((4 * y_hi + x2, {"row": base + x2, "col": z}))
        relays.append((4 - 4 * y_hi + x2, {"row": base + x2, "col": other}))
    forward = {"row": row + 4 - 8 * y_hi, "col": (col + 2) % 4}
    is_own = z == col

    for hop in sorted(HOPS, key=lambda hop: -sum(min(v, 4 - v) for v in hop)):
        device, _ = chip_at(row, col, hop)
        signal(device)
        signal({"row": device["row"], "col": device["col"] + 1 - 2 * half})
    signal(sibling)

    loads = [
        pltpu.make_async_copy(src, dst, load_sems.at[n])
        for n, (src, dst) in enumerate(
            (
                (own_ref, own),
                (gain_hbm, gain_ref),
                (weight_hbm, weight_ref),
                (gate_weight_hbm, gate_weight_ref),
                (out_gain_hbm, out_gain_ref),
                (out_weight_hbm, out_weight_ref),
            )
        )
    ]
    for load in loads:
        load.start()

    for load in loads[1:]:
        load.wait()
    wt[...] = weight_ref[...].astype(F32).T
    parts = [wt[pl.ds(pl.multiple_of(128 * n + HALF * half, HALF), HALF), :] for n in range(4)]
    weight = jnp.concatenate(parts, axis=0).astype(BF16)
    weight_all = wt[...].astype(BF16)
    ones = jnp.full((128, 128), 1.0 / 128, BF16)
    rest[:, 96:128, :] = jnp.zeros((ROWS, 32, 128), BF16)
    for pad in (44, 45, 46, 47):
        main32[pl.ds(pad, CHANNELS, stride=48), :] = jnp.zeros((CHANNELS, 128), F32)
        rest32[pl.ds(pad, HALF, stride=48), :] = jnp.zeros((HALF, 128), F32)
    for pad in (22, 23):
        g32[pl.ds(pad, COLS, stride=ROWS_PAD), :] = jnp.zeros((COLS, 128), F32)

    loads[0].wait()

    @pl.loop(0, 2)
    def _(n):
        for u in range(11):
            i = 11 * n + u
            v = own[i]
            center = v.astype(F32) - jnp.dot(v, ones, preferred_element_type=F32)
            spread = jnp.dot((center * center).astype(BF16), ones, preferred_element_type=F32)
            y = center * lax.rsqrt(spread + 1e-05) * gain_ref[...]
            main[i] = y[0:128].astype(BF16)
            rest[i, 0:48, :] = y[128:176].astype(BF16)
            g32[pl.ds(i, COLS, stride=ROWS_PAD), :] = y

    def factors(target, rows, n, weights, normed):
        projected = lax.dot_general(weights, normed.reshape(256, 128), NT, preferred_element_type=F32)
        one = sigmoid(projected[0:rows]) * projected[rows : 2 * rows]
        two = sigmoid(projected[2 * rows : 3 * rows]) * projected[3 * rows :]
        for u in range(2):
            lanes = slice(128 * u, 128 * (u + 1))
            target[pl.ds(2 * n + u, rows, stride=48), :] = one[:, lanes]
            target[pl.ds(right_row(2 * n + u), rows, stride=48), :] = two[:, lanes]

    def pack_pairs(v):
        for n in range(2):
            rows = pl.ds(pl.multiple_of((22 * v + 11 * n) * ROWS_PAD, 8), 11 * ROWS_PAD)
            g[v, pl.ds(11 * n, 11)] = g32[rows, :].reshape(11, ROWS_PAD, 128).astype(BF16)

    def send_pairs(step):
        n, rows = step // 2, pl.ds(11 * (step % 2), 11)
        v, device = relays[n]
        pltpu.make_async_remote_copy(
            src_ref=g.at[v, rows],
            dst_ref=g_relay.at[x, rows],
            send_sem=g_send.at[v],
            recv_sem=relay_recv.at[x, step % 2],
            device_id=device,
            device_id_type=MESH,
        ).start()

        m = (n + 2) % 4
        v2, device2 = owners[m]

        def send_direct():
            pltpu.make_async_remote_copy(
                src_ref=g.at[v2, rows],
                dst_ref=g_in.at[row % 8, rows],
                send_sem=g_send.at[v2],
                recv_sem=g_recv.at[row % 8],
                device_id=device2,
                device_id_type=MESH,
            ).start()

        if m == 0:

            @pl.when(is_own)
            def _():
                pltpu.make_async_copy(g.at[v2, rows], g_in.at[v2, rows], g_recv.at[v2]).start()

            pl.when(jnp.logical_not(is_own))(send_direct)
        else:
            send_direct()

    def send_on(step):
        s, rows = (x + 4 - step // 2) % 4, pl.ds(11 * (step % 2), 11)
        wait_bytes(g_relay.at[s, rows], relay_recv.at[s, step % 2])
        pltpu.make_async_remote_copy(
            src_ref=g_relay.at[s, rows],
            dst_ref=g_in.at[4 * y_hi + s, rows],
            send_sem=relay_send.at[s],
            recv_sem=g_recv.at[4 * y_hi + s],
            device_id=forward,
            device_id_type=MESH,
        ).start()

    for n in (0, 1):
        pack_pairs(relays[n][0])
        pack_pairs(owners[(n + 2) % 4][0])

    pl.semaphore_wait(barrier, 127)

    swap_rest = pltpu.make_async_remote_copy(
        src_ref=rest.at[:, pl.ds(0, 48), :],
        dst_ref=rest.at[:, pl.ds(48, 48), :],
        send_sem=map_send,
        recv_sem=map_recv,
        device_id=sibling,
        device_id_type=MESH,
    )
    swap_rest.start()
    send_pairs(0)
    send_pairs(1)
    for n in (2, 3):
        pack_pairs(relays[n][0])
        pack_pairs(owners[(n + 2) % 4][0])

    for n in range(11):
        factors(main32, CHANNELS, n, weight_all, main[2 * n : 2 * n + 2])


    lane = lax.broadcasted_iota(jnp.int32, (8, 128), 1)
    place8 = lax.broadcasted_iota(jnp.int32, (8, 128), 0)

    def rows_of(source, channel, start, count):
        return source[pl.ds(pl.multiple_of(channel * 48 + start, 8), count), :]

    def send(buffer, index, target, recv, device, part):
        if device is None:
            pltpu.make_async_copy(buffer.at[index], target, recv.at[row // 2]).start()
        else:
            pltpu.make_async_remote_copy(
                src_ref=buffer.at[index],
                dst_ref=target,
                send_sem=lr_send.at[part],
                recv_sem=recv.at[row // 2],
                device_id=device,
                device_id_type=MESH,
            ).start()

    def send_first(chip, same, device):
        channel = chip + (HALF * half if same else HALF - HALF * half)
        lr_a[channel] = rows_of(main32, channel, 0, 40).astype(BF16)
        send(lr_a, channel, lr_a_in.at[me, half], lr_a_recv, device, 0)

    def send_rest(chip, device):
        held = rows_of(rest32, chip, 0, 40)
        full = [
            jnp.where(lane < 96, held[8 * q : 8 * q + 8], pltpu.roll(held[32:40], 96 - 32 * q, 1)) for q in range(3)
        ]
        lr_r[chip] = jnp.concatenate(full + [held[24:32]], axis=0).astype(BF16)
        send(lr_r, chip, lr_r_in.at[me], lr_r_recv, device, 1)

    def send_second(chip, same, device):
        channel = chip + (HALF * half if same else HALF - HALF * half)
        held = rows_of(main32, channel, 40, 8)
        if same:
            held = jnp.where(place8 < 4, held, pltpu.roll(rows_of(rest32, chip, 40, 8), 4, 0))
        lr_b[channel] = held.astype(BF16)
        send(lr_b, channel, lr_b_in.at[me, half], lr_b_recv, device, 2)

    def send_both(send_one, start, stop):
        for hop in HOPS[start:stop]:
            device, chip = chip_at(row, col, hop)
            send_one(chip, True, device)
            send_one(chip, False, {"row": device["row"], "col": device["col"] + 1 - 2 * half})
        if start == 0:
            send_one(me, False, sibling)
            send_one(me, True, None)

    for step in range(8):
        if 2 <= step < 7:
            send_pairs(step)
        if step == 6:
            send_pairs(7)
        if step < 4:
            send_both(send_first, 16 * step, 16 * step + 16)
        elif step < 6:
            for hop in HOPS[32 * (step - 4) : 32 * (step - 3)]:
                device, chip = chip_at(row, col, hop)
                send_rest(chip, device)
            if step == 4:
                send_rest(me, None)
        else:
            send_both(send_second, 32 * (step - 6), 32 * (step - 5))
        if step == 1:
            swap_rest.wait()
            for n in range(11):
                factors(rest32, HALF, n, weight, rest[2 * n : 2 * n + 2])
        if step >= 1:
            send_on(step - 1)
        if step == 7:
            send_on(7)

    def group(n):
        b = (row // 2 + n) % 16
        return b, pl.ds(pl.multiple_of(4 * b, 4), 4)

    def take_right(b, k, lanes, one, two):
        rows = pl.ds(pl.multiple_of(256 * k + 16 * b, 16), 16)
        right[rows, lanes] = jnp.concatenate([one, two], axis=0).astype(BF16)

    def tiles(b):
        for low in range(2):
            for t in range(3):
                yield 4 * b + low, t, slice(LANES * low + 128 * t, LANES * low + 128 * (t + 1))

    def first_rows(chip, t):
        if t < 2:
            return lr_a_in[chip, t].astype(F32)
        held = lr_r_in[chip].astype(F32)
        last = [pltpu.roll(held[8 * q : 8 * q + 8], 32 + 32 * q, 1) for q in range(3)]
        last = jnp.where(lane < 32, last[0], jnp.where(lane < 64, last[1], last[2]))
        rows = [held[8 * q : 8 * q + 8] for q in range(4)] + [last]
        return jnp.concatenate([jnp.where(lane < 96, v, 0.0) for v in rows], axis=0)

    def second_rows(chip, t):
        if t < 2:
            early, late = lr_a_in[chip, t, 16:32].astype(F32)[:8], lr_b_in[chip, t].astype(F32)
        else:
            early = jnp.where(lane < 96, lr_r_in[chip, 16:32].astype(F32)[:8], 0.0)
            late = pltpu.roll(lr_b_in[chip, half].astype(F32), 4, 0)
        return jnp.where(place8 < 6, late, early)

    def take_first(n):
        b, chips = group(n)
        wait_bytes(lr_a_in.at[chips], lr_a_recv.at[b])
        wait_bytes(lr_r_in.at[chips], lr_r_recv.at[b])
        for chip, t, lanes in tiles(b):
            one, two = first_rows(chip, t), first_rows(chip + 2, t)
            rows = pl.ds(pl.multiple_of(48 * b, 48), 48)
            left[rows, lanes] = jnp.concatenate([one[:24], two[:24]], axis=0).astype(BF16)
            take_right(b, 0, lanes, one[24:32], two[24:32])
            take_right(b, 1, lanes, one[32:], two[32:])

    def take_second(n):
        b, chips = group(n)
        wait_bytes(lr_b_in.at[chips], lr_b_recv.at[b])
        for chip, t, lanes in tiles(b):
            take_right(b, 2, lanes, second_rows(chip, t), second_rows(chip + 2, t))

    def send_products(k):
        acc = lax.dot_general(right[256 * k : 256 * (k + 1), :], left[...], NT, preferred_element_type=F32)
        for r in range(BLOCKS):
            for low in range(2):
                p[k, 2 * r + low] = acc[8 * r : 8 * r + 8, LANES * low : LANES * (low + 1)].astype(BF16)
        pltpu.make_async_copy(p.at[k, me], p_in.at[k, me], p_recv.at[k]).start()
        for hop in HOPS:
            device, chip = chip_at(row, col, hop)
            pltpu.make_async_remote_copy(
                src_ref=p.at[k, chip],
                dst_ref=p_in.at[k, me],
                send_sem=p_send.at[k],
                recv_sem=p_recv.at[k],
                device_id=device,
                device_id_type=MESH,
            ).start()

    pl.loop(0, 16)(take_first)
    send_products(0)
    send_products(1)
    pl.loop(0, 16)(take_second)
    send_products(2)

    for s in range(8):
        wait_bytes(g_in.at[s], g_recv.at[s])

    @pl.loop(0, 2)
    def _(n):
        for u in range(11):
            j = 11 * n + u
            pairs = jnp.concatenate([g_in[s, j].astype(F32) for s in range(8)], axis=0).astype(BF16)
            gates[j] = sigmoid(jnp.dot(pairs, gate_weight_ref[...], preferred_element_type=F32))

    gains[...] = jnp.broadcast_to(out_gain_ref[...], (128, 128)).T
    ws[...] = out_weight_ref[...].astype(F32)
    ours = pl.ds(pl.multiple_of(HALF * half, HALF), HALF)
    theirs = pl.ds(pl.multiple_of(HALF - HALF * half, HALF), HALF)
    gain = jnp.concatenate([gains[ours, :], gains[theirs, :]], axis=0)
    gain = jnp.concatenate([gain, gain], axis=1)
    out_weight = jnp.concatenate([ws[ours, :], ws[theirs, :]], axis=0).astype(BF16)

    for k, members in enumerate(GROUPS):
        wait_bytes(p_in.at[k], p_recv.at[k])
        swap = pltpu.make_async_remote_copy(
            src_ref=p_in.at[k, :, :, pl.ds(pl.multiple_of(128 - 128 * half, 128), 256)],
            dst_ref=p_sib.at[k],
            send_sem=sib_send.at[k],
            recv_sem=sib_recv.at[k],
            device_id=sibling,
            device_id_type=MESH,
        )
        swap.start()
        for t in range(2):
            lanes = pl.ds(pl.multiple_of(128 * half + 128 * t, 128), 128)
            p32[t, 0:512, :] = p_in[k, :, :, lanes].astype(F32).reshape(512, 128)
        swap.wait()
        for t in range(2):
            p32[t, 512:1024, :] = p_sib[k, :, :, 128 * t : 128 * (t + 1)].astype(F32).reshape(512, 128)
        for u, j in members:
            q = jnp.concatenate([p32[t, pl.ds(u, CHANNELS, stride=8), :] for t in range(2)], axis=1)
            center = q - jnp.mean(q, axis=0, keepdims=True)
            spread = jnp.mean(center * center, axis=0, keepdims=True)
            hidden = (center * lax.rsqrt(spread + 1e-05) * gain).astype(BF16)
            mixed[u] = lax.dot_general(hidden, out_weight, TN, preferred_element_type=F32)
            update = gates[j] * mixed[u, pl.ds(pl.multiple_of(64 * half, 64), 192), :]
            for s in range(8):
                packed[u, 22 * s : 22 * s + 24, :] = update[24 * s : 24 * s + 24]
            out_ref[j] = packed[u, 0:COLS, :].astype(BF16)

    wait_bytes(lr_a.at[pl.ds(0, 127)], lr_send.at[0])
    wait_bytes(lr_r.at[pl.ds(0, 63)], lr_send.at[1])
    wait_bytes(lr_b.at[pl.ds(0, 127)], lr_send.at[2])
    for k in range(3):
        wait_bytes(p.at[k, pl.ds(0, 63)], p_send.at[k])
    for v, _ in relays + owners[1:]:
        wait_bytes(g.at[v], g_send.at[v])
    for s in range(4):
        wait_bytes(g_relay.at[s], relay_send.at[s])

    @pl.when(jnp.logical_not(is_own))
    def _():
        wait_bytes(g.at[owners[0][0]], g_send.at[owners[0][0]])


def fused(*args):
    vmem = pl.BlockSpec(memory_space=pltpu.VMEM)
    return pl.pallas_call(
        kernel,
        out_shape=pltpu.VMEM((ROWS, COLS, 128), BF16),
        in_specs=[pl.BlockSpec(memory_space=pl.ANY)] * 6,
        out_specs=vmem,
        scratch_shapes=[
            pltpu.VMEM((1, 128), F32),
            pltpu.VMEM((128, 512), BF16),
            pltpu.VMEM((128, 128), BF16),
            pltpu.VMEM((1, 128), F32),
            pltpu.VMEM((128, 128), BF16),
            pltpu.VMEM((ROWS, COLS, 128), BF16),
            pltpu.VMEM((512, 128), F32),
            pltpu.VMEM((ROWS, 128, 128), BF16),
            pltpu.VMEM((ROWS, 128, 128), BF16),
            pltpu.VMEM((CHANNELS * 48, 128), F32),
            pltpu.VMEM((HALF * 48, 128), F32),
            pltpu.VMEM((COLS * ROWS_PAD, 128), F32),
            pltpu.VMEM((CHANNELS, 40, 128), BF16),
            pltpu.VMEM((HALF, 32, 128), BF16),
            pltpu.VMEM((CHANNELS, 8, 128), BF16),
            pltpu.VMEM((8, ROWS, ROWS_PAD, 128), BF16),
            pltpu.VMEM((4, ROWS, ROWS_PAD, 128), BF16),
            pltpu.VMEM((64, 2, 40, 128), BF16),
            pltpu.VMEM((64, 32, 128), BF16),
            pltpu.VMEM((64, 2, 8, 128), BF16),
            pltpu.VMEM((8, ROWS, ROWS_PAD, 128), BF16),
            pltpu.VMEM((768, 768), BF16),
            pltpu.VMEM((768, 768), BF16),
            pltpu.VMEM((3, 64, 8, LANES), BF16),
            pltpu.VMEM((3, 64, 8, LANES), BF16),
            pltpu.VMEM((3, 64, 8, 256), BF16),
            pltpu.VMEM((2, CHANNELS * 8, 128), F32),
            pltpu.VMEM((ROWS, 192, 128), F32),
            pltpu.VMEM((128, 128), F32),
            pltpu.VMEM((128, 128), F32),
            pltpu.VMEM((8, 256, 128), F32),
            pltpu.VMEM((8, 184, 128), F32),
            pltpu.SemaphoreType.DMA((6,)),
            pltpu.SemaphoreType.DMA,
            pltpu.SemaphoreType.DMA,
            pltpu.SemaphoreType.DMA((3,)),
            pltpu.SemaphoreType.DMA((16,)),
            pltpu.SemaphoreType.DMA((16,)),
            pltpu.SemaphoreType.DMA((16,)),
            pltpu.SemaphoreType.DMA((8,)),
            pltpu.SemaphoreType.DMA((8,)),
            pltpu.SemaphoreType.DMA((4,)),
            pltpu.SemaphoreType.DMA((4, 2)),
            pltpu.SemaphoreType.DMA((3,)),
            pltpu.SemaphoreType.DMA((3,)),
            pltpu.SemaphoreType.DMA((3,)),
            pltpu.SemaphoreType.DMA((3,)),
        ],
        compiler_params=pltpu.CompilerParams(
            collective_id=0, has_side_effects=True, vmem_limit_bytes=VMEM_LIMIT
        ),
        name="triangle_update",
    )(*args)


def copy_kernel(src_ref, dst_ref, sems):
    copies = [pltpu.make_async_copy(src_ref.at[i], dst_ref.at[i], sems.at[i]) for i in range(ROWS)]
    for copy in copies:
        copy.start()
    for copy in copies:
        copy.wait()


def copy_out(x):
    return pl.pallas_call(
        copy_kernel,
        out_shape=jax.ShapeDtypeStruct(x.shape, x.dtype),
        in_specs=[pl.BlockSpec(memory_space=pltpu.VMEM)],
        out_specs=pl.BlockSpec(memory_space=pl.ANY),
        scratch_shapes=[pltpu.SemaphoreType.DMA((ROWS,))],
        name="copy_out",
    )(pltpu.with_memory_space_constraint(x, pltpu.VMEM))


def body(pair_map, in_gain, project_weight, gate_weight, out_gain, out_weight):
    update = fused(
        pair_map, in_gain.reshape(1, 128), project_weight, gate_weight, out_gain.reshape(1, 128), out_weight
    )
    return copy_out(update)


def solution(mesh):
    return jax.shard_map(
        body,
        mesh=mesh,
        in_specs=(P("row", "col", None), P(), P(), P(), P(), P()),
        out_specs=P("row", "col", None),
        check_vma=False,
    )
```

```python
import functools

import jax
import jax.numpy as jnp
from jax import lax
from jax.experimental import pallas as pl
from jax.experimental.pallas import tpu as pltpu
from jax.sharding import PartitionSpec as P

MESH = pl.DeviceIdType.MESH
F32 = jnp.float32
BF16 = jnp.bfloat16
VMEM_LIMIT = 56 * 2**20

ROWS = 22
ROWS_PAD = 24
COLS = 176
CHANNELS = 128
HALF = 64
LANES = 384
BLOCKS = 32
NT = (((1,), (1,)), ((), ()))
TN = (((0,), (0,)), ((), ()))


def sigmoid(x):
    return 0.5 * jnp.tanh(0.5 * x) + 0.5


def place():
    row = lax.axis_index("row")
    col = lax.axis_index("col")
    return row, col


def chip_at(row, col, hop):
    z, y, x = row // 8, ((row // 4) % 2) * 2 + col // 2, row % 4
    z, y, x = (z + hop[0]) % 4, (y + hop[1]) % 4, (x + hop[2]) % 4
    row2 = z * 8 + (y // 2) * 4 + x
    low = y % 2
    return {"row": row2, "col": low * 2 + col % 2}, row2 * 2 + low


HOP_ORDER = (
    42, 4, 46, 58, 16, 1, 43, 41, 3, 48, 26, 12, 38, 54, 28, 34, 8, 59, 17, 45, 7,
    30, 52, 47, 5, 13, 39, 62, 20, 2, 40, 15, 37, 22, 60, 10, 32, 19, 57, 51, 25, 27,
    49, 61, 23, 6, 44, 50, 24, 29, 55, 18, 56, 63, 21, 11, 33, 36, 14, 53, 31, 35, 9,
)
HOPS = [(n // 16, n // 4 % 4, n % 4) for n in HOP_ORDER]
GROUPS = (
    [(u, u) for u in range(8)],
    [(u, 8 + u) for u in range(8)],
    [(0, 18), (1, 19), (2, 20), (3, 21), (6, 16), (7, 17)],
)


def right_row(j):
    return 24 + j if j < 16 else 6 + j if j < 18 else 22 + j


def wait_bytes(ref, sem):
    pltpu.make_async_copy(ref, ref, sem).wait()


def kernel(
    own_ref, gain_hbm, weight_hbm, gate_weight_hbm, out_gain_hbm, out_weight_hbm, out_ref,
    gain_ref, weight_ref, gate_weight_ref, out_gain_ref, out_weight_ref,
    own, wt, main, rest, main32, rest32, g32, lr_a, lr_r, lr_b, g, g_relay, lr_a_in, lr_r_in, lr_b_in, g_in, left, right, p, p_in, p_sib, p32, gates, gains, ws, mixed, packed,
    load_sems, map_send, map_recv, lr_send, lr_a_recv, lr_r_recv, lr_b_recv, g_send, g_recv, relay_send, relay_recv, p_send, p_recv, sib_send, sib_recv,
):
    row, col = place()
    half = col % 2
    me = row * 2 + col // 2
    sibling = {"row": row, "col": col + 1 - 2 * half}
    barrier = pltpu.get_barrier_semaphore()

    def signal(device):
        pl.semaphore_signal(barrier, inc=1, device_id=device, device_id_type=MESH)

    z, y_hi, x = row // 8, (row // 4) % 2, row % 4
    base = 8 * col + 4 * y_hi
    other = (z + 2) % 4
    owners, relays = [], []
    for n in range(4):
        x2 = (x + n) % 4
        owners.append((4 * y_hi + x2, {"row": base + x2, "col": z}))
        relays.append((4 - 4 * y_hi + x2, {"row": base + x2, "col": other}))
    forward = {"row": row + 4 - 8 * y_hi, "col": (col + 2) % 4}
    is_own = z == col

    for hop in sorted(HOPS, key=lambda hop: -sum(min(v, 4 - v) for v in hop)):
        device, _ = chip_at(row, col, hop)
        signal(device)
        signal({"row": device["row"], "col": device["col"] + 1 - 2 * half})
    signal(sibling)

    loads = [
        pltpu.make_async_copy(src, dst, load_sems.at[n])
        for n, (src, dst) in enumerate(
            (
                (own_ref, own),
                (gain_hbm, gain_ref),
                (weight_hbm, weight_ref),
                (gate_weight_hbm, gate_weight_ref),
                (out_gain_hbm, out_gain_ref),
                (out_weight_hbm, out_weight_ref),
            )
        )
    ]
    for load in loads:
        load.start()

    for load in loads[1:]:
        load.wait()
    wt[...] = weight_ref[...].astype(F32).T
    parts = [wt[pl.ds(pl.multiple_of(128 * n + HALF * half, HALF), HALF), :] for n in range(4)]
    weight = jnp.concatenate(parts, axis=0).astype(BF16)
    weight_all = wt[...].astype(BF16)
    ones = jnp.full((128, 128), 1.0 / 128, BF16)
    rest[:, 96:128, :] = jnp.zeros((ROWS, 32, 128), BF16)
    for pad in (44, 45, 46, 47):
        main32[pl.ds(pad, CHANNELS, stride=48), :] = jnp.zeros((CHANNELS, 128), F32)
        rest32[pl.ds(pad, HALF, stride=48), :] = jnp.zeros((HALF, 128), F32)
    for pad in (22, 23):
        g32[pl.ds(pad, COLS, stride=ROWS_PAD), :] = jnp.zeros((COLS, 128), F32)

    loads[0].wait()

    @pl.loop(0, 2)
    def _(n):
        for u in range(11):
            i = 11 * n + u
            v = own[i]
            center = v.astype(F32) - jnp.dot(v, ones, preferred_element_type=F32)
            spread = jnp.dot((center * center).astype(BF16), ones, preferred_element_type=F32)
            y = center * lax.rsqrt(spread + 1e-05) * gain_ref[...]
            main[i] = y[0:128].astype(BF16)
            rest[i, 0:48, :] = y[128:176].astype(BF16)
            g32[pl.ds(i, COLS, stride=ROWS_PAD), :] = y

    def factors(target, rows, n, weights, normed):
        projected = lax.dot_general(weights, normed.reshape(256, 128), NT, preferred_element_type=F32)
        one = sigmoid(projected[0:rows]) * projected[rows : 2 * rows]
        two = sigmoid(projected[2 * rows : 3 * rows]) * projected[3 * rows :]
        for u in range(2):
            lanes = slice(128 * u, 128 * (u + 1))
            target[pl.ds(2 * n + u, rows, stride=48), :] = one[:, lanes]
            target[pl.ds(right_row(2 * n + u), rows, stride=48), :] = two[:, lanes]

    def pack_pairs(v):
        for n in range(2):
            rows = pl.ds(pl.multiple_of((22 * v + 11 * n) * ROWS_PAD, 8), 11 * ROWS_PAD)
            g[v, pl.ds(11 * n, 11)] = g32[rows, :].reshape(11, ROWS_PAD, 128).astype(BF16)

    def send_pairs(step):
        n, rows = step // 2, pl.ds(11 * (step % 2), 11)
        v, device = relays[n]
        pltpu.make_async_remote_copy(
            src_ref=g.at[v, rows],
            dst_ref=g_relay.at[x, rows],
            send_sem=g_send.at[v],
            recv_sem=relay_recv.at[x, step % 2],
            device_id=device,
            device_id_type=MESH,
        ).start()

        m = (n + 2) % 4
        v2, device2 = owners[m]

        def send_direct():
            pltpu.make_async_remote_copy(
                src_ref=g.at[v2, rows],
                dst_ref=g_in.at[row % 8, rows],
                send_sem=g_send.at[v2],
                recv_sem=g_recv.at[row % 8],
                device_id=device2,
                device_id_type=MESH,
            ).start()

        if m == 0:

            @pl.when(is_own)
            def _():
                pltpu.make_async_copy(g.at[v2, rows], g_in.at[v2, rows], g_recv.at[v2]).start()

            pl.when(jnp.logical_not(is_own))(send_direct)
        else:
            send_direct()

    def send_on(step):
        s, rows = (x + 4 - step // 2) % 4, pl.ds(11 * (step % 2), 11)
        wait_bytes(g_relay.at[s, rows], relay_recv.at[s, step % 2])
        pltpu.make_async_remote_copy(
            src_ref=g_relay.at[s, rows],
            dst_ref=g_in.at[4 * y_hi + s, rows],
            send_sem=relay_send.at[s],
            recv_sem=g_recv.at[4 * y_hi + s],
            device_id=forward,
            device_id_type=MESH,
        ).start()

    for n in (0, 1):
        pack_pairs(relays[n][0])
        pack_pairs(owners[(n + 2) % 4][0])

    pl.semaphore_wait(barrier, 127)

    swap_rest = pltpu.make_async_remote_copy(
        src_ref=rest.at[:, pl.ds(0, 48), :],
        dst_ref=rest.at[:, pl.ds(48, 48), :],
        send_sem=map_send,
        recv_sem=map_recv,
        device_id=sibling,
        device_id_type=MESH,
    )
    swap_rest.start()
    send_pairs(0)
    send_pairs(1)
    for n in (2, 3):
        pack_pairs(relays[n][0])
        pack_pairs(owners[(n + 2) % 4][0])

    for n in range(11):
        factors(main32, CHANNELS, n, weight_all, main[2 * n : 2 * n + 2])


    lane = lax.broadcasted_iota(jnp.int32, (8, 128), 1)
    place8 = lax.broadcasted_iota(jnp.int32, (8, 128), 0)

    def rows_of(source, channel, start, count):
        return source[pl.ds(pl.multiple_of(channel * 48 + start, 8), count), :]

    def send(buffer, index, target, recv, device, part):
        if device is None:
            pltpu.make_async_copy(buffer.at[index], target, recv.at[row // 2]).start()
        else:
            pltpu.make_async_remote_copy(
                src_ref=buffer.at[index],
                dst_ref=target,
                send_sem=lr_send.at[part],
                recv_sem=recv.at[row // 2],
                device_id=device,
                device_id_type=MESH,
            ).start()

    def send_first(chip, same, device):
        channel = chip + (HALF * half if same else HALF - HALF * half)
        lr_a[channel] = rows_of(main32, channel, 0, 40).astype(BF16)
        send(lr_a, channel, lr_a_in.at[me, half], lr_a_recv, device, 0)

    def send_rest(chip, device):
        held = rows_of(rest32, chip, 0, 40)
        full = [
            jnp.where(lane < 96, held[8 * q : 8 * q + 8], pltpu.roll(held[32:40], 96 - 32 * q, 1)) for q in range(3)
        ]
        lr_r[chip] = jnp.concatenate(full + [held[24:32]], axis=0).astype(BF16)
        send(lr_r, chip, lr_r_in.at[me], lr_r_recv, device, 1)

    def send_second(chip, same, device):
        channel = chip + (HALF * half if same else HALF - HALF * half)
        held = rows_of(main32, channel, 40, 8)
        if same:
            held = jnp.where(place8 < 4, held, pltpu.roll(rows_of(rest32, chip, 40, 8), 4, 0))
        lr_b[channel] = held.astype(BF16)
        send(lr_b, channel, lr_b_in.at[me, half], lr_b_recv, device, 2)

    def send_both(send_one, start, stop):
        for hop in HOPS[start:stop]:
            device, chip = chip_at(row, col, hop)
            send_one(chip, True, device)
            send_one(chip, False, {"row": device["row"], "col": device["col"] + 1 - 2 * half})
        if start == 0:
            send_one(me, False, sibling)
            send_one(me, True, None)

    for step in range(8):
        if 2 <= step < 7:
            send_pairs(step)
        if step == 6:
            send_pairs(7)
        if step < 4:
            send_both(send_first, 16 * step, 16 * step + 16)
        elif step < 6:
            for hop in HOPS[32 * (step - 4) : 32 * (step - 3)]:
                device, chip = chip_at(row, col, hop)
                send_rest(chip, device)
            if step == 4:
                send_rest(me, None)
        else:
            send_both(send_second, 32 * (step - 6), 32 * (step - 5))
        if step == 1:
            swap_rest.wait()
            for n in range(11):
                factors(rest32, HALF, n, weight, rest[2 * n : 2 * n + 2])
        if step >= 1:
            send_on(step - 1)
        if step == 7:
            send_on(7)

    def group(n):
        b = (row // 2 + n) % 16
        return b, pl.ds(pl.multiple_of(4 * b, 4), 4)

    def take_right(b, k, lanes, one, two):
        rows = pl.ds(pl.multiple_of(256 * k + 16 * b, 16), 16)
        right[rows, lanes] = jnp.concatenate([one, two], axis=0).astype(BF16)

    def tiles(b):
        for low in range(2):
            for t in range(3):
                yield 4 * b + low, t, slice(LANES * low + 128 * t, LANES * low + 128 * (t + 1))

    def first_rows(chip, t):
        if t < 2:
            return lr_a_in[chip, t].astype(F32)
        held = lr_r_in[chip].astype(F32)
        last = [pltpu.roll(held[8 * q : 8 * q + 8], 32 + 32 * q, 1) for q in range(3)]
        last = jnp.where(lane < 32, last[0], jnp.where(lane < 64, last[1], last[2]))
        rows = [held[8 * q : 8 * q + 8] for q in range(4)] + [last]
        return jnp.concatenate([jnp.where(lane < 96, v, 0.0) for v in rows], axis=0)

    def second_rows(chip, t):
        if t < 2:
            early, late = lr_a_in[chip, t, 16:32].astype(F32)[:8], lr_b_in[chip, t].astype(F32)
        else:
            early = jnp.where(lane < 96, lr_r_in[chip, 16:32].astype(F32)[:8], 0.0)
            late = pltpu.roll(lr_b_in[chip, half].astype(F32), 4, 0)
        return jnp.where(place8 < 6, late, early)

    def take_first(n):
        b, chips = group(n)
        wait_bytes(lr_a_in.at[chips], lr_a_recv.at[b])
        wait_bytes(lr_r_in.at[chips], lr_r_recv.at[b])
        for chip, t, lanes in tiles(b):
            one, two = first_rows(chip, t), first_rows(chip + 2, t)
            rows = pl.ds(pl.multiple_of(48 * b, 48), 48)
            left[rows, lanes] = jnp.concatenate([one[:24], two[:24]], axis=0).astype(BF16)
            take_right(b, 0, lanes, one[24:32], two[24:32])
            take_right(b, 1, lanes, one[32:], two[32:])

    def take_second(n):
        b, chips = group(n)
        wait_bytes(lr_b_in.at[chips], lr_b_recv.at[b])
        for chip, t, lanes in tiles(b):
            take_right(b, 2, lanes, second_rows(chip, t), second_rows(chip + 2, t))

    def send_products(k):
        acc = lax.dot_general(right[256 * k : 256 * (k + 1), :], left[...], NT, preferred_element_type=F32)
        for r in range(BLOCKS):
            for low in range(2):
                p[k, 2 * r + low] = acc[8 * r : 8 * r + 8, LANES * low : LANES * (low + 1)].astype(BF16)
        pltpu.make_async_copy(p.at[k, me], p_in.at[k, me], p_recv.at[k]).start()
        for hop in HOPS:
            device, chip = chip_at(row, col, hop)
            pltpu.make_async_remote_copy(
                src_ref=p.at[k, chip],
                dst_ref=p_in.at[k, me],
                send_sem=p_send.at[k],
                recv_sem=p_recv.at[k],
                device_id=device,
                device_id_type=MESH,
            ).start()

    pl.loop(0, 16)(take_first)
    send_products(0)
    send_products(1)
    pl.loop(0, 16)(take_second)
    send_products(2)

    for s in range(8):
        wait_bytes(g_in.at[s], g_recv.at[s])

    @pl.loop(0, 2)
    def _(n):
        for u in range(11):
            j = 11 * n + u
            pairs = jnp.concatenate([g_in[s, j].astype(F32) for s in range(8)], axis=0).astype(BF16)
            gates[j] = sigmoid(jnp.dot(pairs, gate_weight_ref[...], preferred_element_type=F32))

    gains[...] = jnp.broadcast_to(out_gain_ref[...], (128, 128)).T
    ws[...] = out_weight_ref[...].astype(F32)
    ours = pl.ds(pl.multiple_of(HALF * half, HALF), HALF)
    theirs = pl.ds(pl.multiple_of(HALF - HALF * half, HALF), HALF)
    gain = jnp.concatenate([gains[ours, :], gains[theirs, :]], axis=0)
    gain = jnp.concatenate([gain, gain], axis=1)
    out_weight = jnp.concatenate([ws[ours, :], ws[theirs, :]], axis=0).astype(BF16)

    for k, members in enumerate(GROUPS):
        wait_bytes(p_in.at[k], p_recv.at[k])
        swap = pltpu.make_async_remote_copy(
            src_ref=p_in.at[k, :, :, pl.ds(pl.multiple_of(128 - 128 * half, 128), 256)],
            dst_ref=p_sib.at[k],
            send_sem=sib_send.at[k],
            recv_sem=sib_recv.at[k],
            device_id=sibling,
            device_id_type=MESH,
        )
        swap.start()
        for t in range(2):
            lanes = pl.ds(pl.multiple_of(128 * half + 128 * t, 128), 128)
            p32[t, 0:512, :] = p_in[k, :, :, lanes].astype(F32).reshape(512, 128)
        swap.wait()
        for t in range(2):
            p32[t, 512:1024, :] = p_sib[k, :, :, 128 * t : 128 * (t + 1)].astype(F32).reshape(512, 128)
        for u, j in members:
            q = jnp.concatenate([p32[t, pl.ds(u, CHANNELS, stride=8), :] for t in range(2)], axis=1)
            center = q - jnp.mean(q, axis=0, keepdims=True)
            spread = jnp.mean(center * center, axis=0, keepdims=True)
            hidden = (center * lax.rsqrt(spread + 1e-05) * gain).astype(BF16)
            mixed[u] = lax.dot_general(hidden, out_weight, TN, preferred_element_type=F32)
            update = gates[j] * mixed[u, pl.ds(pl.multiple_of(64 * half, 64), 192), :]
            for s in range(8):
                packed[u, 22 * s : 22 * s + 24, :] = update[24 * s : 24 * s + 24]
            out_ref[j] = packed[u, 0:COLS, :].astype(BF16)

    wait_bytes(lr_a.at[pl.ds(0, 127)], lr_send.at[0])
    wait_bytes(lr_r.at[pl.ds(0, 63)], lr_send.at[1])
    wait_bytes(lr_b.at[pl.ds(0, 127)], lr_send.at[2])
    for k in range(3):
        wait_bytes(p.at[k, pl.ds(0, 63)], p_send.at[k])
    for v, _ in relays + owners[1:]:
        wait_bytes(g.at[v], g_send.at[v])
    for s in range(4):
        wait_bytes(g_relay.at[s], relay_send.at[s])

    @pl.when(jnp.logical_not(is_own))
    def _():
        wait_bytes(g.at[owners[0][0]], g_send.at[owners[0][0]])


def fused(*args):
    vmem = pl.BlockSpec(memory_space=pltpu.VMEM)
    return pl.pallas_call(
        kernel,
        out_shape=pltpu.VMEM((ROWS, COLS, 128), BF16),
        in_specs=[pl.BlockSpec(memory_space=pl.ANY)] * 6,
        out_specs=vmem,
        scratch_shapes=[
            pltpu.VMEM((1, 128), F32),
            pltpu.VMEM((128, 512), BF16),
            pltpu.VMEM((128, 128), BF16),
            pltpu.VMEM((1, 128), F32),
            pltpu.VMEM((128, 128), BF16),
            pltpu.VMEM((ROWS, COLS, 128), BF16),
            pltpu.VMEM((512, 128), F32),
            pltpu.VMEM((ROWS, 128, 128), BF16),
            pltpu.VMEM((ROWS, 128, 128), BF16),
            pltpu.VMEM((CHANNELS * 48 + 48, 128), F32),
            pltpu.VMEM((HALF * 48 + 48, 128), F32),
            pltpu.VMEM((COLS * ROWS_PAD + ROWS_PAD, 128), F32),
            pltpu.VMEM((CHANNELS, 40, 128), BF16),
            pltpu.VMEM((HALF, 32, 128), BF16),
            pltpu.VMEM((CHANNELS, 8, 128), BF16),
            pltpu.VMEM((8, ROWS, ROWS_PAD, 128), BF16),
            pltpu.VMEM((4, ROWS, ROWS_PAD, 128), BF16),
            pltpu.VMEM((64, 2, 40, 128), BF16),
            pltpu.VMEM((64, 32, 128), BF16),
            pltpu.VMEM((64, 2, 8, 128), BF16),
            pltpu.VMEM((8, ROWS, ROWS_PAD, 128), BF16),
            pltpu.VMEM((768, 768), BF16),
            pltpu.VMEM((768, 768), BF16),
            pltpu.VMEM((3, 64, 8, LANES), BF16),
            pltpu.VMEM((3, 64, 8, LANES), BF16),
            pltpu.VMEM((3, 64, 8, 256), BF16),
            pltpu.VMEM((2, CHANNELS * 8 + 8, 128), F32),
            pltpu.VMEM((ROWS, 192, 128), F32),
            pltpu.VMEM((128, 128), F32),
            pltpu.VMEM((128, 128), F32),
            pltpu.VMEM((8, 256, 128), F32),
            pltpu.VMEM((8, 184, 128), F32),
            pltpu.SemaphoreType.DMA((6,)),
            pltpu.SemaphoreType.DMA,
            pltpu.SemaphoreType.DMA,
            pltpu.SemaphoreType.DMA((3,)),
            pltpu.SemaphoreType.DMA((16,)),
            pltpu.SemaphoreType.DMA((16,)),
            pltpu.SemaphoreType.DMA((16,)),
            pltpu.SemaphoreType.DMA((8,)),
            pltpu.SemaphoreType.DMA((8,)),
            pltpu.SemaphoreType.DMA((4,)),
            pltpu.SemaphoreType.DMA((4, 2)),
            pltpu.SemaphoreType.DMA((3,)),
            pltpu.SemaphoreType.DMA((3,)),
            pltpu.SemaphoreType.DMA((3,)),
            pltpu.SemaphoreType.DMA((3,)),
        ],
        compiler_params=pltpu.CompilerParams(
            collective_id=0, has_side_effects=True, vmem_limit_bytes=VMEM_LIMIT
        ),
        name="triangle_update",
    )(*args)


def copy_kernel(src_ref, dst_ref, sems):
    copies = [pltpu.make_async_copy(src_ref.at[i], dst_ref.at[i], sems.at[i]) for i in range(ROWS)]
    for copy in copies:
        copy.start()
    for copy in copies:
        copy.wait()


def copy_out(x):
    return pl.pallas_call(
        copy_kernel,
        out_shape=jax.ShapeDtypeStruct(x.shape, x.dtype),
        in_specs=[pl.BlockSpec(memory_space=pltpu.VMEM)],
        out_specs=pl.BlockSpec(memory_space=pl.ANY),
        scratch_shapes=[pltpu.SemaphoreType.DMA((ROWS,))],
        name="copy_out",
    )(pltpu.with_memory_space_constraint(x, pltpu.VMEM))


def body(pair_map, in_gain, project_weight, gate_weight, out_gain, out_weight):
    update = fused(
        pair_map, in_gain.reshape(1, 128), project_weight, gate_weight, out_gain.reshape(1, 128), out_weight
    )
    return copy_out(update)


def solution(mesh):
    return jax.shard_map(
        body,
        mesh=mesh,
        in_specs=(P("row", "col", None), P(), P(), P(), P(), P()),
        out_specs=P("row", "col", None),
        check_vma=False,
    )
```
